512 devices in a mesh: batch: 16 (over y, x_hi, core), seq: 32 (over z, x_lo).
Axes of the slice: x: 4 (x_hi: 2, x_lo: 2; x = x_hi * 2 + x_lo), y: 4, z: 16, core: 2. Of those that a mesh axis runs over, the one named last changes fastest.
Arguments:
- history_keys: bfloat16 [131072, 1024], P(('batch', 'seq')), parts along dimension 0, may hold values from -6 to 6
- history_values: bfloat16 [131072, 1024], P(('batch', 'seq')), parts along dimension 0, may hold values from -6 to 6
- lengths: int32 [16], P('batch'), parts along dimension 0, may hold values from 1024 to 8192, as said below
- item_ids: int32 [8192], P('batch'), parts along dimension 0, may hold values from 0 to 16383
- item_table: bfloat16 [16384, 1024], P('seq'), may hold values from -6 to 6
- w_proj: bfloat16 [1024, 4, 1024], P(None, None, 'seq'), may hold values from -0.1875 to 0.1875
- rab: float32 [8, 16], replicated, may hold values from -4 to 4
- norm_gain: float32 [1024], replicated, may hold values from 0.1 to 1.9
- w_out: bfloat16 [1024, 1024], P('seq'), may hold values from -0.1875 to 0.1875
Outputs:
- scored: bfloat16 [8192, 1024], P(('batch', 'seq')), parts along dimension 0
The draws below stay inside these ranges and needn't reach their ends.
There are 16 independent parts, one for each index of `batch`. The reference program is written for one: setup_inputs(seed, part) draws one part's arguments, and reference() takes and returns one part's arrays. A program takes and returns all parts, laid end to end along the dimension named above; an argument that names none is the same for every part. Nothing has to cross between parts.
Inputs may be any that keep to these rules, and one draw needn't show every extreme that they name: `lengths`: in every fourth part, starting with the fourth, the history is full: L = 8192.
All inputs are finite; a program needn't handle non-finite values.
Results may differ from the reference program's by a relative error of at most 0.0085.
Values may be sent and summed in bfloat16 or wider, within the bound.
No kernel may reach another device: no remote copies, remote signals or barrier semaphores. Data moves between devices by JAX's collectives and lax.ppermute only.
A program may use at most 64 MiB of HBM per device.

```python
import jax
import jax.numpy as jnp
from jax import lax

D = 1024
HEADS = 8
BUCKETS = 16
CAND = 512
HIST = 8192
ITEMS = 16384


def draw_lengths(key, part):
    key = jax.random.fold_in(key, 7)
    drawn = jax.random.randint(key, (1,), HIST // 8, HIST + 1)
    return jnp.where(part % 4 == 3, HIST, drawn).astype(jnp.int32)


def with_ends(entries, key, low, top_value):
    longest = entries.shape.index(max(entries.shape))
    spots = []
    for shift in (0, 1):
        where = [jax.random.randint(jax.random.fold_in(key, axis), (), 0, length) for axis, length in enumerate(entries.shape)]
        where[longest] = (where[longest] + shift) % entries.shape[longest]
        spots.append(tuple(where))
    return entries.at[spots[0]].set(low).at[spots[1]].set(top_value)


def block_scale(own_key, shape, cuts, smallest, top_value):
    level, own = 1.0, jax.random.fold_in(own_key, 6)
    for axis_at, parts in cuts:
        heights = jnp.exp(jax.random.uniform(jax.random.fold_in(own, axis_at), (parts,), jnp.float32, smallest / len(cuts), top_value / len(cuts)))
        level = level * jnp.repeat(heights, shape[axis_at] // parts).reshape([-1 if axis == axis_at else 1 for axis in range(len(shape))])
    return level


def bell_draw(rng, shape, scale, reach, split=(), kind=jnp.bfloat16):
    array = scale * jax.random.normal(rng, shape, jnp.float32)
    if split:
        array = array * block_scale(rng, shape, split, -0.22, 0.18)
    return jnp.clip(array, -reach, reach).astype(kind)


def setup_inputs(seed: int = 0, part: int = 0) -> dict:
    streams_of = jax.random.split(jax.random.key(seed), 10)
    own_keys = jax.random.split(jax.random.fold_in(streams_of[9], part), 10)
    history_keys = bell_draw(own_keys[0], (HIST, D), 1.0, 6.0, ((0, 32),))
    history_values = bell_draw(own_keys[1], (HIST, D), 1.0, 6.0, ((0, 32),))
    lengths = draw_lengths(jax.random.fold_in(jax.random.fold_in(streams_of[9], part), 71), part)
    item_ids = with_ends(jax.random.randint(own_keys[3], (CAND,), 0, ITEMS), jax.random.fold_in(own_keys[3], 1), 0, ITEMS - 1).astype(jnp.int32)
    item_table = bell_draw(streams_of[4], (ITEMS, D), 1.0, 6.0, ((0, 32),))
    w_proj = bell_draw(streams_of[5], (D, 4, D), D ** -0.5, 0.1875, ((2, 32),))
    rab = bell_draw(streams_of[6], (HEADS, BUCKETS), 1.0, 4.0, (), jnp.float32)
    norm_gain = jnp.clip(1.0 + 0.18 * jax.random.normal(streams_of[7], (D,), jnp.float32), 0.1, 1.9)
    w_out = bell_draw(streams_of[8], (D, D), D ** -0.5, 0.1875, ((0, 32),))
    return {"history_keys": history_keys, "history_values": history_values, "lengths": lengths, "item_ids": item_ids, "item_table": item_table, "w_proj": w_proj, "rab": rab, "norm_gain": norm_gain, "w_out": w_out}


def bucket_bias(rab_table, distance):
    bucket_count = rab_table.shape[1]
    powers = 2 ** jnp.arange(bucket_count - 1, dtype=jnp.int32)
    bucket = lax.optimization_barrier(jnp.sum((distance[:, None] >= powers[None, :]).astype(jnp.int32), axis=1))
    hits = bucket[None, :] == jnp.arange(bucket_count, dtype=jnp.int32)[:, None]
    return lax.optimization_barrier(jnp.sum(jnp.where(hits[None, :, :], rab_table[:, :, None], 0.0), axis=1))

def reference(history_keys, history_values, lengths, item_ids, item_table, w_proj, rab, norm_gain, w_out):
    head_size = D // HEADS
    scale = head_size ** (-0.5)
    length = lengths[0]
    embedded = jnp.take(item_table, item_ids, axis=0)
    proj = jax.nn.silu(jnp.dot(embedded, w_proj.reshape(D, 4 * D), preferred_element_type=jnp.float32))
    proj = proj.reshape(CAND, 4, D).astype(jnp.bfloat16)
    gate_u = proj[:, 0, :]
    own_v = proj[:, 1, :]
    queries = proj[:, 2, :]
    own_k = proj[:, 3, :]
    query_heads = queries.reshape(CAND, HEADS, head_size).astype(jnp.float32)
    history_block = 512
    block_count = HIST // history_block

    def visit(carried, block_index):
        first_row = block_index * history_block
        key_block = lax.dynamic_slice_in_dim(history_keys, first_row, history_block, 0)
        value_block = lax.dynamic_slice_in_dim(history_values, first_row, history_block, 0)
        key_block = key_block.reshape(history_block, HEADS, head_size).astype(jnp.float32)
        value_block = value_block.reshape(history_block, HEADS, head_size).astype(jnp.float32)
        positions = first_row + jnp.arange(history_block, dtype=jnp.int32)
        bias = bucket_bias(rab, length - positions)
        scores = jnp.einsum('chd,rhd->hcr', query_heads, key_block) * scale + bias[:, None, :]
        weights = jnp.where((positions < length)[None, None, :], jax.nn.silu(scores), 0.0).astype(jnp.bfloat16)
        carried = carried + jnp.einsum('hcr,rhd->chd', weights.astype(jnp.float32), value_block)
        return (carried, None)
    history_sum, unused = lax.scan(visit, jnp.zeros((CAND, HEADS, head_size), jnp.float32), jnp.arange(block_count, dtype=jnp.int32))
    self_scores = lax.optimization_barrier(jnp.sum((queries.astype(jnp.float32) * own_k.astype(jnp.float32)).reshape(CAND, HEADS, head_size), axis=2))
    self_scores = self_scores * scale + rab[:, 0][None, :]
    self_term = jax.nn.silu(self_scores)[:, :, None] * own_v.astype(jnp.float32).reshape(CAND, HEADS, head_size)
    attended = history_sum.reshape(CAND, D) * lax.rsqrt(length.astype(jnp.float32)) + self_term.reshape(CAND, D)
    centre = lax.optimization_barrier(jnp.mean(attended, axis=1, keepdims=True))
    spread = lax.optimization_barrier(jnp.mean((attended - centre) ** 2, axis=1, keepdims=True))
    normed = (attended - centre) * lax.rsqrt(spread + 1e-05) * norm_gain[None, :] * gate_u.astype(jnp.float32)
    normed = normed.astype(jnp.bfloat16)
    scored = jnp.dot(normed, w_out, preferred_element_type=jnp.float32) + embedded.astype(jnp.float32)
    return scored.astype(jnp.bfloat16)
```

```python
import jax
import jax.numpy as jnp
from jax import lax
from jax.experimental import pallas as pl
from jax.experimental.pallas import tpu as pltpu
from jax.sharding import PartitionSpec as P

slot_rows = 32


near_places = 4


def groups_of(places):
    return [[2 * place + side for place in group] for side in range(2) for group in places]


def column_groups():
    return groups_of([list(range(lax.axis_size("seq") // 2))])


def exchange(blocks, groups):
    return lax.all_to_all(
        blocks, "seq", split_axis=0, concat_axis=0, tiled=True, axis_index_groups=groups
    )


def two_step_gather(block):
    column = lax.axis_size("seq") // 2
    far_places = column // near_places
    far = groups_of([list(range(at, column, near_places)) for at in range(near_places)])
    near = groups_of(
        [list(range(at, at + near_places)) for at in range(0, column, near_places)]
    )
    blocks = exchange(jnp.broadcast_to(block[None], (far_places,) + block.shape), far)
    return exchange(
        jnp.broadcast_to(blocks[None], (near_places,) + blocks.shape).reshape(
            (column,) + block.shape
        ),
        near,
    )


def swap_pair(block):
    return lax.ppermute(block, "seq", [(i, i ^ 1) for i in range(lax.axis_size("seq"))])


def bucket_bias(rab_table, distance):
    bucket_count = rab_table.shape[1]
    powers = 2 ** jnp.arange(bucket_count - 1, dtype=jnp.int32)
    bucket = jnp.sum((distance[:, None] >= powers[None, :]).astype(jnp.int32), axis=1)
    hits = (bucket[None, :] == jnp.arange(bucket_count, dtype=jnp.int32)[:, None]).astype(
        jnp.float32
    )
    return jnp.dot(
        rab_table, hits, precision=lax.Precision.HIGHEST, preferred_element_type=jnp.float32
    )


def attend_kernel(
    scale, queries, keys_a, keys_b, values_a, values_b, bias_a, bias_b, live_a, live_b, summed
):
    head = pl.program_id(0)
    head_queries = queries[...].T
    total = None
    for keys, values, bias, live in (
        (keys_a, values_a, bias_a, live_a),
        (keys_b, values_b, bias_b, live_b),
    ):
        scores = lax.dot_general(
            head_queries, keys[...], (((1,), (1,)), ((), ())), preferred_element_type=jnp.float32
        )
        scores = scores * scale + bias[pl.ds(head, 1), :]
        weights = scores * (0.5 + 0.5 * jnp.tanh(0.5 * scores))
        weights = jnp.where(live[...] > 0.0, weights, 0.0).astype(jnp.bfloat16)
        part = jnp.dot(weights, values[...], preferred_element_type=jnp.float32)
        total = part if total is None else total + part
    summed[...] = total.astype(summed.dtype)


def attend(queries, keys, values, bias, live, head_count):
    width, cand = queries.shape
    events = keys[0].shape[0]
    head_size = width // head_count
    event_spec = pl.BlockSpec((events, head_size), lambda h: (0, h))
    bias_spec = pl.BlockSpec((head_count, events), lambda h: (0, 0))
    live_spec = pl.BlockSpec((1, events), lambda h: (0, 0))

    def body(*refs):
        attend_kernel(head_size ** (-0.5), *refs)

    return pl.pallas_call(
        body,
        grid=(head_count,),
        in_specs=[pl.BlockSpec((head_size, cand), lambda h: (h, 0))]
        + [event_spec] * 4
        + [bias_spec] * 2
        + [live_spec] * 2,
        out_specs=pl.BlockSpec((cand, head_size), lambda h: (0, h)),
        out_shape=jax.ShapeDtypeStruct((cand, width), jnp.bfloat16),
        compiler_params=pltpu.CompilerParams(vmem_limit_bytes=32 * 1024 * 1024),
        cost_estimate=pl.CostEstimate(
            flops=8 * cand * events * width,
            bytes_accessed=8 * events * width + 4 * cand * width,
            transcendentals=2 * cand * events * head_count,
        ),
    )(queries, keys[0], keys[1], values[0], values[1], bias[0], bias[1], live[0], live[1])


def local(
    history_keys, history_values, lengths, item_ids, item_table, w_proj, rab, norm_gain, w_out
):
    device_count = lax.axis_size("seq")
    column = device_count // 2
    index_here = lax.axis_index("seq")
    place, side = index_here // 2, index_here % 2
    events_here, width = history_keys.shape
    head_count = rab.shape[0]
    head_size = width // head_count
    scale = head_size ** (-0.5)
    table_rows = item_table.shape[0]
    cand_total = item_ids.shape[0]
    cand_here = cand_total // device_count
    cand_side = cand_total // 2
    feature_here = w_proj.shape[2]
    length = lengths[0]

    ids = item_ids.reshape(column, 2, cand_here).transpose(1, 0, 2).reshape(cand_total)
    shard = ids // table_rows
    row_there = ids - shard * table_rows
    same = shard[:, None] == shard[None, :]
    order = jnp.arange(cand_total, dtype=jnp.int32)
    rank = jnp.sum((same & (order[None, :] < order[:, None])).astype(jnp.int32), axis=1)
    most = jnp.max(rank) + 1

    w_mine = w_proj.reshape(width, 4 * feature_here)
    w_other = swap_pair(w_mine)
    w_first = jnp.where(side == 0, w_mine, w_other).reshape(width, 4, 1, feature_here)
    w_second = jnp.where(side == 0, w_other, w_mine).reshape(width, 4, 1, feature_here)
    w_pair = jnp.concatenate([w_first, w_second], axis=2).reshape(width, 8 * feature_here)
    w_query = w_pair[:, 4 * feature_here : 6 * feature_here]
    keys = (history_keys, swap_pair(history_keys))
    values = (history_values, swap_pair(history_values))
    w_out_all = lax.all_gather(w_out, "seq", axis=0, tiled=True)

    def lookup(first_rank):
        slot = rank - first_rank
        slots_here = jnp.arange(slot_rows, dtype=jnp.int32)
        taken = (shard == index_here)[:, None] & (slot[:, None] == slots_here[None, :])
        slot_row = jnp.sum(jnp.where(taken, row_there[:, None], 0), axis=0)
        picks = (
            slot_row[:, None] == jnp.arange(table_rows, dtype=jnp.int32)[None, :]
        ).astype(jnp.bfloat16)
        packed = jnp.dot(picks, item_table, preferred_element_type=jnp.float32)
        rows = two_step_gather(packed.astype(jnp.bfloat16)).reshape(column * slot_rows, width)
        inside = (shard % 2 == side) & (slot >= 0) & (slot < slot_rows)
        source = shard // 2
        block = (source % near_places) * (column // near_places) + source // near_places
        at = jnp.where(inside, block * slot_rows + slot, -1)
        chosen = (
            at[:, None] == jnp.arange(column * slot_rows, dtype=jnp.int32)[None, :]
        ).astype(jnp.bfloat16)
        queries = jax.nn.silu(
            lax.dot_general(
                w_query, rows, (((0,), (1,)), ((), ())), preferred_element_type=jnp.float32
            )
        ).astype(jnp.bfloat16)
        queries = lax.dot_general(
            queries, chosen, (((1,), (1,)), ((), ())), preferred_element_type=jnp.float32
        ).astype(jnp.bfloat16)
        proj = jax.nn.silu(jnp.dot(rows, w_pair, preferred_element_type=jnp.float32)).astype(
            jnp.bfloat16
        )
        proj = jnp.dot(chosen, proj, preferred_element_type=jnp.float32).astype(jnp.bfloat16)
        pair_chosen = lax.dynamic_slice_in_dim(
            chosen.reshape(2, cand_side, column * slot_rows), place * cand_here, cand_here, 1
        ).reshape(2 * cand_here, column * slot_rows)
        embedded = jnp.dot(pair_chosen, rows, preferred_element_type=jnp.float32).astype(
            jnp.bfloat16
        )
        return queries, proj, embedded

    def another(state):
        first_rank, found = state
        more = lookup(first_rank)
        return first_rank + slot_rows, tuple(a + b for a, b in zip(found, more))

    _, (queries, proj, embedded) = lax.while_loop(
        lambda state: state[0] < most, another, (jnp.int32(slot_rows), lookup(jnp.int32(0)))
    )

    def join(both, axis, size):
        mine = lax.dynamic_slice_in_dim(both, side * size, size, axis)
        other = lax.dynamic_slice_in_dim(both, (1 - side) * size, size, axis)
        return mine + swap_pair(other)

    side_queries = join(queries, 1, cand_side)
    own_embedded = join(embedded, 0, cand_here)
    all_queries = lax.all_gather(
        side_queries, "seq", axis=0, tiled=True, axis_index_groups=column_groups()
    )
    own_proj = exchange(
        join(proj, 0, cand_side).reshape(column, cand_here, 8 * feature_here), column_groups()
    )
    own_proj = (
        own_proj.reshape(column, cand_here, 4, 2 * feature_here)
        .transpose(2, 1, 0, 3)
        .reshape(4, cand_here, width)
        .astype(jnp.float32)
    )
    gate_u, own_v, own_queries, own_k = own_proj[0], own_proj[1], own_proj[2], own_proj[3]

    def bias_of(index):
        positions = index * events_here + jnp.arange(events_here, dtype=jnp.int32)
        return (
            bucket_bias(rab, length - positions),
            (positions < length).astype(jnp.float32)[None, :],
        )

    bias, live = zip(bias_of(index_here), bias_of(index_here + 1 - 2 * side))
    summed = attend(all_queries, keys, values, bias, live, head_count)
    parts = exchange(summed.reshape(column, cand_here, width), column_groups())
    history_sum = jnp.sum(parts.astype(jnp.float32), axis=0)

    self_scores = jnp.sum((own_queries * own_k).reshape(cand_here, head_count, head_size), axis=2)
    self_scores = self_scores * scale + rab[:, 0][None, :]
    self_term = jax.nn.silu(self_scores)[:, :, None] * own_v.reshape(
        cand_here, head_count, head_size
    )
    attended = history_sum * lax.rsqrt(length.astype(jnp.float32)) + self_term.reshape(
        cand_here, width
    )
    centre = jnp.mean(attended, axis=1, keepdims=True)
    spread = jnp.mean((attended - centre) ** 2, axis=1, keepdims=True)
    normed = (attended - centre) * lax.rsqrt(spread + 1e-05) * norm_gain[None, :] * gate_u
    normed = normed.astype(jnp.bfloat16)
    projected = jnp.dot(normed, w_out_all, preferred_element_type=jnp.float32)
    return (projected + own_embedded.astype(jnp.float32)).astype(jnp.bfloat16)


def solution(mesh):
    return jax.shard_map(
        local,
        mesh=mesh,
        in_specs=(
            P(("batch", "seq"), None),
            P(("batch", "seq"), None),
            P("batch"),
            P("batch"),
            P("seq", None),
            P(None, None, "seq"),
            P(),
            P(),
            P("seq", None),
        ),
        out_specs=P(("batch", "seq"), None),
        check_vma=False,
    )
```

```python
import jax
import jax.numpy as jnp
from jax import lax
from jax.experimental import pallas as pl
from jax.experimental.pallas import tpu as pltpu
from jax.sharding import PartitionSpec as P

slot_rows = 32
near_places = 4


def groups_of(places):
    return [[2 * place + side for place in group] for side in range(2) for group in places]


def exchange(blocks, groups):
    return lax.all_to_all(
        blocks, "seq", split_axis=0, concat_axis=0, tiled=True, axis_index_groups=groups
    )


def column_groups():
    return groups_of([list(range(lax.axis_size("seq") // 2))])


def from_place(block, shift):
    count = lax.axis_size("seq")
    return lax.ppermute(block, "seq", [(i, (i + 2 * shift) % count) for i in range(count)])


def swap_pair(block):
    return lax.ppermute(block, "seq", [(i, i ^ 1) for i in range(lax.axis_size("seq"))])


def swap_core(block):
    return lax.ppermute(block, "batch", [(i, i ^ 1) for i in range(lax.axis_size("batch"))])


def from_row(block, shift):
    count = lax.axis_size("batch")
    return lax.ppermute(block, "batch", [(i, (i + 4 * shift) % count) for i in range(count)])


def gather_slots(block):
    column = lax.axis_size("seq") // 2
    far_places = column // near_places
    far = groups_of([list(range(at, column, near_places)) for at in range(near_places)])
    blocks = exchange(jnp.broadcast_to(block[None], (far_places,) + block.shape), far)
    rows = blocks.reshape(far_places * block.shape[0], block.shape[1])
    half = rows.shape[0] // 2
    return (
        rows,
        from_place(rows, 1),
        from_place(rows, -1),
        from_place(rows[:half], 2),
        from_place(rows[half:], -2),
    )


def bucket_bias(rab_table, distance):
    bucket_count = rab_table.shape[1]
    powers = 2 ** jnp.arange(bucket_count - 1, dtype=jnp.int32)
    bucket = jnp.sum((distance[:, None] >= powers[None, :]).astype(jnp.int32), axis=1)
    hits = (bucket[None, :] == jnp.arange(bucket_count, dtype=jnp.int32)[:, None]).astype(
        jnp.float32
    )
    return jnp.dot(
        rab_table, hits, precision=lax.Precision.HIGHEST, preferred_element_type=jnp.float32
    )


def silu(value):
    return value * (0.5 + 0.5 * jnp.tanh(0.5 * value))


def project_kernel(at, at_pair, rows_0, rows_1, rows_2, rows_3, rows_4, weights, *rest):
    proj_mine, proj_other, own_rows, other_rows, slots = rest
    cand_side = proj_mine.shape[0]
    own = own_rows.shape[0]
    first = 0
    for rows in (rows_0, rows_1, rows_2, rows_3, rows_4):
        count = rows.shape[0]
        slots[first : first + count, :] = silu(
            jnp.dot(rows[...], weights[...], preferred_element_type=jnp.float32)
        ).astype(jnp.bfloat16)
        first += count
    place = lax.broadcasted_iota(jnp.int32, (cand_side, first), 1)
    for side, proj in ((0, proj_mine), (1, proj_other)):
        chosen = (at[side * cand_side : (side + 1) * cand_side, :] == place).astype(jnp.float32)
        proj[...] = jnp.dot(
            chosen.astype(jnp.bfloat16), slots[...], preferred_element_type=jnp.float32
        ).astype(jnp.bfloat16)
    place = lax.broadcasted_iota(jnp.int32, (2 * own, first), 1)
    chosen = (at_pair[...] == place).astype(jnp.float32).astype(jnp.bfloat16)
    total = None
    first = 0
    for rows in (rows_0, rows_1, rows_2, rows_3, rows_4):
        count = rows.shape[0]
        part = jnp.dot(
            chosen[:, first : first + count], rows[...], preferred_element_type=jnp.float32
        )
        total = part if total is None else total + part
        first += count
    own_rows[...] = total[:own].astype(jnp.bfloat16)
    other_rows[...] = total[own:].astype(jnp.bfloat16)


def project(at, at_pair, rows, weights):
    width, columns = weights.shape
    cand_side = at.shape[0] // 2
    own = at_pair.shape[0] // 2
    slot_count = sum(piece.shape[0] for piece in rows)
    return pl.pallas_call(
        project_kernel,
        out_shape=[jax.ShapeDtypeStruct((cand_side, columns), jnp.bfloat16)] * 2
        + [jax.ShapeDtypeStruct((own, width), jnp.bfloat16)] * 2,
        scratch_shapes=[pltpu.VMEM((slot_count, columns), jnp.bfloat16)],
        compiler_params=pltpu.CompilerParams(vmem_limit_bytes=32 * 1024 * 1024),
        cost_estimate=pl.CostEstimate(
            flops=2 * slot_count * columns * (width + 2 * cand_side),
            bytes_accessed=2 * (slot_count + columns) * width,
            transcendentals=slot_count * columns,
        ),
    )(at, at_pair, *rows, weights)


def pack_kernel(feature_here, mine, arrived, w_slice, *rest):
    queries, packed = rest[-2:]
    proj = mine[...].astype(jnp.float32) + arrived[...].astype(jnp.float32)
    block = 4 * feature_here
    query = jnp.concatenate(
        [proj[:, side * block + 2 * feature_here : side * block + 3 * feature_here] for side in (0, 1)],
        axis=1,
    )
    queries[...] = query.T.astype(jnp.bfloat16)
    column, own, _ = packed.shape
    columns = 2 * block
    packed[:, :, :columns] = proj.astype(jnp.bfloat16).reshape(column, own, columns)
    lanes = w_slice.shape[1]
    for part in range(w_slice.shape[0] // own):
        packed[:, :, columns + part * lanes : columns + (part + 1) * lanes] = jnp.broadcast_to(
            w_slice[part * own : (part + 1) * own, :][None], (column, own, lanes)
        )


def pack(mine, arrived, w_slice, ready, feature_here, own):
    cand_side, columns = mine.shape
    column = cand_side // own
    packed_width = columns + w_slice.shape[0] * w_slice.shape[1] // own
    whole = pl.BlockSpec(memory_space=pltpu.VMEM)
    return pl.pallas_call(
        lambda *refs: pack_kernel(feature_here, *refs),
        in_specs=[whole] * 3 + [pl.BlockSpec(memory_space=pl.ANY)] * len(ready),
        out_specs=[whole] * 2,
        out_shape=[
            jax.ShapeDtypeStruct((2 * feature_here, cand_side), jnp.bfloat16),
            jax.ShapeDtypeStruct((column, own, packed_width), jnp.bfloat16),
        ],
        compiler_params=pltpu.CompilerParams(vmem_limit_bytes=32 * 1024 * 1024),
        cost_estimate=pl.CostEstimate(
            flops=cand_side * columns, bytes_accessed=8 * cand_side * columns, transcendentals=0
        ),
    )(mine, arrived, w_slice, *ready)


def attend_kernel(scale, *refs):
    queries, keys_a, keys_b, values_a, values_b, bias_a, bias_b, live_a, live_b = refs[:9]
    summed = refs[-3]
    head = pl.program_id(0)
    head_queries = queries[...].T
    total = None
    for keys, values, bias, live in (
        (keys_a, values_a, bias_a, live_a),
        (keys_b, values_b, bias_b, live_b),
    ):
        scores = lax.dot_general(
            head_queries, keys[...], (((1,), (1,)), ((), ())), preferred_element_type=jnp.float32
        )
        weights = silu(scores * scale + bias[pl.ds(head, 1), :])
        weights = jnp.where(live[...] > 0.0, weights, 0.0).astype(jnp.bfloat16)
        part = jnp.dot(weights, values[...], preferred_element_type=jnp.float32)
        total = part if total is None else total + part
    summed[...] = total.astype(summed.dtype)


def attend(queries, keys, values, bias, live, head_count, through):
    width, cand = queries.shape
    events = keys[0].shape[0]
    head_size = width // head_count
    event_spec = pl.BlockSpec((events, head_size), lambda h: (0, h))
    bias_spec = pl.BlockSpec((head_count, events), lambda h: (0, 0))
    live_spec = pl.BlockSpec((1, events), lambda h: (0, 0))
    held = pl.BlockSpec(memory_space=pl.ANY)
    return pl.pallas_call(
        lambda *refs: attend_kernel(head_size ** (-0.5), *refs),
        grid=(head_count,),
        in_specs=[pl.BlockSpec((head_size, cand), lambda h: (h, 0))]
        + [event_spec] * 4
        + [bias_spec] * 2
        + [live_spec] * 2
        + [held] * 2,
        out_specs=[pl.BlockSpec((cand, head_size), lambda h: (0, h)), held, held],
        out_shape=[jax.ShapeDtypeStruct((cand, width), jnp.bfloat16)]
        + [jax.ShapeDtypeStruct(array.shape, array.dtype) for array in through],
        input_output_aliases={9: 1, 10: 2},
        compiler_params=pltpu.CompilerParams(vmem_limit_bytes=32 * 1024 * 1024),
        cost_estimate=pl.CostEstimate(
            flops=8 * cand * events * width,
            bytes_accessed=8 * events * width + 4 * cand * width,
            transcendentals=2 * cand * events * head_count,
        ),
    )(queries, *keys, *values, *bias, *live, *through)


def finish_kernel(numbers, parts, self_term, gate, embedded, weights_a, weights_b, scored):
    history_sum = parts[0].astype(jnp.float32)
    for part in range(1, parts.shape[0]):
        history_sum = history_sum + parts[part].astype(jnp.float32)
    length = jnp.full((1, 1), numbers[0], jnp.int32).astype(jnp.float32)
    attended = history_sum * lax.rsqrt(length) + self_term[...]
    centre = jnp.mean(attended, axis=1, keepdims=True)
    spread = jnp.mean((attended - centre) ** 2, axis=1, keepdims=True)
    normed = (attended - centre) * lax.rsqrt(spread + 1e-05) * gate[...]
    normed = normed.astype(jnp.bfloat16)
    row_count, _, lanes = weights_a.shape
    row, core = numbers[1], numbers[2]
    for weights, owner in ((weights_a, core), (weights_b, 1 - core)):
        for shift in range(row_count):
            block = owner * row_count + lax.rem(row + row_count - shift, row_count)
            columns = pl.ds(pl.multiple_of(block * lanes, lanes), lanes)
            projected = jnp.dot(normed, weights[shift], preferred_element_type=jnp.float32)
            scored[:, columns] = (
                projected + embedded[:, columns].astype(jnp.float32)
            ).astype(scored.dtype)


def finish(numbers, parts, self_term, gate, embedded, weights_a, weights_b):
    whole = pl.BlockSpec(memory_space=pltpu.VMEM)
    rows, width = embedded.shape
    return pl.pallas_call(
        finish_kernel,
        in_specs=[pl.BlockSpec(memory_space=pltpu.SMEM)] + [whole] * 6,
        out_specs=whole,
        out_shape=jax.ShapeDtypeStruct((rows, width), jnp.bfloat16),
        compiler_params=pltpu.CompilerParams(vmem_limit_bytes=32 * 1024 * 1024),
        cost_estimate=pl.CostEstimate(
            flops=2 * rows * width * width, bytes_accessed=4 * width * width, transcendentals=0
        ),
    )(numbers, parts, self_term, gate, embedded, weights_a, weights_b)


def local(
    history_keys, history_values, lengths, item_ids, item_table, w_proj, rab, norm_gain, w_out
):
    device_count = lax.axis_size("seq")
    column = device_count // 2
    index_here = lax.axis_index("seq")
    place, side = index_here // 2, index_here % 2
    batch_here = lax.axis_index("batch")
    row, core = batch_here // 4, batch_here % 2
    row_count = lax.axis_size("batch") // 4
    events_here, width = history_keys.shape
    head_count = rab.shape[0]
    head_size = width // head_count
    scale = head_size ** (-0.5)
    table_rows = item_table.shape[0]
    cand_total = item_ids.shape[0]
    cand_here = cand_total // device_count
    cand_side = cand_total // 2
    feature_here = w_proj.shape[2]
    out_lanes = width // (2 * row_count)
    length = lengths[0]

    by_side = jnp.arange(cand_total, dtype=jnp.int32).reshape(column, 2, cand_here)
    by_side = by_side.transpose(1, 0, 2).reshape(2, cand_side)
    ids = item_ids.reshape(column, 2, cand_here).transpose(1, 0, 2).reshape(2, cand_side)
    order = jnp.where(side == 0, by_side, by_side[::-1]).reshape(cand_total)
    ids = jnp.where(side == 0, ids, ids[::-1]).reshape(cand_total)
    shard = ids // table_rows
    row_there = ids - shard * table_rows
    same = shard[:, None] == shard[None, :]
    rank = jnp.sum((same & (order[None, :] < order[:, None])).astype(jnp.int32), axis=1)
    most = jnp.max(rank) + 1

    w_mine = w_proj.reshape(width, 4 * feature_here)
    w_other = swap_pair(w_mine)
    w_pair = jnp.concatenate(
        [jnp.where(side == 0, w_mine, w_other), jnp.where(side == 0, w_other, w_mine)], axis=1
    )
    keys = (history_keys, swap_pair(history_keys))
    values = (history_values, swap_pair(history_values))
    w_slice = lax.dynamic_slice_in_dim(w_out, (core * row_count + row) * out_lanes, out_lanes, 1)

    def lookup(first_rank):
        slot = rank - first_rank
        slots_here = jnp.arange(slot_rows, dtype=jnp.int32)
        taken = (shard == index_here)[:, None] & (slot[:, None] == slots_here[None, :])
        slot_row = jnp.sum(jnp.where(taken, row_there[:, None], 0), axis=0)
        picks = (
            slot_row[:, None] == jnp.arange(table_rows, dtype=jnp.int32)[None, :]
        ).astype(jnp.bfloat16)
        packed = jnp.dot(picks, item_table, preferred_element_type=jnp.float32)
        rows = gather_slots(packed.astype(jnp.bfloat16))
        inside = (shard % 2 == side) & (slot >= 0) & (slot < slot_rows)
        source = shard // 2
        ahead = (source - place) % near_places
        piece = jnp.where(ahead == 0, 0, jnp.where(ahead == near_places - 1, 1, ahead + 1))
        block = piece * (column // near_places) + source // near_places
        at = jnp.where(inside, block * slot_rows + slot, -1)
        at_pair = lax.dynamic_slice_in_dim(
            at.reshape(2, cand_side), place * cand_here, cand_here, 1
        )
        return tuple(
            project(at.reshape(cand_total, 1), at_pair.reshape(2 * cand_here, 1), rows, w_pair)
        )

    def another(state):
        first_rank, found = state
        more = lookup(first_rank)
        return first_rank + slot_rows, tuple(a + b for a, b in zip(found, more))

    _, (proj_mine, proj_other, own_rows, other_rows) = lax.while_loop(
        lambda state: state[0] < most, another, (jnp.int32(slot_rows), lookup(jnp.int32(0)))
    )
    side_queries, packed = pack(
        proj_mine, swap_pair(proj_other), w_slice, (keys[1], values[1]), feature_here, cand_here
    )
    received = exchange(packed, column_groups())
    all_queries = lax.all_gather(
        side_queries, "seq", axis=0, tiled=True, axis_index_groups=column_groups()
    )

    def bias_of(index):
        positions = index * events_here + jnp.arange(events_here, dtype=jnp.int32)
        return (
            bucket_bias(rab, length - positions),
            (positions < length).astype(jnp.float32)[None, :],
        )

    bias, live = zip(bias_of(index_here), bias_of(index_here + 1 - 2 * side))
    summed, received, other_rows = attend(
        all_queries, keys, values, bias, live, head_count, (received, other_rows)
    )
    parts = exchange(summed.reshape(column, cand_here, width), column_groups())
    embedded = own_rows + swap_pair(other_rows)

    own_proj = (
        received[:, :, : 8 * feature_here]
        .reshape(column, cand_here, 2, 4, feature_here)
        .transpose(3, 1, 0, 2, 4)
        .reshape(4, cand_here, width)
        .astype(jnp.float32)
    )
    gate_u, own_v, own_queries, own_k = own_proj[0], own_proj[1], own_proj[2], own_proj[3]
    self_scores = jnp.sum((own_queries * own_k).reshape(cand_here, head_count, head_size), axis=2)
    self_scores = self_scores * scale + rab[:, 0][None, :]
    self_term = jax.nn.silu(self_scores)[:, :, None] * own_v.reshape(
        cand_here, head_count, head_size
    )
    self_term = self_term.reshape(cand_here, width)
    gate = norm_gain[None, :] * gate_u

    w_here = (
        received[:, :, 8 * feature_here :]
        .reshape(column, cand_here, -1, out_lanes)
        .transpose(0, 2, 1, 3)
        .reshape(column, 1, -1, out_lanes)
    )
    w_rows = jnp.stack(
        [w_here] + [from_row(w_here, shift) for shift in range(1, row_count)], axis=0
    )
    w_far = swap_pair(w_rows)
    w_rows = jnp.concatenate(
        [jnp.where(side == 0, w_rows, w_far), jnp.where(side == 0, w_far, w_rows)], axis=2
    ).reshape(row_count, width, out_lanes)
    w_core = swap_core(w_rows)
    numbers = jnp.stack([length, row, core])
    return finish(numbers, parts, self_term, gate, embedded, w_rows, w_core)


def solution(mesh):
    return jax.shard_map(
        local,
        mesh=mesh,
        in_specs=(
            P(("batch", "seq"), None),
            P(("batch", "seq"), None),
            P("batch"),
            P("batch"),
            P("seq", None),
            P(None, None, "seq"),
            P(),
            P(),
            P("seq", None),
        ),
        out_specs=P(("batch", "seq"), None),
        check_vma=False,
    )
```

```python
import jax
import jax.numpy as jnp
from jax import lax
from jax.experimental import pallas as pl
from jax.experimental.pallas import tpu as pltpu
from jax.sharding import PartitionSpec as P

slot_rows = 32
near_places = 4


def groups_of(places):
    return [[2 * place + side for place in group] for side in range(2) for group in places]


def exchange(blocks, groups):
    return lax.all_to_all(
        blocks, "seq", split_axis=0, concat_axis=0, tiled=True, axis_index_groups=groups
    )


def column_groups():
    return groups_of([list(range(lax.axis_size("seq") // 2))])


def from_place(block, shift):
    count = lax.axis_size("seq")
    return lax.ppermute(block, "seq", [(i, (i + 2 * shift) % count) for i in range(count)])


def swap_pair(block):
    return lax.ppermute(block, "seq", [(i, i ^ 1) for i in range(lax.axis_size("seq"))])


def from_replica(block, rows, cores):
    count = lax.axis_size("batch")
    return lax.ppermute(
        block, "batch", [(i, ((i + 4 * rows) % count) ^ cores) for i in range(count)]
    )


def gather_slots(block):
    column = lax.axis_size("seq") // 2
    far_places = column // near_places
    far = groups_of([list(range(at, column, near_places)) for at in range(near_places)])
    blocks = exchange(jnp.broadcast_to(block[None], (far_places,) + block.shape), far)
    rows = blocks.reshape(far_places * block.shape[0], block.shape[1])
    half = rows.shape[0] // 2
    return (
        rows,
        from_place(rows, 1),
        from_place(rows, -1),
        from_place(rows[:half], 2),
        from_place(rows[half:], -2),
    )


def bucket_bias(rab_table, distance):
    bucket_count = rab_table.shape[1]
    powers = 2 ** jnp.arange(bucket_count - 1, dtype=jnp.int32)
    bucket = jnp.sum((distance[:, None] >= powers[None, :]).astype(jnp.int32), axis=1)
    hits = (bucket[None, :] == jnp.arange(bucket_count, dtype=jnp.int32)[:, None]).astype(
        jnp.float32
    )
    return jnp.dot(
        rab_table, hits, precision=lax.Precision.HIGHEST, preferred_element_type=jnp.float32
    )


def silu(value):
    return value * (0.5 + 0.5 * jnp.tanh(0.5 * value))


def pick_kernel(numbers, ids, table, packed):
    rows, count = table.shape[0], ids.shape[1]
    there = ids[...] - numbers[0] * rows
    here = (there >= 0) & (there < rows)
    before = lax.broadcasted_iota(jnp.int32, (count, count), 0) < lax.broadcasted_iota(
        jnp.int32, (count, count), 1
    )
    marks = jnp.broadcast_to(here.astype(jnp.float32), (8, count)).astype(jnp.bfloat16)
    rank = jnp.dot(
        marks,
        before.astype(jnp.float32).astype(jnp.bfloat16),
        preferred_element_type=jnp.float32,
    )[:1].astype(jnp.int32)
    slot = jnp.where(here, rank - numbers[1], -1)
    taken = slot == lax.broadcasted_iota(jnp.int32, (packed.shape[0], count), 0)
    wanted = there == lax.broadcasted_iota(jnp.int32, (rows, count), 0)
    picks = lax.dot_general(
        taken.astype(jnp.float32).astype(jnp.bfloat16),
        wanted.astype(jnp.float32).astype(jnp.bfloat16),
        (((1,), (1,)), ((), ())),
        preferred_element_type=jnp.float32,
    ).astype(jnp.bfloat16)
    packed[...] = jnp.dot(picks, table[...], preferred_element_type=jnp.float32).astype(
        jnp.bfloat16
    )


def pick(numbers, ids, table):
    whole = pl.BlockSpec(memory_space=pltpu.VMEM)
    return pl.pallas_call(
        pick_kernel,
        in_specs=[pl.BlockSpec(memory_space=pltpu.SMEM), whole, whole],
        out_specs=whole,
        out_shape=jax.ShapeDtypeStruct((slot_rows, table.shape[1]), jnp.bfloat16),
        compiler_params=pltpu.CompilerParams(vmem_limit_bytes=32 * 1024 * 1024),
        cost_estimate=pl.CostEstimate(
            flops=2 * slot_rows * table.shape[0] * table.shape[1],
            bytes_accessed=2 * table.shape[0] * table.shape[1],
            transcendentals=0,
        ),
    )(numbers, ids.reshape(1, -1), table)


def project_kernel(at, at_pair, rows_0, rows_1, rows_2, rows_3, rows_4, weights, *rest):
    proj_mine, proj_other, own_rows, other_rows, slots = rest
    cand_side = proj_mine.shape[0]
    own = own_rows.shape[0]
    first = 0
    for rows in (rows_0, rows_1, rows_2, rows_3, rows_4):
        count = rows.shape[0]
        slots[first : first + count, :] = silu(
            jnp.dot(rows[...], weights[...], preferred_element_type=jnp.float32)
        ).astype(jnp.bfloat16)
        first += count
    place = lax.broadcasted_iota(jnp.int32, (cand_side, first), 1)
    for side, proj in ((0, proj_mine), (1, proj_other)):
        chosen = (at[side * cand_side : (side + 1) * cand_side, :] == place).astype(jnp.float32)
        proj[...] = jnp.dot(
            chosen.astype(jnp.bfloat16), slots[...], preferred_element_type=jnp.float32
        ).astype(jnp.bfloat16)
    place = lax.broadcasted_iota(jnp.int32, (2 * own, first), 1)
    chosen = (at_pair[...] == place).astype(jnp.float32).astype(jnp.bfloat16)
    total = None
    first = 0
    for rows in (rows_0, rows_1, rows_2, rows_3, rows_4):
        count = rows.shape[0]
        part = jnp.dot(
            chosen[:, first : first + count], rows[...], preferred_element_type=jnp.float32
        )
        total = part if total is None else total + part
        first += count
    own_rows[...] = total[:own].astype(jnp.bfloat16)
    other_rows[...] = total[own:].astype(jnp.bfloat16)


def project(at, at_pair, rows, weights):
    width, columns = weights.shape
    cand_side = at.shape[0] // 2
    own = at_pair.shape[0] // 2
    slot_count = sum(piece.shape[0] for piece in rows)
    return pl.pallas_call(
        project_kernel,
        out_shape=[jax.ShapeDtypeStruct((cand_side, columns), jnp.bfloat16)] * 2
        + [jax.ShapeDtypeStruct((own, width), jnp.bfloat16)] * 2,
        scratch_shapes=[pltpu.VMEM((slot_count, columns), jnp.bfloat16)],
        compiler_params=pltpu.CompilerParams(vmem_limit_bytes=32 * 1024 * 1024),
        cost_estimate=pl.CostEstimate(
            flops=2 * slot_count * columns * (width + 2 * cand_side),
            bytes_accessed=2 * (slot_count + columns) * width,
            transcendentals=slot_count * columns,
        ),
    )(at, at_pair, *rows, weights)


def pack_kernel(feature_here, mine, arrived, w_slice, *rest):
    queries, packed = rest[-2:]
    proj = mine[...].astype(jnp.float32) + arrived[...].astype(jnp.float32)
    block = 4 * feature_here
    query = jnp.concatenate(
        [proj[:, side * block + 2 * feature_here : side * block + 3 * feature_here] for side in (0, 1)],
        axis=1,
    )
    queries[...] = query.T.astype(jnp.bfloat16)
    column, own, _ = packed.shape
    columns = 2 * block
    packed[:, :, :columns] = proj.astype(jnp.bfloat16).reshape(column, own, columns)
    lanes = w_slice.shape[1]
    for part in range(w_slice.shape[0] // own):
        packed[:, :, columns + part * lanes : columns + (part + 1) * lanes] = jnp.broadcast_to(
            w_slice[part * own : (part + 1) * own, :][None], (column, own, lanes)
        )


def pack(mine, arrived, w_slice, ready, feature_here, own):
    cand_side, columns = mine.shape
    column = cand_side // own
    packed_width = columns + w_slice.shape[0] * w_slice.shape[1] // own
    whole = pl.BlockSpec(memory_space=pltpu.VMEM)
    return pl.pallas_call(
        lambda *refs: pack_kernel(feature_here, *refs),
        in_specs=[whole] * 3 + [pl.BlockSpec(memory_space=pl.ANY)] * len(ready),
        out_specs=[whole] * 2,
        out_shape=[
            jax.ShapeDtypeStruct((2 * feature_here, cand_side), jnp.bfloat16),
            jax.ShapeDtypeStruct((column, own, packed_width), jnp.bfloat16),
        ],
        compiler_params=pltpu.CompilerParams(vmem_limit_bytes=32 * 1024 * 1024),
        cost_estimate=pl.CostEstimate(
            flops=cand_side * columns, bytes_accessed=8 * cand_side * columns, transcendentals=0
        ),
    )(mine, arrived, w_slice, *ready)


def attend_kernel(scale, *refs):
    queries, keys_a, keys_b, values_a, values_b, bias_a, bias_b, live_a, live_b = refs[:9]
    summed = refs[-3]
    head = pl.program_id(0)
    head_queries = queries[...].T
    total = None
    for keys, values, bias, live in (
        (keys_a, values_a, bias_a, live_a),
        (keys_b, values_b, bias_b, live_b),
    ):
        scores = lax.dot_general(
            head_queries, keys[...], (((1,), (1,)), ((), ())), preferred_element_type=jnp.float32
        )
        weights = silu(scores * scale + bias[pl.ds(head, 1), :])
        weights = jnp.where(live[...] > 0.0, weights, 0.0).astype(jnp.bfloat16)
        part = jnp.dot(weights, values[...], preferred_element_type=jnp.float32)
        total = part if total is None else total + part
    summed[...] = total.astype(summed.dtype)


def attend(queries, keys, values, bias, live, head_count, through):
    width, cand = queries.shape
    events = keys[0].shape[0]
    head_size = width // head_count
    event_spec = pl.BlockSpec((events, head_size), lambda h: (0, h))
    bias_spec = pl.BlockSpec((head_count, events), lambda h: (0, 0))
    live_spec = pl.BlockSpec((1, events), lambda h: (0, 0))
    held = pl.BlockSpec(memory_space=pl.ANY)
    return pl.pallas_call(
        lambda *refs: attend_kernel(head_size ** (-0.5), *refs),
        grid=(head_count,),
        in_specs=[pl.BlockSpec((head_size, cand), lambda h: (h, 0))]
        + [event_spec] * 4
        + [bias_spec] * 2
        + [live_spec] * 2
        + [held] * 2,
        out_specs=[pl.BlockSpec((cand, head_size), lambda h: (0, h)), held, held],
        out_shape=[jax.ShapeDtypeStruct((cand, width), jnp.bfloat16)]
        + [jax.ShapeDtypeStruct(array.shape, array.dtype) for array in through],
        input_output_aliases={9: 1, 10: 2},
        compiler_params=pltpu.CompilerParams(vmem_limit_bytes=32 * 1024 * 1024),
        cost_estimate=pl.CostEstimate(
            flops=8 * cand * events * width,
            bytes_accessed=8 * events * width + 4 * cand * width,
            transcendentals=2 * cand * events * head_count,
        ),
    )(queries, *keys, *values, *bias, *live, *through)


def finish_kernel(numbers, parts, self_term, gate, embedded, *rest):
    weights, scored = rest[:-1], rest[-1]
    history_sum = parts[0].astype(jnp.float32)
    for part in range(1, parts.shape[0]):
        history_sum = history_sum + parts[part].astype(jnp.float32)
    length = jnp.full((1, 1), numbers[0], jnp.int32).astype(jnp.float32)
    attended = history_sum * lax.rsqrt(length) + self_term[...]
    centre = jnp.mean(attended, axis=1, keepdims=True)
    spread = jnp.mean((attended - centre) ** 2, axis=1, keepdims=True)
    normed = (attended - centre) * lax.rsqrt(spread + 1e-05) * gate[...]
    normed = normed.astype(jnp.bfloat16)
    lanes = weights[0].shape[1]
    row_count = len(weights) // 2
    row, core = numbers[1], numbers[2]
    for index, columns_of in enumerate(weights):
        owner = core if index < row_count else 1 - core
        block = owner * row_count + lax.rem(row + row_count - index % row_count, row_count)
        columns = pl.ds(pl.multiple_of(block * lanes, lanes), lanes)
        projected = jnp.dot(normed, columns_of[...], preferred_element_type=jnp.float32)
        scored[:, columns] = (projected + embedded[:, columns].astype(jnp.float32)).astype(
            scored.dtype
        )


def finish(numbers, parts, self_term, gate, embedded, weights):
    whole = pl.BlockSpec(memory_space=pltpu.VMEM)
    rows, width = embedded.shape
    return pl.pallas_call(
        finish_kernel,
        in_specs=[pl.BlockSpec(memory_space=pltpu.SMEM)] + [whole] * (4 + len(weights)),
        out_specs=whole,
        out_shape=jax.ShapeDtypeStruct((rows, width), jnp.bfloat16),
        compiler_params=pltpu.CompilerParams(vmem_limit_bytes=32 * 1024 * 1024),
        cost_estimate=pl.CostEstimate(
            flops=2 * rows * width * width, bytes_accessed=4 * width * width, transcendentals=0
        ),
    )(numbers, parts, self_term, gate, embedded, *weights)


def local(
    history_keys, history_values, lengths, item_ids, item_table, w_proj, rab, norm_gain, w_out
):
    device_count = lax.axis_size("seq")
    column = device_count // 2
    index_here = lax.axis_index("seq")
    place, side = index_here // 2, index_here % 2
    batch_here = lax.axis_index("batch")
    row, core = batch_here // 4, batch_here % 2
    row_count = lax.axis_size("batch") // 4
    events_here, width = history_keys.shape
    head_count = rab.shape[0]
    head_size = width // head_count
    scale = head_size ** (-0.5)
    table_rows = item_table.shape[0]
    cand_total = item_ids.shape[0]
    cand_here = cand_total // device_count
    cand_side = cand_total // 2
    feature_here = w_proj.shape[2]
    out_lanes = width // (2 * row_count)
    length = lengths[0]

    by_side = jnp.arange(cand_total, dtype=jnp.int32).reshape(column, 2, cand_here)
    by_side = by_side.transpose(1, 0, 2).reshape(2, cand_side)
    ids = item_ids.reshape(column, 2, cand_here).transpose(1, 0, 2).reshape(2, cand_side)
    order = jnp.where(side == 0, by_side, by_side[::-1]).reshape(cand_total)
    ids = jnp.where(side == 0, ids, ids[::-1]).reshape(cand_total)
    shard = ids // table_rows
    row_there = ids - shard * table_rows
    same = shard[:, None] == shard[None, :]
    rank = jnp.sum((same & (order[None, :] < order[:, None])).astype(jnp.int32), axis=1)
    most = jnp.max(rank) + 1

    w_slice = lax.dynamic_slice_in_dim(w_out, (core * row_count + row) * out_lanes, out_lanes, 1)
    slice_rows = w_slice.shape[0]

    def lookup(first_rank, send):
        packed = pick(jnp.stack([index_here, first_rank]), item_ids, item_table)
        packed, send = lax.optimization_barrier((packed, send))
        return gather_slots(packed), [swap_pair(block) for block in send]

    def place_of(first_rank):
        slot = rank - first_rank
        inside = (shard % 2 == side) & (slot >= 0) & (slot < slot_rows)
        source = shard // 2
        ahead = (source - place) % near_places
        piece = jnp.where(ahead == 0, 0, jnp.where(ahead == near_places - 1, 1, ahead + 1))
        block = piece * (column // near_places) + source // near_places
        at = jnp.where(inside, block * slot_rows + slot, -1)
        at_pair = lax.dynamic_slice_in_dim(
            at.reshape(2, cand_side), place * cand_here, cand_here, 1
        )
        return at.reshape(cand_total, 1), at_pair.reshape(2 * cand_here, 1)

    w_mine = w_proj.reshape(width, 4 * feature_here)
    w_send = jnp.concatenate([w_mine, w_slice.reshape(-1, 4 * feature_here)])
    rows, (w_other, keys_other, values_other) = lookup(
        jnp.int32(0), (w_send, history_keys, history_values)
    )
    slice_other = w_other[width:].reshape(w_slice.shape)
    w_other = w_other[:width]
    keys, values = (history_keys, keys_other), (history_values, values_other)
    w_pair = jnp.concatenate(
        [jnp.where(side == 0, w_mine, w_other), jnp.where(side == 0, w_other, w_mine)], axis=1
    )
    slices = jnp.concatenate(
        [jnp.where(side == 0, w_slice, slice_other), jnp.where(side == 0, slice_other, w_slice)]
    )
    found = tuple(project(*place_of(jnp.int32(0)), rows, w_pair))

    def another(state):
        first_rank, found = state
        rows, _ = lookup(first_rank, ())
        more = project(*place_of(first_rank), rows, w_pair)
        return first_rank + slot_rows, tuple(a + b for a, b in zip(found, more))

    _, (proj_mine, proj_other, own_rows, other_rows) = lax.while_loop(
        lambda state: state[0] < most, another, (jnp.int32(slot_rows), found)
    )
    side_queries, packed = pack(
        proj_mine, swap_pair(proj_other), slices, (keys_other,), feature_here, cand_here
    )
    received = exchange(packed, column_groups())
    all_queries = lax.all_gather(
        side_queries, "seq", axis=0, tiled=True, axis_index_groups=column_groups()
    )

    def bias_of(index):
        positions = index * events_here + jnp.arange(events_here, dtype=jnp.int32)
        return (
            bucket_bias(rab, length - positions),
            (positions < length).astype(jnp.float32)[None, :],
        )

    bias, live = zip(bias_of(index_here), bias_of(index_here + 1 - 2 * side))
    summed, received, other_rows = attend(
        all_queries, keys, values, bias, live, head_count, (received, other_rows)
    )
    parts = exchange(summed.reshape(column, cand_here, width), column_groups())
    embedded = own_rows + swap_pair(other_rows)

    own_proj = (
        received[:, :, : 8 * feature_here]
        .reshape(column, cand_here, 2, 4, feature_here)
        .transpose(3, 1, 0, 2, 4)
        .reshape(4, cand_here, width)
        .astype(jnp.float32)
    )
    gate_u, own_v, own_queries, own_k = own_proj[0], own_proj[1], own_proj[2], own_proj[3]
    self_scores = jnp.sum((own_queries * own_k).reshape(cand_here, head_count, head_size), axis=2)
    self_scores = self_scores * scale + rab[:, 0][None, :]
    self_term = jax.nn.silu(self_scores)[:, :, None] * own_v.reshape(
        cand_here, head_count, head_size
    )
    self_term = self_term.reshape(cand_here, width)
    gate = norm_gain[None, :] * gate_u

    w_here = (
        received[:, :, 8 * feature_here :]
        .reshape(column, cand_here, 2 * slice_rows // cand_here, out_lanes)
        .transpose(0, 2, 1, 3)
        .reshape(width, out_lanes)
    )
    weights = [
        from_replica(w_here, rows_before, other) if rows_before or other else w_here
        for other in range(2)
        for rows_before in range(row_count)
    ]
    numbers = jnp.stack([length, row, core])
    return finish(numbers, parts, self_term, gate, embedded, weights)


def solution(mesh):
    return jax.shard_map(
        local,
        mesh=mesh,
        in_specs=(
            P(("batch", "seq"), None),
            P(("batch", "seq"), None),
            P("batch"),
            P("batch"),
            P("seq", None),
            P(None, None, "seq"),
            P(),
            P(),
            P("seq", None),
        ),
        out_specs=P(("batch", "seq"), None),
        check_vma=False,
    )
```

```python
import jax
import jax.numpy as jnp
from jax import lax
from jax.experimental import pallas as pl
from jax.experimental.pallas import tpu as pltpu
from jax.sharding import PartitionSpec as P

slot_rows = 32
near_places = 4


def groups_of(places):
    return [[2 * place + side for place in group] for side in range(2) for group in places]


def exchange(blocks, groups):
    return lax.all_to_all(
        blocks, "seq", split_axis=0, concat_axis=0, tiled=True, axis_index_groups=groups
    )


def column_groups():
    return groups_of([list(range(lax.axis_size("seq") // 2))])


def from_place(block, shift):
    count = lax.axis_size("seq")
    return lax.ppermute(block, "seq", [(i, (i + 2 * shift) % count) for i in range(count)])


def swap_pair(block):
    return lax.ppermute(block, "seq", [(i, i ^ 1) for i in range(lax.axis_size("seq"))])


def swap_core(block):
    return lax.ppermute(block, "batch", [(i, i ^ 1) for i in range(lax.axis_size("batch"))])


def from_row(block, shift):
    count = lax.axis_size("batch")
    return lax.ppermute(block, "batch", [(i, (i + 4 * shift) % count) for i in range(count)])


def gather_slots(block):
    column = lax.axis_size("seq") // 2
    far_places = column // near_places
    far = groups_of([list(range(at, column, near_places)) for at in range(near_places)])
    blocks = exchange(jnp.broadcast_to(block[None], (far_places,) + block.shape), far)
    rows = blocks.reshape(far_places * block.shape[0], block.shape[1])
    half = rows.shape[0] // 2
    return (
        rows,
        from_place(rows, 1),
        from_place(rows, -1),
        from_place(rows[:half], 2),
        from_place(rows[half:], -2),
    )


def bucket_bias(rab_table, distance):
    bucket_count = rab_table.shape[1]
    powers = 2 ** jnp.arange(bucket_count - 1, dtype=jnp.int32)
    bucket = jnp.sum((distance[:, None] >= powers[None, :]).astype(jnp.int32), axis=1)
    hits = (bucket[None, :] == jnp.arange(bucket_count, dtype=jnp.int32)[:, None]).astype(
        jnp.float32
    )
    return jnp.dot(
        rab_table, hits, precision=lax.Precision.HIGHEST, preferred_element_type=jnp.float32
    )


def silu(value):
    return value * (0.5 + 0.5 * jnp.tanh(0.5 * value))


def marked(condition):
    return condition.astype(jnp.float32).astype(jnp.bfloat16)


def pick_kernel(numbers, ids, table, packed, slots, pair_slots, most):
    rows, count = table.shape[0], ids.shape[1]
    index, first_rank, devices = numbers[0], numbers[1], most.shape[0]
    place, side = index // 2, lax.rem(index, 2)
    slot_count = packed.shape[0]
    shard_lanes = ids[...] // rows
    shards = lax.broadcasted_iota(jnp.int32, (most.shape[0], count), 0)
    member = shards == shard_lanes
    before = lax.broadcasted_iota(jnp.int32, (count, count), 0) < lax.broadcasted_iota(
        jnp.int32, (count, count), 1
    )
    ranks = jnp.dot(marked(member), marked(before), preferred_element_type=jnp.float32)
    rank = jnp.sum(jnp.where(member, ranks, 0.0), axis=0, keepdims=True)
    counts = jnp.sum(member.astype(jnp.float32), axis=1, keepdims=True)
    most[...] = jnp.broadcast_to(
        jnp.max(counts, axis=0, keepdims=True), most.shape
    ).astype(jnp.int32)
    slot = rank.astype(jnp.int32) - first_rank
    there = ids[...] - index * rows
    own_slot = jnp.where((there >= 0) & (there < rows), slot, -1)
    taken = own_slot == lax.broadcasted_iota(jnp.int32, (slot_count, count), 0)
    wanted = there == lax.broadcasted_iota(jnp.int32, (rows, count), 0)
    picks = lax.dot_general(
        marked(taken), marked(wanted), (((1,), (1,)), ((), ())), preferred_element_type=jnp.float32
    ).astype(jnp.bfloat16)
    packed[...] = jnp.dot(picks, table[...], preferred_element_type=jnp.float32).astype(
        jnp.bfloat16
    )
    source = shard_lanes // 2
    inside = (shard_lanes - 2 * source == side) & (slot >= 0) & (slot < slot_count)
    ahead = lax.rem(source - place + devices, near_places)
    piece = jnp.where(ahead == 0, 0, jnp.where(ahead == near_places - 1, 1, ahead + 1))
    block = piece * (devices // 2 // near_places) + source // near_places
    facts = jnp.concatenate(
        [
            jnp.broadcast_to(jnp.where(inside, fact, -1).astype(jnp.float32), (8, count))
            for fact in (block, slot)
        ],
        axis=0,
    ).astype(jnp.bfloat16)

    def spread(chosen, out):
        both = lax.dot_general(
            marked(chosen), facts, (((1,), (1,)), ((), ())), preferred_element_type=jnp.float32
        )
        block_at, slot_at = both[:, :1].astype(jnp.int32), both[:, 8:9].astype(jnp.int32)
        out[...] = jnp.where(block_at < 0, -1, block_at * slot_count + slot_at)

    own = count // devices
    at = lax.broadcasted_iota(jnp.int32, (count, count), 0)
    half = at // (count // 2)
    inner = at - half * (count // 2)
    owner_side = jnp.where(half == 0, side, 1 - side)
    original = (inner // own) * (2 * own) + owner_side * own + lax.rem(inner, own)
    spread(original == lax.broadcasted_iota(jnp.int32, (count, count), 1), slots)
    at = lax.broadcasted_iota(jnp.int32, (2 * own, count), 0)
    half = at // own
    owner_side = jnp.where(half == 0, side, 1 - side)
    original = place * (2 * own) + owner_side * own + at - half * own
    spread(original == lax.broadcasted_iota(jnp.int32, (2 * own, count), 1), pair_slots)


def pick(numbers, ids, table, devices):
    whole = pl.BlockSpec(memory_space=pltpu.VMEM)
    count = ids.shape[0]
    return pl.pallas_call(
        pick_kernel,
        in_specs=[pl.BlockSpec(memory_space=pltpu.SMEM), whole, whole],
        out_specs=[whole] * 4,
        out_shape=[
            jax.ShapeDtypeStruct((slot_rows, table.shape[1]), jnp.bfloat16),
            jax.ShapeDtypeStruct((count, 1), jnp.int32),
            jax.ShapeDtypeStruct((2 * count // devices, 1), jnp.int32),
            jax.ShapeDtypeStruct((devices, 128), jnp.int32),
        ],
        compiler_params=pltpu.CompilerParams(vmem_limit_bytes=32 * 1024 * 1024),
        cost_estimate=pl.CostEstimate(
            flops=2 * slot_rows * table.shape[0] * table.shape[1],
            bytes_accessed=2 * table.shape[0] * table.shape[1],
            transcendentals=0,
        ),
    )(numbers, ids.reshape(1, -1), table)


def project_kernel(at, at_pair, rows_0, rows_1, rows_2, rows_3, rows_4, weights, *rest):
    proj_mine, proj_other, own_rows, slots = rest
    cand_side, columns = proj_mine.shape
    own, width = own_rows.shape
    first = 0
    for rows in (rows_0, rows_1, rows_2, rows_3, rows_4):
        count = rows.shape[0]
        slots[first : first + count, :] = silu(
            lax.dot_general(
                rows[...],
                weights[...],
                (((1,), (1,)), ((), ())),
                preferred_element_type=jnp.float32,
            )
        ).astype(jnp.bfloat16)
        first += count
    place = lax.broadcasted_iota(jnp.int32, (cand_side, first), 1)
    for side, proj in ((0, proj_mine), (1, proj_other)):
        chosen = (at[side * cand_side : (side + 1) * cand_side, :] == place).astype(jnp.float32)
        proj[:cand_side, :] = jnp.dot(
            chosen.astype(jnp.bfloat16), slots[...], preferred_element_type=jnp.float32
        ).astype(jnp.bfloat16)
    place = lax.broadcasted_iota(jnp.int32, (2 * own, first), 1)
    chosen = (at_pair[...] == place).astype(jnp.float32).astype(jnp.bfloat16)
    total = None
    first = 0
    for rows in (rows_0, rows_1, rows_2, rows_3, rows_4):
        count = rows.shape[0]
        part = jnp.dot(
            chosen[:, first : first + count], rows[...], preferred_element_type=jnp.float32
        )
        total = part if total is None else total + part
        first += count
    own_rows[...] = total[:own].astype(jnp.bfloat16)
    for part in range(width // columns):
        proj_other[cand_side + part * own : cand_side + (part + 1) * own, :] = total[
            own:, part * columns : (part + 1) * columns
        ].astype(jnp.bfloat16)


def project(at, at_pair, rows, weights):
    columns, width = weights.shape
    cand_side = at.shape[0] // 2
    own = at_pair.shape[0] // 2
    slot_count = sum(piece.shape[0] for piece in rows)
    return pl.pallas_call(
        project_kernel,
        out_shape=[
            jax.ShapeDtypeStruct((cand_side, columns), jnp.bfloat16),
            jax.ShapeDtypeStruct((cand_side + own * width // columns, columns), jnp.bfloat16),
            jax.ShapeDtypeStruct((own, width), jnp.bfloat16),
        ],
        scratch_shapes=[pltpu.VMEM((slot_count, columns), jnp.bfloat16)],
        compiler_params=pltpu.CompilerParams(vmem_limit_bytes=32 * 1024 * 1024),
        cost_estimate=pl.CostEstimate(
            flops=2 * slot_count * columns * (width + 2 * cand_side),
            bytes_accessed=2 * (slot_count + columns) * width,
            transcendentals=slot_count * columns,
        ),
    )(at, at_pair, *rows, weights)


def pack_kernel(feature_here, mine, arrived, own_rows, w_slice, *rest):
    queries, packed, embedded = rest[-3:]
    cand_side, columns = mine.shape
    own = own_rows.shape[0]
    proj = mine[...].astype(jnp.float32) + arrived[:cand_side, :].astype(jnp.float32)
    for part in range(own_rows.shape[1] // columns):
        lanes = slice(part * columns, (part + 1) * columns)
        other = arrived[cand_side + part * own : cand_side + (part + 1) * own, :]
        embedded[:, lanes] = (
            own_rows[:, lanes].astype(jnp.float32) + other.astype(jnp.float32)
        ).astype(jnp.bfloat16)
    block = 4 * feature_here
    query = jnp.concatenate(
        [proj[:, side * block + 2 * feature_here : side * block + 3 * feature_here] for side in (0, 1)],
        axis=1,
    )
    queries[...] = query.T.astype(jnp.bfloat16)
    column, own, _ = packed.shape
    columns = 2 * block
    packed[:, :, :columns] = proj.astype(jnp.bfloat16).reshape(column, own, columns)
    lanes = w_slice.shape[1]
    for part in range(w_slice.shape[0] // own):
        packed[:, :, columns + part * lanes : columns + (part + 1) * lanes] = jnp.broadcast_to(
            w_slice[part * own : (part + 1) * own, :][None], (column, own, lanes)
        )


def pack(mine, arrived, own_rows, w_slice, ready, feature_here):
    cand_side, columns = mine.shape
    own = own_rows.shape[0]
    column = cand_side // own
    packed_width = columns + w_slice.shape[0] * w_slice.shape[1] // own
    whole = pl.BlockSpec(memory_space=pltpu.VMEM)
    return pl.pallas_call(
        lambda *refs: pack_kernel(feature_here, *refs),
        in_specs=[whole] * 4 + [pl.BlockSpec(memory_space=pl.ANY)] * len(ready),
        out_specs=[whole] * 3,
        out_shape=[
            jax.ShapeDtypeStruct((2 * feature_here, cand_side), jnp.bfloat16),
            jax.ShapeDtypeStruct((column, own, packed_width), jnp.bfloat16),
            jax.ShapeDtypeStruct(own_rows.shape, jnp.bfloat16),
        ],
        compiler_params=pltpu.CompilerParams(vmem_limit_bytes=32 * 1024 * 1024),
        cost_estimate=pl.CostEstimate(
            flops=cand_side * columns, bytes_accessed=8 * cand_side * columns, transcendentals=0
        ),
    )(mine, arrived, own_rows, w_slice, *ready)


def attend_kernel(scale, *refs):
    queries, keys_a, keys_b, values_a, values_b, bias_a, bias_b, live_a, live_b = refs[:9]
    summed = refs[-2]
    head = pl.program_id(0)
    head_queries = queries[...].T
    total = None
    for keys, values, bias, live in (
        (keys_a, values_a, bias_a, live_a),
        (keys_b, values_b, bias_b, live_b),
    ):
        scores = lax.dot_general(
            head_queries, keys[...], (((1,), (1,)), ((), ())), preferred_element_type=jnp.float32
        )
        weights = silu(scores * scale + bias[pl.ds(head, 1), :])
        weights = jnp.where(live[...] > 0.0, weights, 0.0).astype(jnp.bfloat16)
        part = jnp.dot(weights, values[...], preferred_element_type=jnp.float32)
        total = part if total is None else total + part
    summed[...] = total.astype(summed.dtype)


def attend(queries, keys, values, bias, live, head_count, through):
    width, cand = queries.shape
    events = keys[0].shape[0]
    head_size = width // head_count
    event_spec = pl.BlockSpec((events, head_size), lambda h: (0, h))
    bias_spec = pl.BlockSpec((head_count, events), lambda h: (0, 0))
    live_spec = pl.BlockSpec((1, events), lambda h: (0, 0))
    held = pl.BlockSpec(memory_space=pl.ANY)
    return pl.pallas_call(
        lambda *refs: attend_kernel(head_size ** (-0.5), *refs),
        grid=(head_count,),
        in_specs=[pl.BlockSpec((head_size, cand), lambda h: (h, 0))]
        + [event_spec] * 4
        + [bias_spec] * 2
        + [live_spec] * 2
        + [held],
        out_specs=[pl.BlockSpec((cand, head_size), lambda h: (0, h)), held],
        out_shape=[
            jax.ShapeDtypeStruct((cand, width), jnp.bfloat16),
            jax.ShapeDtypeStruct(through.shape, through.dtype),
        ],
        input_output_aliases={9: 1},
        compiler_params=pltpu.CompilerParams(vmem_limit_bytes=32 * 1024 * 1024),
        cost_estimate=pl.CostEstimate(
            flops=8 * cand * events * width,
            bytes_accessed=8 * events * width + 4 * cand * width,
            transcendentals=2 * cand * events * head_count,
        ),
    )(queries, *keys, *values, *bias, *live, through)


def finish_kernel(numbers, parts, self_term, gate, embedded, *rest):
    weights, scored = rest[:-1], rest[-1]
    history_sum = parts[0].astype(jnp.float32)
    for part in range(1, parts.shape[0]):
        history_sum = history_sum + parts[part].astype(jnp.float32)
    length = jnp.full((1, 1), numbers[0], jnp.int32).astype(jnp.float32)
    attended = history_sum * lax.rsqrt(length) + self_term[...]
    centre = jnp.mean(attended, axis=1, keepdims=True)
    spread = jnp.mean((attended - centre) ** 2, axis=1, keepdims=True)
    normed = (attended - centre) * lax.rsqrt(spread + 1e-05) * gate[...]
    normed = normed.astype(jnp.bfloat16)
    lanes = weights[0].shape[1]
    row_count = len(weights) // 2
    row, core = numbers[1], numbers[2]
    for index, columns_of in enumerate(weights):
        owner = core if index < row_count else 1 - core
        block = owner * row_count + lax.rem(row + row_count - index % row_count, row_count)
        columns = pl.ds(pl.multiple_of(block * lanes, lanes), lanes)
        projected = jnp.dot(normed, columns_of[...], preferred_element_type=jnp.float32)
        scored[:, columns] = (projected + embedded[:, columns].astype(jnp.float32)).astype(
            scored.dtype
        )


def finish(numbers, parts, self_term, gate, embedded, weights):
    whole = pl.BlockSpec(memory_space=pltpu.VMEM)
    rows, width = embedded.shape
    return pl.pallas_call(
        finish_kernel,
        in_specs=[pl.BlockSpec(memory_space=pltpu.SMEM)] + [whole] * (4 + len(weights)),
        out_specs=whole,
        out_shape=jax.ShapeDtypeStruct((rows, width), jnp.bfloat16),
        compiler_params=pltpu.CompilerParams(vmem_limit_bytes=32 * 1024 * 1024),
        cost_estimate=pl.CostEstimate(
            flops=2 * rows * width * width, bytes_accessed=4 * width * width, transcendentals=0
        ),
    )(numbers, parts, self_term, gate, embedded, *weights)


def local(
    history_keys, history_values, lengths, item_ids, item_table, w_proj, rab, norm_gain, w_out
):
    device_count = lax.axis_size("seq")
    column = device_count // 2
    index_here = lax.axis_index("seq")
    place, side = index_here // 2, index_here % 2
    batch_here = lax.axis_index("batch")
    row, core = batch_here // 4, batch_here % 2
    row_count = lax.axis_size("batch") // 4
    events_here, width = history_keys.shape
    head_count = rab.shape[0]
    head_size = width // head_count
    scale = head_size ** (-0.5)
    table_rows = item_table.shape[0]
    cand_total = item_ids.shape[0]
    cand_here = cand_total // device_count
    cand_side = cand_total // 2
    feature_here = w_proj.shape[2]
    out_lanes = width // (2 * row_count)
    length = lengths[0]

    w_slice = lax.dynamic_slice_in_dim(w_out, (core * row_count + row) * out_lanes, out_lanes, 1)
    slice_rows = w_slice.shape[0]

    def lookup(first_rank, send):
        numbers = jnp.stack([index_here, first_rank])
        packed, slots, pair_slots, most = pick(numbers, item_ids, item_table, device_count)
        packed, send = lax.optimization_barrier((packed, send))
        rows = gather_slots(packed)
        return rows, slots, pair_slots, most[0, 0], [swap_pair(block) for block in send]

    w_mine = w_proj.transpose(1, 2, 0).reshape(4 * feature_here, width)
    w_send = jnp.concatenate([w_mine, w_slice.reshape(-1, width)])
    rows, slots, pair_slots, most, (w_other, keys_other, values_other) = lookup(
        jnp.int32(0), (w_send, history_keys, history_values)
    )
    slice_other = w_other[4 * feature_here :].reshape(w_slice.shape)
    w_other = w_other[: 4 * feature_here]
    keys, values = (history_keys, keys_other), (history_values, values_other)
    w_pair = jnp.concatenate(
        [jnp.where(side == 0, w_mine, w_other), jnp.where(side == 0, w_other, w_mine)]
    )
    slices = jnp.concatenate(
        [jnp.where(side == 0, w_slice, slice_other), jnp.where(side == 0, slice_other, w_slice)]
    )
    found = tuple(project(slots, pair_slots, rows, w_pair))

    def another(state):
        first_rank, found = state
        rows, slots, pair_slots, _, _ = lookup(first_rank, ())
        more = project(slots, pair_slots, rows, w_pair)
        return first_rank + slot_rows, tuple(a + b for a, b in zip(found, more))

    _, (proj_mine, proj_other, own_rows) = lax.while_loop(
        lambda state: state[0] < most, another, (jnp.int32(slot_rows), found)
    )
    side_queries, packed, embedded = pack(
        proj_mine, swap_pair(proj_other), own_rows, slices, (keys_other,), feature_here
    )
    received = exchange(packed, column_groups())
    all_queries = lax.all_gather(
        side_queries, "seq", axis=0, tiled=True, axis_index_groups=column_groups()
    )

    def bias_of(index):
        positions = index * events_here + jnp.arange(events_here, dtype=jnp.int32)
        return (
            bucket_bias(rab, length - positions),
            (positions < length).astype(jnp.float32)[None, :],
        )

    bias, live = zip(bias_of(index_here), bias_of(index_here + 1 - 2 * side))
    summed, received = attend(all_queries, keys, values, bias, live, head_count, received)
    parts = exchange(summed.reshape(column, cand_here, width), column_groups())

    own_proj = (
        received[:, :, : 8 * feature_here]
        .reshape(column, cand_here, 2, 4, feature_here)
        .transpose(3, 1, 0, 2, 4)
        .reshape(4, cand_here, width)
        .astype(jnp.float32)
    )
    gate_u, own_v, own_queries, own_k = own_proj[0], own_proj[1], own_proj[2], own_proj[3]
    self_scores = jnp.sum((own_queries * own_k).reshape(cand_here, head_count, head_size), axis=2)
    self_scores = self_scores * scale + rab[:, 0][None, :]
    self_term = jax.nn.silu(self_scores)[:, :, None] * own_v.reshape(
        cand_here, head_count, head_size
    )
    self_term = self_term.reshape(cand_here, width)
    gate = norm_gain[None, :] * gate_u

    w_here = (
        received[:, :, 8 * feature_here :]
        .reshape(column, cand_here, 2 * slice_rows // cand_here, out_lanes)
        .transpose(0, 2, 1, 3)
        .reshape(width, out_lanes)
    )
    weights = [w_here] + [from_row(w_here, shift) for shift in range(1, row_count)]
    weights = [*weights, *swap_core(jnp.stack(weights))]
    numbers = jnp.stack([length, row, core])
    return finish(numbers, parts, self_term, gate, embedded, weights)


def solution(mesh):
    return jax.shard_map(
        local,
        mesh=mesh,
        in_specs=(
            P(("batch", "seq"), None),
            P(("batch", "seq"), None),
            P("batch"),
            P("batch"),
            P("seq", None),
            P(None, None, "seq"),
            P(),
            P(),
            P("seq", None),
        ),
        out_specs=P(("batch", "seq"), None),
        check_vma=False,
    )
```

```python
import jax
import jax.numpy as jnp
from jax import lax
from jax.experimental import pallas as pl
from jax.experimental.pallas import tpu as pltpu
from jax.sharding import PartitionSpec as P

slot_rows = 32
near_places = 4


def groups_of(places):
    return [[2 * place + side for place in group] for side in range(2) for group in places]


def exchange(blocks, groups):
    return lax.all_to_all(
        blocks, "seq", split_axis=0, concat_axis=0, tiled=True, axis_index_groups=groups
    )


def column_groups():
    return groups_of([list(range(lax.axis_size("seq") // 2))])


def from_place(block, shift):
    count = lax.axis_size("seq")
    return lax.ppermute(block, "seq", [(i, (i + 2 * shift) % count) for i in range(count)])


def swap_pair(block):
    return lax.ppermute(block, "seq", [(i, i ^ 1) for i in range(lax.axis_size("seq"))])


def swap_core(block):
    return lax.ppermute(block, "batch", [(i, i ^ 1) for i in range(lax.axis_size("batch"))])


def from_row(block, shift):
    count = lax.axis_size("batch")
    return lax.ppermute(block, "batch", [(i, (i + 4 * shift) % count) for i in range(count)])


def gather_slots(blocks):
    column = lax.axis_size("seq") // 2
    far = groups_of([list(range(at, column, near_places)) for at in range(near_places)])
    blocks = exchange(blocks, far)
    rows = blocks.reshape(blocks.shape[0] * blocks.shape[1], blocks.shape[2])
    half = rows.shape[0] // 2
    return (
        rows,
        from_place(rows, 1),
        from_place(rows, -1),
        from_place(rows[:half], 2),
        from_place(rows[half:], -2),
    )


def bucket_bias(rab_table, distance):
    bucket_count = rab_table.shape[1]
    powers = 2 ** jnp.arange(bucket_count - 1, dtype=jnp.int32)
    bucket = jnp.sum((distance[:, None] >= powers[None, :]).astype(jnp.int32), axis=1)
    hits = (bucket[None, :] == jnp.arange(bucket_count, dtype=jnp.int32)[:, None]).astype(
        jnp.float32
    )
    return jnp.dot(
        rab_table, hits, precision=lax.Precision.HIGHEST, preferred_element_type=jnp.float32
    )


def silu(value):
    return half_silu(0.5 * value)


def half_silu(half):
    return half + half * jnp.tanh(half)


def marked(condition):
    return condition.astype(jnp.float32).astype(jnp.bfloat16)


def earlier(count):
    return lax.broadcasted_iota(jnp.int32, (count, count), 0) < lax.broadcasted_iota(
        jnp.int32, (count, count), 1
    )


def pick_kernel(numbers, ids, table, packed):
    rows, count = table.shape[0], ids.shape[1]
    copies, slot_count, _ = packed.shape
    there = ids[...] - numbers[0] * rows
    here = (there >= 0) & (there < rows)
    marks = jnp.broadcast_to(here.astype(jnp.float32), (8, count)).astype(jnp.bfloat16)
    rank = jnp.dot(marks, marked(earlier(count)), preferred_element_type=jnp.float32)[:1]
    slot = jnp.where(here, rank.astype(jnp.int32) - numbers[1], -1)
    taken = slot == lax.broadcasted_iota(jnp.int32, (slot_count, count), 0)
    wanted = there == lax.broadcasted_iota(jnp.int32, (rows, count), 0)
    picks = lax.dot_general(
        marked(taken), marked(wanted), (((1,), (1,)), ((), ())), preferred_element_type=jnp.float32
    ).astype(jnp.bfloat16)
    found = jnp.dot(picks, table[...], preferred_element_type=jnp.float32).astype(jnp.bfloat16)
    for copy in range(copies):
        packed[copy] = found


def pick(numbers, ids, table, copies):
    whole = pl.BlockSpec(memory_space=pltpu.VMEM)
    return pl.pallas_call(
        pick_kernel,
        in_specs=[pl.BlockSpec(memory_space=pltpu.SMEM), whole, whole],
        out_specs=whole,
        out_shape=jax.ShapeDtypeStruct((copies, slot_rows, table.shape[1]), jnp.bfloat16),
        compiler_params=pltpu.CompilerParams(vmem_limit_bytes=32 * 1024 * 1024),
        cost_estimate=pl.CostEstimate(
            flops=2 * slot_rows * table.shape[0] * table.shape[1],
            bytes_accessed=2 * table.shape[0] * table.shape[1],
            transcendentals=0,
        ),
    )(numbers, ids.reshape(1, -1), table)


def locate_kernel(table_rows, numbers, ids, slots, pair_slots, most):
    count, devices = ids.shape[1], most.shape[0]
    index = numbers[0]
    place, side = index // 2, lax.rem(index, 2)
    shard = ids[...] // table_rows
    member = lax.broadcasted_iota(jnp.int32, (devices, count), 0) == shard
    ranks = jnp.dot(marked(member), marked(earlier(count)), preferred_element_type=jnp.float32)
    rank = jnp.sum(jnp.where(member, ranks, 0.0), axis=0, keepdims=True)
    counts = jnp.sum(member.astype(jnp.float32), axis=1, keepdims=True)
    most[...] = jnp.broadcast_to(jnp.max(counts, axis=0, keepdims=True), most.shape).astype(
        jnp.int32
    )
    slot = rank.astype(jnp.int32) - numbers[1]
    source = shard // 2
    inside = (shard - 2 * source == side) & (slot >= 0) & (slot < slot_rows)
    ahead = lax.rem(source - place + devices, near_places)
    piece = jnp.where(ahead == 0, 0, jnp.where(ahead == near_places - 1, 1, ahead + 1))
    block = piece * (devices // 2 // near_places) + source // near_places
    facts = jnp.concatenate(
        [
            jnp.broadcast_to(jnp.where(inside, fact, -1).astype(jnp.float32), (8, count))
            for fact in (block, slot)
        ],
        axis=0,
    ).astype(jnp.bfloat16)

    def spread(chosen, out):
        both = lax.dot_general(
            marked(chosen), facts, (((1,), (1,)), ((), ())), preferred_element_type=jnp.float32
        )
        block_at, slot_at = both[:, :1].astype(jnp.int32), both[:, 8:9].astype(jnp.int32)
        out[...] = jnp.where(block_at < 0, -1, block_at * slot_rows + slot_at)

    own = count // devices
    at = lax.broadcasted_iota(jnp.int32, (count, count), 0)
    half = at // (count // 2)
    inner = at - half * (count // 2)
    owner_side = jnp.where(half == 0, side, 1 - side)
    original = (inner // own) * (2 * own) + owner_side * own + lax.rem(inner, own)
    spread(original == lax.broadcasted_iota(jnp.int32, (count, count), 1), slots)
    at = lax.broadcasted_iota(jnp.int32, (2 * own, count), 0)
    half = at // own
    owner_side = jnp.where(half == 0, side, 1 - side)
    original = place * (2 * own) + owner_side * own + at - half * own
    spread(original == lax.broadcasted_iota(jnp.int32, (2 * own, count), 1), pair_slots)


def locate(numbers, ids, table_rows, devices):
    whole = pl.BlockSpec(memory_space=pltpu.VMEM)
    count = ids.shape[0]
    return pl.pallas_call(
        lambda *refs: locate_kernel(table_rows, *refs),
        in_specs=[pl.BlockSpec(memory_space=pltpu.SMEM), whole],
        out_specs=[whole] * 3,
        out_shape=[
            jax.ShapeDtypeStruct((count, 1), jnp.int32),
            jax.ShapeDtypeStruct((2 * count // devices, 1), jnp.int32),
            jax.ShapeDtypeStruct((devices, 128), jnp.int32),
        ],
        compiler_params=pltpu.CompilerParams(vmem_limit_bytes=32 * 1024 * 1024),
        cost_estimate=pl.CostEstimate(
            flops=2 * count * count * devices, bytes_accessed=8 * count, transcendentals=0
        ),
    )(numbers, ids.reshape(1, -1))


def project_kernel(at, at_pair, rows_0, rows_1, rows_2, rows_3, rows_4, weights, *rest):
    proj_mine, proj_other, own_rows, slots = rest[-4:]
    cand_side, columns = proj_mine.shape
    own, width = own_rows.shape
    first = 0
    for rows in (rows_0, rows_1, rows_2, rows_3, rows_4):
        count = rows.shape[0]
        slots[first : first + count, :] = silu(
            lax.dot_general(
                rows[...],
                weights[...],
                (((1,), (1,)), ((), ())),
                preferred_element_type=jnp.float32,
            )
        ).astype(jnp.bfloat16)
        first += count
    place = lax.broadcasted_iota(jnp.int32, (cand_side, first), 1)
    for side, proj in ((0, proj_mine), (1, proj_other)):
        chosen = (at[side * cand_side : (side + 1) * cand_side, :] == place).astype(jnp.float32)
        proj[:cand_side, :] = jnp.dot(
            chosen.astype(jnp.bfloat16), slots[...], preferred_element_type=jnp.float32
        ).astype(jnp.bfloat16)
    place = lax.broadcasted_iota(jnp.int32, (2 * own, first), 1)
    chosen = (at_pair[...] == place).astype(jnp.float32).astype(jnp.bfloat16)
    total = None
    first = 0
    for rows in (rows_0, rows_1, rows_2, rows_3, rows_4):
        count = rows.shape[0]
        part = jnp.dot(
            chosen[:, first : first + count], rows[...], preferred_element_type=jnp.float32
        )
        total = part if total is None else total + part
        first += count
    own_rows[...] = total[:own].astype(jnp.bfloat16)
    for part in range(width // columns):
        proj_other[cand_side + part * own : cand_side + (part + 1) * own, :] = total[
            own:, part * columns : (part + 1) * columns
        ].astype(jnp.bfloat16)


def project(at, at_pair, rows, weights, ready):
    columns, width = weights.shape
    cand_side = at.shape[0] // 2
    own = at_pair.shape[0] // 2
    slot_count = sum(piece.shape[0] for piece in rows)
    whole = pl.BlockSpec(memory_space=pltpu.VMEM)
    return pl.pallas_call(
        project_kernel,
        in_specs=[whole] * (3 + len(rows)) + [pl.BlockSpec(memory_space=pl.ANY)] * len(ready),
        out_specs=[whole] * 3,
        out_shape=[
            jax.ShapeDtypeStruct((cand_side, columns), jnp.bfloat16),
            jax.ShapeDtypeStruct((cand_side + own * width // columns, columns), jnp.bfloat16),
            jax.ShapeDtypeStruct((own, width), jnp.bfloat16),
        ],
        scratch_shapes=[pltpu.VMEM((slot_count, columns), jnp.bfloat16)],
        compiler_params=pltpu.CompilerParams(vmem_limit_bytes=32 * 1024 * 1024),
        cost_estimate=pl.CostEstimate(
            flops=2 * slot_count * columns * (width + 2 * cand_side),
            bytes_accessed=2 * (slot_count + columns) * width,
            transcendentals=slot_count * columns,
        ),
    )(at, at_pair, *rows, weights, *ready)


def pack_kernel(feature_here, mine, arrived, own_rows, w_slice, *rest):
    queries, packed, embedded = rest[-3:]
    cand_side, columns = mine.shape
    own = own_rows.shape[0]
    proj = mine[...].astype(jnp.float32) + arrived[:cand_side, :].astype(jnp.float32)
    for part in range(own_rows.shape[1] // columns):
        lanes = slice(part * columns, (part + 1) * columns)
        other = arrived[cand_side + part * own : cand_side + (part + 1) * own, :]
        embedded[:, lanes] = (
            own_rows[:, lanes].astype(jnp.float32) + other.astype(jnp.float32)
        ).astype(jnp.bfloat16)
    block = 4 * feature_here
    queries[...] = proj[:, block : block + 2 * feature_here].T.astype(jnp.bfloat16)
    column, own, _ = packed.shape
    columns = 2 * block
    packed[:, :, :columns] = proj.astype(jnp.bfloat16).reshape(column, own, columns)
    lanes = w_slice.shape[1]
    for part in range(w_slice.shape[0] // own):
        packed[:, :, columns + part * lanes : columns + (part + 1) * lanes] = jnp.broadcast_to(
            w_slice[part * own : (part + 1) * own, :][None], (column, own, lanes)
        )


def pack(mine, arrived, own_rows, w_slice, feature_here):
    cand_side, columns = mine.shape
    own = own_rows.shape[0]
    column = cand_side // own
    packed_width = columns + w_slice.shape[0] * w_slice.shape[1] // own
    whole = pl.BlockSpec(memory_space=pltpu.VMEM)
    return pl.pallas_call(
        lambda *refs: pack_kernel(feature_here, *refs),
        in_specs=[whole] * 4,
        out_specs=[whole] * 3,
        out_shape=[
            jax.ShapeDtypeStruct((2 * feature_here, cand_side), jnp.bfloat16),
            jax.ShapeDtypeStruct((column, own, packed_width), jnp.bfloat16),
            jax.ShapeDtypeStruct(own_rows.shape, jnp.bfloat16),
        ],
        compiler_params=pltpu.CompilerParams(vmem_limit_bytes=32 * 1024 * 1024),
        cost_estimate=pl.CostEstimate(
            flops=cand_side * columns, bytes_accessed=8 * cand_side * columns, transcendentals=0
        ),
    )(mine, arrived, own_rows, w_slice)


def attend_kernel(scale, heads, *refs):
    queries, keys_a, keys_b, values_a, values_b, bias_a, bias_b, live_a, live_b = refs[:9]
    summed = refs[-2]
    first_head = pl.program_id(0) * heads
    head_size = keys_a.shape[1] // heads
    for head in range(heads):
        lanes = slice(head * head_size, (head + 1) * head_size)
        head_queries = queries[lanes, :].T
        total = None
        for keys, values, bias, live in (
            (keys_a, values_a, bias_a, live_a),
            (keys_b, values_b, bias_b, live_b),
        ):
            scores = lax.dot_general(
                head_queries,
                keys[:, lanes],
                (((1,), (1,)), ((), ())),
                preferred_element_type=jnp.float32,
            )
            half_bias = 0.5 * bias[pl.ds(first_head + head, 1), :]
            weights = half_silu(scores * (0.5 * scale) + half_bias)
            weights = jnp.where(live[...] > 0.0, weights, 0.0).astype(jnp.bfloat16)
            part = jnp.dot(weights, values[:, lanes], preferred_element_type=jnp.float32)
            total = part if total is None else total + part
        summed[:, lanes] = total.astype(summed.dtype)


def attend(queries, keys, values, keys_other, values_other, bias, live, head_count, through):
    width, cand = queries.shape
    events = keys.shape[0]
    head_size = width // head_count
    heads = 4
    lanes = heads * head_size
    bias_spec = pl.BlockSpec((head_count, events), lambda h: (0, 0))
    live_spec = pl.BlockSpec((1, events), lambda h: (0, 0))
    held = pl.BlockSpec(memory_space=pl.ANY)
    return pl.pallas_call(
        lambda *refs: attend_kernel(head_size ** (-0.5), heads, *refs),
        grid=(head_count // heads,),
        in_specs=[
            pl.BlockSpec((lanes, cand), lambda h: (h, 0)),
            pl.BlockSpec((events, lanes), lambda h: (0, h)),
            pl.BlockSpec((events, lanes), lambda h: (0, h)),
            pl.BlockSpec((events, lanes), lambda h: (0, h)),
            pl.BlockSpec((events, lanes), lambda h: (0, h)),
        ]
        + [bias_spec] * 2
        + [live_spec] * 2
        + [held],
        out_specs=[pl.BlockSpec((cand, lanes), lambda h: (0, h)), held],
        out_shape=[
            jax.ShapeDtypeStruct((cand, width), jnp.bfloat16),
            jax.ShapeDtypeStruct(through.shape, through.dtype),
        ],
        input_output_aliases={9: 1},
        compiler_params=pltpu.CompilerParams(vmem_limit_bytes=32 * 1024 * 1024),
        cost_estimate=pl.CostEstimate(
            flops=8 * cand * events * width,
            bytes_accessed=8 * events * width + 4 * cand * width,
            transcendentals=2 * cand * events * head_count,
        ),
    )(queries, keys, keys_other, values, values_other, *bias, *live, through)


def own_kernel(scale, rab, received, gain, self_term, gate):
    own, width = self_term.shape
    column = received.shape[0]
    lanes = width // column
    gate_u, own_v, own_queries, own_k = (
        jnp.concatenate(
            [
                received[place, :, part * lanes : (part + 1) * lanes].astype(jnp.float32)
                for place in range(column)
            ],
            axis=1,
        )
        for part in range(4)
    )
    gate[...] = gate_u * gain[...]
    products = own_queries * own_k
    head_count = rab.shape[0]
    head_size = width // head_count
    for head in range(head_count):
        head_lanes = slice(head * head_size, (head + 1) * head_size)
        score = jnp.sum(products[:, head_lanes], axis=1, keepdims=True) * scale + rab[head, 0]
        self_term[:, head_lanes] = silu(score) * own_v[:, head_lanes]


def own_parts(received, rab, gain, own):
    width = gain.shape[0]
    whole = pl.BlockSpec(memory_space=pltpu.VMEM)
    scale = (width // rab.shape[0]) ** (-0.5)
    return pl.pallas_call(
        lambda *refs: own_kernel(scale, *refs),
        in_specs=[pl.BlockSpec(memory_space=pltpu.SMEM), whole, whole],
        out_specs=[whole] * 2,
        out_shape=[jax.ShapeDtypeStruct((own, width), jnp.float32)] * 2,
        compiler_params=pltpu.CompilerParams(vmem_limit_bytes=32 * 1024 * 1024),
        cost_estimate=pl.CostEstimate(
            flops=8 * own * width, bytes_accessed=32 * own * width, transcendentals=own
        ),
    )(rab, received, gain.reshape(1, -1))


def finish_kernel(numbers, parts, self_term, gate, embedded, *rest):
    weights, scored = rest[:-1], rest[-1]
    history_sum = parts[0].astype(jnp.float32)
    for part in range(1, parts.shape[0]):
        history_sum = history_sum + parts[part].astype(jnp.float32)
    length = jnp.full((1, 1), numbers[0], jnp.int32).astype(jnp.float32)
    attended = history_sum * lax.rsqrt(length) + self_term[...]
    centre = jnp.mean(attended, axis=1, keepdims=True)
    spread = jnp.mean((attended - centre) ** 2, axis=1, keepdims=True)
    normed = (attended - centre) * lax.rsqrt(spread + 1e-05) * gate[...]
    normed = normed.astype(jnp.bfloat16)
    lanes = weights[0].shape[1]
    row_count = len(weights) // 2
    row, core = numbers[1], numbers[2]
    for index, columns_of in enumerate(weights):
        owner = core if index < row_count else 1 - core
        block = owner * row_count + lax.rem(row + row_count - index % row_count, row_count)
        columns = pl.ds(pl.multiple_of(block * lanes, lanes), lanes)
        projected = jnp.dot(normed, columns_of[...], preferred_element_type=jnp.float32)
        scored[:, columns] = (projected + embedded[:, columns].astype(jnp.float32)).astype(
            scored.dtype
        )


def finish(numbers, parts, self_term, gate, embedded, weights):
    whole = pl.BlockSpec(memory_space=pltpu.VMEM)
    rows, width = embedded.shape
    return pl.pallas_call(
        finish_kernel,
        in_specs=[pl.BlockSpec(memory_space=pltpu.SMEM)] + [whole] * (4 + len(weights)),
        out_specs=whole,
        out_shape=jax.ShapeDtypeStruct((rows, width), jnp.bfloat16),
        compiler_params=pltpu.CompilerParams(vmem_limit_bytes=32 * 1024 * 1024),
        cost_estimate=pl.CostEstimate(
            flops=2 * rows * width * width, bytes_accessed=4 * width * width, transcendentals=0
        ),
    )(numbers, parts, self_term, gate, embedded, *weights)


def local(
    history_keys, history_values, lengths, item_ids, item_table, w_proj, rab, norm_gain, w_out
):
    device_count = lax.axis_size("seq")
    column = device_count // 2
    index_here = lax.axis_index("seq")
    place, side = index_here // 2, index_here % 2
    batch_here = lax.axis_index("batch")
    row, core = batch_here // 4, batch_here % 2
    row_count = lax.axis_size("batch") // 4
    events_here, width = history_keys.shape
    head_count = rab.shape[0]
    table_rows = item_table.shape[0]
    cand_total = item_ids.shape[0]
    cand_here = cand_total // device_count
    cand_side = cand_total // 2
    feature_here = w_proj.shape[2]
    out_lanes = width // (2 * row_count)
    length = lengths[0]

    w_slice = lax.dynamic_slice_in_dim(w_out, (core * row_count + row) * out_lanes, out_lanes, 1)
    slice_rows = w_slice.shape[0]

    far_places = column // near_places
    w_mine = w_proj.transpose(1, 2, 0).reshape(4 * feature_here, width)

    def numbers_at(first_rank):
        return jnp.stack([index_here, first_rank])

    picked = pick(numbers_at(jnp.int32(0)), item_ids, item_table, far_places)
    picked, w_sent, *sent = lax.optimization_barrier(
        (picked, w_mine, history_values, history_keys, w_slice)
    )
    values_sent, keys_sent, slice_sent = sent
    rows = gather_slots(picked)
    w_other = swap_pair(jnp.concatenate([w_sent, slice_sent.reshape(-1, width)]))
    slice_other = w_other[4 * feature_here :].reshape(w_slice.shape)
    w_other = w_other[: 4 * feature_here]
    keys_other, values_other = swap_pair(keys_sent), swap_pair(values_sent)
    w_pair = jnp.stack(
        [
            jnp.where(side == 0, w_mine, w_other).reshape(4, feature_here, width),
            jnp.where(side == 0, w_other, w_mine).reshape(4, feature_here, width),
        ],
        axis=1,
    ).reshape(8 * feature_here, width)
    slices = jnp.concatenate(
        [jnp.where(side == 0, w_slice, slice_other), jnp.where(side == 0, slice_other, w_slice)]
    )
    slots, pair_slots, most = locate(
        numbers_at(jnp.int32(0)), item_ids, table_rows, device_count
    )
    found = tuple(project(slots, pair_slots, rows, w_pair, (keys_other, values_other)))

    def another(state):
        first_rank, found = state
        numbers = numbers_at(first_rank)
        rows = gather_slots(pick(numbers, item_ids, item_table, far_places))
        slots, pair_slots, _ = locate(numbers, item_ids, table_rows, device_count)
        more = project(slots, pair_slots, rows, w_pair, ())
        return first_rank + slot_rows, tuple(a + b for a, b in zip(found, more))

    _, (proj_mine, proj_other, own_rows) = lax.while_loop(
        lambda state: state[0] < most[0, 0], another, (jnp.int32(slot_rows), found)
    )
    side_queries, packed, embedded = pack(
        proj_mine, swap_pair(proj_other), own_rows, slices, feature_here
    )
    received = exchange(packed, column_groups())
    all_queries = lax.all_gather(
        side_queries, "seq", axis=0, tiled=True, axis_index_groups=column_groups()
    )

    def bias_of(index):
        positions = index * events_here + jnp.arange(events_here, dtype=jnp.int32)
        return (
            bucket_bias(rab, length - positions),
            (positions < length).astype(jnp.float32)[None, :],
        )

    bias, live = zip(bias_of(index_here), bias_of(index_here + 1 - 2 * side))
    summed, received = attend(
        all_queries,
        history_keys,
        history_values,
        keys_other,
        values_other,
        bias,
        live,
        head_count,
        received,
    )
    parts = exchange(summed.reshape(column, cand_here, width), column_groups())

    self_term, gate = own_parts(received, rab, norm_gain, cand_here)

    w_here = (
        received[:, :, 8 * feature_here :]
        .reshape(column, cand_here, 2 * slice_rows // cand_here, out_lanes)
        .transpose(0, 2, 1, 3)
        .reshape(width, out_lanes)
    )
    weights = [w_here] + [from_row(w_here, shift) for shift in range(1, row_count)]
    weights = [*weights, *swap_core(jnp.stack(weights))]
    numbers = jnp.stack([length, row, core])
    return finish(numbers, parts, self_term, gate, embedded, weights)


def solution(mesh):
    return jax.shard_map(
        local,
        mesh=mesh,
        in_specs=(
            P(("batch", "seq"), None),
            P(("batch", "seq"), None),
            P("batch"),
            P("batch"),
            P("seq", None),
            P(None, None, "seq"),
            P(),
            P(),
            P("seq", None),
        ),
        out_specs=P(("batch", "seq"), None),
        check_vma=False,
    )
```

```python
import jax
import jax.numpy as jnp
from jax import lax
from jax.experimental import pallas as pl
from jax.experimental.pallas import tpu as pltpu
from jax.sharding import PartitionSpec as P

slot_rows = 32
near_places = 4


def groups_of(places):
    return [[2 * place + side for place in group] for side in range(2) for group in places]


def exchange(blocks, groups):
    return lax.all_to_all(
        blocks, "seq", split_axis=0, concat_axis=0, tiled=True, axis_index_groups=groups
    )


def column_groups():
    return groups_of([list(range(lax.axis_size("seq") // 2))])


def class_groups():
    column = lax.axis_size("seq") // 2
    return groups_of([list(range(at, column, 2)) for at in range(2)])


def from_place(block, shift):
    count = lax.axis_size("seq")
    return lax.ppermute(block, "seq", [(i, (i + 2 * shift) % count) for i in range(count)])


def swap_pair(block):
    return lax.ppermute(block, "seq", [(i, i ^ 1) for i in range(lax.axis_size("seq"))])


def swap_place(block):
    return lax.ppermute(block, "seq", [(i, i ^ 2) for i in range(lax.axis_size("seq"))])


def swap_core(block):
    return lax.ppermute(block, "batch", [(i, i ^ 1) for i in range(lax.axis_size("batch"))])


def from_row(block, shift):
    count = lax.axis_size("batch")
    return lax.ppermute(block, "batch", [(i, (i + 4 * shift) % count) for i in range(count)])


def gather_slots(blocks):
    column = lax.axis_size("seq") // 2
    far = groups_of([list(range(at, column, near_places)) for at in range(near_places)])
    blocks = exchange(blocks, far)
    rows = blocks.reshape(blocks.shape[0] * blocks.shape[1], blocks.shape[2])
    half = rows.shape[0] // 2
    return (
        rows,
        from_place(rows, 1),
        from_place(rows, -1),
        from_place(rows[:half], 2),
        from_place(rows[half:], -2),
    )


def bucket_bias(rab_table, distance):
    bucket_count = rab_table.shape[1]
    powers = 2 ** jnp.arange(bucket_count - 1, dtype=jnp.int32)
    bucket = jnp.sum((distance[:, None] >= powers[None, :]).astype(jnp.int32), axis=1)
    hits = (bucket[None, :] == jnp.arange(bucket_count, dtype=jnp.int32)[:, None]).astype(
        jnp.float32
    )
    return jnp.dot(
        rab_table, hits, precision=lax.Precision.HIGHEST, preferred_element_type=jnp.float32
    )


def silu(value):
    return half_silu(0.5 * value)


def half_silu(half):
    return half + half * jnp.tanh(half)


def marked(condition):
    return condition.astype(jnp.float32).astype(jnp.bfloat16)


def earlier(count):
    return lax.broadcasted_iota(jnp.int32, (count, count), 0) < lax.broadcasted_iota(
        jnp.int32, (count, count), 1
    )


def pick_kernel(numbers, ids, table, packed):
    rows, count = table.shape[0], ids.shape[1]
    copies, slot_count, _ = packed.shape
    there = ids[...] - numbers[0] * rows
    here = (there >= 0) & (there < rows)
    marks = jnp.broadcast_to(here.astype(jnp.float32), (8, count)).astype(jnp.bfloat16)
    rank = jnp.dot(marks, marked(earlier(count)), preferred_element_type=jnp.float32)[:1]
    slot = jnp.where(here, rank.astype(jnp.int32) - numbers[1], -1)
    taken = slot == lax.broadcasted_iota(jnp.int32, (slot_count, count), 0)
    wanted = there == lax.broadcasted_iota(jnp.int32, (rows, count), 0)
    picks = lax.dot_general(
        marked(taken), marked(wanted), (((1,), (1,)), ((), ())), preferred_element_type=jnp.float32
    ).astype(jnp.bfloat16)
    found = jnp.dot(picks, table[...], preferred_element_type=jnp.float32).astype(jnp.bfloat16)
    for copy in range(copies):
        packed[copy] = found


def pick(numbers, ids, table, copies):
    whole = pl.BlockSpec(memory_space=pltpu.VMEM)
    return pl.pallas_call(
        pick_kernel,
        in_specs=[pl.BlockSpec(memory_space=pltpu.SMEM), whole, whole],
        out_specs=whole,
        out_shape=jax.ShapeDtypeStruct((copies, slot_rows, table.shape[1]), jnp.bfloat16),
        compiler_params=pltpu.CompilerParams(vmem_limit_bytes=32 * 1024 * 1024),
        cost_estimate=pl.CostEstimate(
            flops=2 * slot_rows * table.shape[0] * table.shape[1],
            bytes_accessed=2 * table.shape[0] * table.shape[1],
            transcendentals=0,
        ),
    )(numbers, ids.reshape(1, -1), table)


def locate_kernel(table_rows, numbers, ids, slots, pair_slots, most):
    count, devices = ids.shape[1], most.shape[0]
    index = numbers[0]
    place, side = index // 2, lax.rem(index, 2)
    shard = ids[...] // table_rows
    member = lax.broadcasted_iota(jnp.int32, (devices, count), 0) == shard
    ranks = jnp.dot(marked(member), marked(earlier(count)), preferred_element_type=jnp.float32)
    rank = jnp.sum(jnp.where(member, ranks, 0.0), axis=0, keepdims=True)
    counts = jnp.sum(member.astype(jnp.float32), axis=1, keepdims=True)
    most[...] = jnp.broadcast_to(jnp.max(counts, axis=0, keepdims=True), most.shape).astype(
        jnp.int32
    )
    slot = rank.astype(jnp.int32) - numbers[1]
    source = shard // 2
    inside = (shard - 2 * source == side) & (slot >= 0) & (slot < slot_rows)
    ahead = lax.rem(source - place + devices, near_places)
    piece = jnp.where(ahead == 0, 0, jnp.where(ahead == near_places - 1, 1, ahead + 1))
    block = piece * (devices // 2 // near_places) + source // near_places
    facts = jnp.concatenate(
        [
            jnp.broadcast_to(jnp.where(inside, fact, -1).astype(jnp.float32), (8, count))
            for fact in (block, slot)
        ],
        axis=0,
    ).astype(jnp.bfloat16)

    def spread(chosen, out):
        both = lax.dot_general(
            marked(chosen), facts, (((1,), (1,)), ((), ())), preferred_element_type=jnp.float32
        )
        block_at, slot_at = both[:, :1].astype(jnp.int32), both[:, 8:9].astype(jnp.int32)
        out[...] = jnp.where(block_at < 0, -1, block_at * slot_rows + slot_at)

    own = count // devices
    at = lax.broadcasted_iota(jnp.int32, (count, count), 0)
    half = at // (count // 2)
    inner = at - half * (count // 2)
    owner_side = jnp.where(half == 0, side, 1 - side)
    kind = inner // (count // 4)
    owner = 2 * ((inner - kind * (count // 4)) // own) + kind
    original = owner * (2 * own) + owner_side * own + lax.rem(inner, own)
    spread(original == lax.broadcasted_iota(jnp.int32, (count, count), 1), slots)
    at = lax.broadcasted_iota(jnp.int32, (2 * own, count), 0)
    half = at // own
    owner_side = jnp.where(half == 0, side, 1 - side)
    original = place * (2 * own) + owner_side * own + at - half * own
    spread(original == lax.broadcasted_iota(jnp.int32, (2 * own, count), 1), pair_slots)


def locate(numbers, ids, table_rows, devices):
    whole = pl.BlockSpec(memory_space=pltpu.VMEM)
    count = ids.shape[0]
    return pl.pallas_call(
        lambda *refs: locate_kernel(table_rows, *refs),
        in_specs=[pl.BlockSpec(memory_space=pltpu.SMEM), whole],
        out_specs=[whole] * 3,
        out_shape=[
            jax.ShapeDtypeStruct((count, 1), jnp.int32),
            jax.ShapeDtypeStruct((2 * count // devices, 1), jnp.int32),
            jax.ShapeDtypeStruct((devices, 128), jnp.int32),
        ],
        compiler_params=pltpu.CompilerParams(vmem_limit_bytes=32 * 1024 * 1024),
        cost_estimate=pl.CostEstimate(
            flops=2 * count * count * devices, bytes_accessed=8 * count, transcendentals=0
        ),
    )(numbers, ids.reshape(1, -1))


def project_kernel(numbers, at, at_pair, rows_0, rows_1, rows_2, rows_3, rows_4, mine, other, *rest):
    proj_mine, proj_other, own_rows, slots = rest[-4:]
    cand_side, columns = proj_mine.shape
    own, width = own_rows.shape
    first = 0
    for rows in (rows_0, rows_1, rows_2, rows_3, rows_4):
        count = rows.shape[0]
        product_mine, product_other = (
            silu(
                lax.dot_general(
                    rows[...], part, (((1,), (1,)), ((), ())), preferred_element_type=jnp.float32
                )
            )
            for part in (mine[...], other[: mine.shape[0], :])
        )
        here = jnp.broadcast_to(numbers[0], product_mine.shape) % 2 == 0
        lanes = mine.shape[0]
        slots[first : first + count, :lanes] = jnp.where(
            here, product_mine, product_other
        ).astype(jnp.bfloat16)
        slots[first : first + count, lanes:] = jnp.where(
            here, product_other, product_mine
        ).astype(jnp.bfloat16)
        first += count
    place = lax.broadcasted_iota(jnp.int32, (cand_side, first), 1)
    for side, proj in ((0, proj_mine), (1, proj_other)):
        chosen = (at[side * cand_side : (side + 1) * cand_side, :] == place).astype(jnp.float32)
        proj[:cand_side, :] = jnp.dot(
            chosen.astype(jnp.bfloat16), slots[...], preferred_element_type=jnp.float32
        ).astype(jnp.bfloat16)
    place = lax.broadcasted_iota(jnp.int32, (2 * own, first), 1)
    chosen = (at_pair[...] == place).astype(jnp.float32).astype(jnp.bfloat16)
    total = None
    first = 0
    for rows in (rows_0, rows_1, rows_2, rows_3, rows_4):
        count = rows.shape[0]
        part = jnp.dot(
            chosen[:, first : first + count], rows[...], preferred_element_type=jnp.float32
        )
        total = part if total is None else total + part
        first += count
    own_rows[...] = total[:own].astype(jnp.bfloat16)
    for part in range(width // columns):
        proj_other[cand_side + part * own : cand_side + (part + 1) * own, :] = total[
            own:, part * columns : (part + 1) * columns
        ].astype(jnp.bfloat16)


def project(numbers, at, at_pair, rows, mine, other, ready):
    columns, width = 2 * mine.shape[0], mine.shape[1]
    cand_side = at.shape[0] // 2
    own = at_pair.shape[0] // 2
    slot_count = sum(piece.shape[0] for piece in rows)
    whole = pl.BlockSpec(memory_space=pltpu.VMEM)
    return pl.pallas_call(
        project_kernel,
        in_specs=[pl.BlockSpec(memory_space=pltpu.SMEM)]
        + [whole] * (4 + len(rows))
        + [pl.BlockSpec(memory_space=pl.ANY)] * len(ready),
        out_specs=[whole] * 3,
        out_shape=[
            jax.ShapeDtypeStruct((cand_side, columns), jnp.bfloat16),
            jax.ShapeDtypeStruct((cand_side + own * width // columns, columns), jnp.bfloat16),
            jax.ShapeDtypeStruct((own, width), jnp.bfloat16),
        ],
        scratch_shapes=[pltpu.VMEM((slot_count, columns), jnp.bfloat16)],
        compiler_params=pltpu.CompilerParams(vmem_limit_bytes=32 * 1024 * 1024),
        cost_estimate=pl.CostEstimate(
            flops=2 * slot_count * columns * (width + 2 * cand_side),
            bytes_accessed=2 * (slot_count + columns) * width,
            transcendentals=slot_count * columns,
        ),
    )(numbers, at, at_pair, *rows, mine, other, *ready)


def pack_kernel(feature_here, mine, arrived, own_rows, *rest):
    packed, embedded = rest[-2:]
    cand_side, columns = mine.shape
    own = own_rows.shape[0]
    proj = mine[...].astype(jnp.float32) + arrived[:cand_side, :].astype(jnp.float32)
    for part in range(own_rows.shape[1] // columns):
        lanes = slice(part * columns, (part + 1) * columns)
        other = arrived[cand_side + part * own : cand_side + (part + 1) * own, :]
        embedded[:, lanes] = (
            own_rows[:, lanes].astype(jnp.float32) + other.astype(jnp.float32)
        ).astype(jnp.bfloat16)
    block = 4 * feature_here
    queries = jnp.concatenate(
        [
            proj[:, side * block + 2 * feature_here : side * block + 3 * feature_here]
            for side in range(2)
        ],
        axis=1,
    ).T.astype(jnp.bfloat16)
    proj = proj.astype(jnp.bfloat16)
    column = packed.shape[0]
    cand_class = cand_side // 2
    for place in range(column):
        kind = place % 2
        first = kind * cand_class + place // 2 * own
        packed[place, :, :columns] = proj[first : first + own, :]
        for part in range(queries.shape[0] // own):
            lanes = slice(columns + part * cand_class, columns + (part + 1) * cand_class)
            packed[place, :, lanes] = queries[
                part * own : (part + 1) * own, kind * cand_class : (kind + 1) * cand_class
            ]


def pack(mine, arrived, own_rows, ready, feature_here):
    cand_side, columns = mine.shape
    own = own_rows.shape[0]
    column = cand_side // own
    packed_width = columns + 2 * feature_here * (cand_side // 2) // own
    whole = pl.BlockSpec(memory_space=pltpu.VMEM)
    return pl.pallas_call(
        lambda *refs: pack_kernel(feature_here, *refs),
        in_specs=[whole] * 3 + [pl.BlockSpec(memory_space=pl.ANY)] * len(ready),
        out_specs=[whole] * 2,
        out_shape=[
            jax.ShapeDtypeStruct((column, own, packed_width), jnp.bfloat16),
            jax.ShapeDtypeStruct(own_rows.shape, jnp.bfloat16),
        ],
        compiler_params=pltpu.CompilerParams(vmem_limit_bytes=32 * 1024 * 1024),
        cost_estimate=pl.CostEstimate(
            flops=cand_side * columns, bytes_accessed=8 * cand_side * columns, transcendentals=0
        ),
    )(mine, arrived, own_rows, *ready)


def spread_kernel(numbers, w_slice, other, out):
    rows, lanes = w_slice.shape
    half = rows // 2
    first = other.shape[0] - half
    theirs = jnp.concatenate(
        [other[first:, :lanes], other[first:, lanes : 2 * lanes]], axis=0
    )
    here = jnp.broadcast_to(numbers[0], (rows, lanes)) % 2 == 0
    ours = w_slice[...].astype(jnp.float32)
    theirs = theirs.astype(jnp.float32)
    top = jnp.where(here, ours, theirs).astype(jnp.bfloat16)
    bottom = jnp.where(here, theirs, ours).astype(jnp.bfloat16)
    for place in range(out.shape[0]):
        out[place, :rows, :] = top
        out[place, rows:, :] = bottom


def spread(numbers, w_slice, other, column):
    rows, lanes = w_slice.shape
    whole = pl.BlockSpec(memory_space=pltpu.VMEM)
    return pl.pallas_call(
        spread_kernel,
        in_specs=[pl.BlockSpec(memory_space=pltpu.SMEM), whole, whole],
        out_specs=whole,
        out_shape=jax.ShapeDtypeStruct((column, 2 * rows, lanes), jnp.bfloat16),
        compiler_params=pltpu.CompilerParams(vmem_limit_bytes=32 * 1024 * 1024),
        cost_estimate=pl.CostEstimate(
            flops=rows * lanes, bytes_accessed=4 * column * rows * lanes, transcendentals=0
        ),
    )(numbers, w_slice, other)


def attend_kernel(scale, heads, received, *refs):
    keys_values, bias, live, summed = refs[:8], refs[8], refs[9], refs[-1]
    first_head = pl.program_id(0) * heads
    cand, lanes = summed.shape
    head_size = lanes // heads
    events = keys_values[0].shape[0]
    own = received.shape[1]
    places = received.shape[0] // heads
    parts = head_size // (places * own)
    skip = received.shape[2] - parts * cand
    for head in range(heads):
        head_queries = jnp.concatenate(
            [
                received[head * places + place, :, skip + part * cand : skip + (part + 1) * cand]
                for place in range(places)
                for part in range(parts)
            ],
            axis=0,
        ).T
        lanes = slice(head * head_size, (head + 1) * head_size)
        head_bias = 0.5 * bias[pl.ds(first_head + head, 1), :]
        total = None
        for source in range(4):
            keys, values = keys_values[2 * source], keys_values[2 * source + 1]
            here = slice(source * events, (source + 1) * events)
            scores = lax.dot_general(
                head_queries,
                keys[:, lanes],
                (((1,), (1,)), ((), ())),
                preferred_element_type=jnp.float32,
            )
            weights = half_silu(scores * (0.5 * scale) + head_bias[:, here])
            weights = jnp.where(live[:, here] > 0.0, weights, 0.0).astype(jnp.bfloat16)
            part = jnp.dot(weights, values[:, lanes], preferred_element_type=jnp.float32)
            total = part if total is None else total + part
        summed[:, lanes] = total.astype(summed.dtype)


def attend(received, keys, values, others, bias, live, cand, ready):
    events, width = keys.shape
    head_count = bias.shape[0]
    head_size = width // head_count
    heads = 4
    lanes = heads * head_size
    column, own, packed_width = received.shape
    steps = head_count // heads
    first = pl.BlockSpec((events, lanes), lambda h: (0, h))
    second = pl.BlockSpec((events, lanes), lambda h: (1, h))
    key_values = [keys, values] + [array for other in others for array in (other, other)]
    return pl.pallas_call(
        lambda *refs: attend_kernel(head_size ** (-0.5), heads, *refs),
        grid=(steps,),
        in_specs=[
            pl.BlockSpec((column // steps, own, packed_width), lambda h: (h, 0, 0)),
            first,
            first,
        ]
        + [second, first] * len(others)
        + [
            pl.BlockSpec(bias.shape, lambda h: (0, 0)),
            pl.BlockSpec(live.shape, lambda h: (0, 0)),
        ]
        + [pl.BlockSpec(memory_space=pl.ANY)] * len(ready),
        out_specs=pl.BlockSpec((cand, lanes), lambda h: (0, h)),
        out_shape=jax.ShapeDtypeStruct((cand, width), jnp.bfloat16),
        compiler_params=pltpu.CompilerParams(vmem_limit_bytes=32 * 1024 * 1024),
        cost_estimate=pl.CostEstimate(
            flops=16 * cand * events * width,
            bytes_accessed=16 * events * width + 4 * cand * width,
            transcendentals=4 * cand * events * head_count,
        ),
    )(received, *key_values, bias, live, *ready)


def own_kernel(scale, rab, received, gain, after, self_term, gate):
    own, width = self_term.shape
    column = received.shape[0]
    lanes = width // column // 2
    gate_u, own_v, own_queries, own_k = (
        jnp.concatenate(
            [
                received[place, :, first : first + lanes].astype(jnp.float32)
                for place in range(column)
                for first in (part * lanes, (part + 4) * lanes)
            ],
            axis=1,
        )
        for part in range(4)
    )
    gate[...] = gate_u * gain[...]
    products = own_queries * own_k
    head_count = rab.shape[0]
    head_size = width // head_count
    for head in range(head_count):
        head_lanes = slice(head * head_size, (head + 1) * head_size)
        score = jnp.sum(products[:, head_lanes], axis=1, keepdims=True) * scale + rab[head, 0]
        self_term[:, head_lanes] = silu(score) * own_v[:, head_lanes]


def own_parts(received, rab, gain, own, after):
    width = gain.shape[0]
    whole = pl.BlockSpec(memory_space=pltpu.VMEM)
    scale = (width // rab.shape[0]) ** (-0.5)
    return pl.pallas_call(
        lambda *refs: own_kernel(scale, *refs),
        in_specs=[pl.BlockSpec(memory_space=pltpu.SMEM), whole, whole]
        + [pl.BlockSpec(memory_space=pl.ANY)],
        out_specs=[whole] * 2,
        out_shape=[jax.ShapeDtypeStruct((own, width), jnp.float32)] * 2,
        compiler_params=pltpu.CompilerParams(vmem_limit_bytes=32 * 1024 * 1024),
        cost_estimate=pl.CostEstimate(
            flops=8 * own * width, bytes_accessed=32 * own * width, transcendentals=own
        ),
    )(rab, received, gain.reshape(1, -1), after)


def finish_kernel(numbers, parts, self_term, gate, embedded, *rest):
    weights, scored = rest[:-1], rest[-1]
    history_sum = parts[0].astype(jnp.float32)
    for part in range(1, parts.shape[0]):
        history_sum = history_sum + parts[part].astype(jnp.float32)
    length = jnp.full((1, 1), numbers[0], jnp.int32).astype(jnp.float32)
    attended = history_sum * lax.rsqrt(length) + self_term[...]
    centre = jnp.mean(attended, axis=1, keepdims=True)
    spread = jnp.mean((attended - centre) ** 2, axis=1, keepdims=True)
    normed = (attended - centre) * lax.rsqrt(spread + 1e-05) * gate[...]
    normed = normed.astype(jnp.bfloat16)
    lanes = weights[0].shape[1]
    row_count = len(weights) // 2
    row, core = numbers[1], numbers[2]
    for index, columns_of in enumerate(weights):
        owner = core if index < row_count else 1 - core
        block = owner * row_count + lax.rem(row + row_count - index % row_count, row_count)
        columns = pl.ds(pl.multiple_of(block * lanes, lanes), lanes)
        projected = jnp.dot(normed, columns_of[...], preferred_element_type=jnp.float32)
        scored[:, columns] = (projected + embedded[:, columns].astype(jnp.float32)).astype(
            scored.dtype
        )


def finish(numbers, parts, self_term, gate, embedded, weights):
    whole = pl.BlockSpec(memory_space=pltpu.VMEM)
    rows, width = embedded.shape
    return pl.pallas_call(
        finish_kernel,
        in_specs=[pl.BlockSpec(memory_space=pltpu.SMEM)] + [whole] * (4 + len(weights)),
        out_specs=whole,
        out_shape=jax.ShapeDtypeStruct((rows, width), jnp.bfloat16),
        compiler_params=pltpu.CompilerParams(vmem_limit_bytes=32 * 1024 * 1024),
        cost_estimate=pl.CostEstimate(
            flops=2 * rows * width * width, bytes_accessed=4 * width * width, transcendentals=0
        ),
    )(numbers, parts, self_term, gate, embedded, *weights)


def local(
    history_keys, history_values, lengths, item_ids, item_table, w_proj, rab, norm_gain, w_out
):
    device_count = lax.axis_size("seq")
    column = device_count // 2
    index_here = lax.axis_index("seq")
    place, side = index_here // 2, index_here % 2
    batch_here = lax.axis_index("batch")
    row, core = batch_here // 4, batch_here % 2
    row_count = lax.axis_size("batch") // 4
    events_here, width = history_keys.shape
    head_count = rab.shape[0]
    table_rows = item_table.shape[0]
    cand_total = item_ids.shape[0]
    cand_here = cand_total // device_count
    cand_side = cand_total // 2
    feature_here = w_proj.shape[2]
    out_lanes = width // (2 * row_count)
    length = lengths[0]

    far_places = column // near_places

    def numbers_at(first_rank):
        return jnp.stack([index_here, first_rank])

    numbers = numbers_at(jnp.int32(0))
    picked = pick(numbers, item_ids, item_table, far_places)
    picked, w_proj, values, keys, w_out = lax.optimization_barrier(
        (picked, w_proj, history_values, history_keys, w_out)
    )
    rows = gather_slots(picked)

    w_mine = w_proj.transpose(1, 2, 0).reshape(4 * feature_here, width)
    w_slice = lax.dynamic_slice_in_dim(w_out, (core * row_count + row) * out_lanes, out_lanes, 1)
    w_half = w_slice.shape[0] // 2
    w_sent = jnp.concatenate([w_slice[:w_half], w_slice[w_half:]], axis=1)
    w_sent = jnp.concatenate([w_mine, jnp.tile(w_sent, (1, width // (2 * out_lanes)))])
    w_other = swap_pair(w_sent)
    w_here = exchange(spread(numbers, w_slice, w_other, column), column_groups())
    w_here = w_here.reshape(width, out_lanes)

    events_sent = jnp.concatenate([values, keys])
    pair_events, place_events = swap_pair(events_sent), swap_place(events_sent)
    others = pair_events, place_events, swap_pair(place_events)

    slots, pair_slots, most = locate(numbers, item_ids, table_rows, device_count)
    found = tuple(project(numbers, slots, pair_slots, rows, w_mine, w_other, (w_here, place_events, pair_events)))

    def another(state):
        first_rank, limit, found = state
        numbers = numbers_at(first_rank)
        rows = gather_slots(pick(numbers, item_ids, item_table, far_places))
        slots, pair_slots, _ = locate(numbers, item_ids, table_rows, device_count)
        more = project(numbers, slots, pair_slots, rows, w_mine, w_other, ())
        return first_rank + slot_rows, limit, tuple(a + b for a, b in zip(found, more))

    _, _, (proj_mine, proj_other, own_rows) = lax.while_loop(
        lambda state: state[0] < state[1], another, (jnp.int32(slot_rows), most[0, 0], found)
    )
    packed, embedded = pack(
        proj_mine, swap_pair(proj_other), own_rows, (), feature_here
    )
    received = exchange(packed, column_groups())

    sources = index_here ^ jnp.arange(4, dtype=jnp.int32)
    positions = sources[:, None] * events_here + jnp.arange(events_here, dtype=jnp.int32)[None, :]
    positions = positions.reshape(4 * events_here)
    bias = bucket_bias(rab, length - positions)
    live = (positions < length).astype(jnp.float32)[None, :]

    weights = [w_here] + [from_row(w_here, shift) for shift in range(1, row_count)]
    summed = attend(
        received, history_keys, history_values, others, bias, live, cand_side // 2, weights[1:]
    )
    parts = exchange(summed.reshape(column // 2, cand_here, width), class_groups())
    self_term, gate = own_parts(received, rab, norm_gain, cand_here, summed)
    weights = [*weights, *swap_core(jnp.stack(weights))]
    numbers = jnp.stack([length, row, core])
    return finish(numbers, parts, self_term, gate, embedded, weights)


def solution(mesh):
    return jax.shard_map(
        local,
        mesh=mesh,
        in_specs=(
            P(("batch", "seq"), None),
            P(("batch", "seq"), None),
            P("batch"),
            P("batch"),
            P("seq", None),
            P(None, None, "seq"),
            P(),
            P(),
            P("seq", None),
        ),
        out_specs=P(("batch", "seq"), None),
        check_vma=False,
    )
```

```python
import jax
import jax.numpy as jnp
from jax import lax
from jax.experimental import pallas as pl
from jax.experimental.pallas import tpu as pltpu
from jax.sharding import PartitionSpec as P

slot_rows = 32
near_places = 4


def groups_of(places):
    return [[2 * place + side for place in group] for side in range(2) for group in places]


def exchange(blocks, groups):
    return lax.all_to_all(
        blocks, "seq", split_axis=0, concat_axis=0, tiled=True, axis_index_groups=groups
    )


def column_groups():
    return groups_of([list(range(lax.axis_size("seq") // 2))])


def class_groups():
    column = lax.axis_size("seq") // 2
    return groups_of(
        [[place for place in range(column) if head_class(place) == kind] for kind in range(2)]
    )


def from_place(block, shift):
    count = lax.axis_size("seq")
    return lax.ppermute(block, "seq", [(i, (i + 2 * shift) % count) for i in range(count)])


def swap_pair(block):
    return lax.ppermute(block, "seq", [(i, i ^ 1) for i in range(lax.axis_size("seq"))])


def head_class(place):
    return place // 2 % 2


def partner_place(place, column):
    return (place + 2 * (place % 2) - 1) % column


def swap_place(block):
    count = lax.axis_size("seq")
    return lax.ppermute(
        block,
        "seq",
        [(i, 2 * partner_place(i // 2, count // 2) + i % 2) for i in range(count)],
    )


def swap_core(block):
    return lax.ppermute(block, "batch", [(i, i ^ 1) for i in range(lax.axis_size("batch"))])


def from_row(block, shift):
    count = lax.axis_size("batch")
    return lax.ppermute(block, "batch", [(i, (i + 4 * shift) % count) for i in range(count)])


def gather_slots(blocks):
    column = lax.axis_size("seq") // 2
    far = groups_of([list(range(at, column, near_places)) for at in range(near_places)])
    blocks = exchange(blocks, far)
    rows = blocks.reshape(blocks.shape[0] * blocks.shape[1], blocks.shape[2])
    half = rows.shape[0] // 2
    return (
        rows,
        from_place(rows, 1),
        from_place(rows, -1),
        from_place(rows[:half], 2),
        from_place(rows[half:], -2),
    )


def bias_kernel(numbers, rab, bias, live):
    head_count, bucket_count = rab.shape
    sources = numbers.shape[0] - 1
    events = bias.shape[1] // sources
    step = lax.broadcasted_iota(jnp.int32, (head_count, events), 1)
    for source in range(sources):
        here = slice(source * events, (source + 1) * events)
        distance = numbers[0] - numbers[1 + source] * events - step
        bucket = jnp.zeros((head_count, events), jnp.int32)
        for power in range(bucket_count - 1):
            bucket = bucket + (distance >= 2**power).astype(jnp.int32)
        total = jnp.zeros((head_count, events), jnp.float32)
        for entry in range(bucket_count):
            total = total + jnp.where(bucket == entry, rab[:, entry : entry + 1], 0.0)
        bias[:, here] = total
        live[:, here] = (distance[:1] > 0).astype(jnp.float32)


def biases(numbers, rab, events):
    whole = pl.BlockSpec(memory_space=pltpu.VMEM)
    count = (numbers.shape[0] - 1) * events
    return pl.pallas_call(
        bias_kernel,
        in_specs=[pl.BlockSpec(memory_space=pltpu.SMEM), whole],
        out_specs=[whole] * 2,
        out_shape=[
            jax.ShapeDtypeStruct((rab.shape[0], count), jnp.float32),
            jax.ShapeDtypeStruct((1, count), jnp.float32),
        ],
        cost_estimate=pl.CostEstimate(
            flops=64 * rab.shape[0] * count, bytes_accessed=40 * count, transcendentals=0
        ),
    )(numbers, rab)


def silu(value):
    return half_silu(0.5 * value)


def half_silu(half):
    return half + half * jnp.tanh(half)


def marked(condition):
    return condition.astype(jnp.float32).astype(jnp.bfloat16)


def earlier(count):
    return lax.broadcasted_iota(jnp.int32, (count, count), 0) < lax.broadcasted_iota(
        jnp.int32, (count, count), 1
    )


def pick_kernel(numbers, ids, table, packed):
    rows, count = table.shape[0], ids.shape[1]
    copies, slot_count, _ = packed.shape
    there = ids[...] - numbers[0] * rows
    here = (there >= 0) & (there < rows)
    marks = jnp.broadcast_to(here.astype(jnp.float32), (8, count)).astype(jnp.bfloat16)
    rank = jnp.dot(marks, marked(earlier(count)), preferred_element_type=jnp.float32)[:1]
    slot = jnp.where(here, rank.astype(jnp.int32) - numbers[1], -1)
    taken = slot == lax.broadcasted_iota(jnp.int32, (slot_count, count), 0)
    wanted = there == lax.broadcasted_iota(jnp.int32, (rows, count), 0)
    picks = lax.dot_general(
        marked(taken), marked(wanted), (((1,), (1,)), ((), ())), preferred_element_type=jnp.float32
    ).astype(jnp.bfloat16)
    found = jnp.dot(picks, table[...], preferred_element_type=jnp.float32).astype(jnp.bfloat16)
    for copy in range(copies):
        packed[copy] = found


def pick(numbers, ids, table, copies):
    whole = pl.BlockSpec(memory_space=pltpu.VMEM)
    return pl.pallas_call(
        pick_kernel,
        in_specs=[pl.BlockSpec(memory_space=pltpu.SMEM), whole, whole],
        out_specs=whole,
        out_shape=jax.ShapeDtypeStruct((copies, slot_rows, table.shape[1]), jnp.bfloat16),
        compiler_params=pltpu.CompilerParams(vmem_limit_bytes=32 * 1024 * 1024),
        cost_estimate=pl.CostEstimate(
            flops=2 * slot_rows * table.shape[0] * table.shape[1],
            bytes_accessed=2 * table.shape[0] * table.shape[1],
            transcendentals=0,
        ),
    )(numbers, ids.reshape(1, -1), table)


def split_kernel(head_size, kind, keys, values, kept, sent):
    events, width = keys.shape

    def place(parity):
        for first, array in ((0, keys), (events, values)):
            for head in range(0, width // head_size, 2):
                lanes = slice(head // 2 * head_size, (head // 2 + 1) * head_size)
                for out, which in ((kept, head + parity), (sent, head + 1 - parity)):
                    out[first : first + events, lanes] = array[
                        :, which * head_size : (which + 1) * head_size
                    ]

    @pl.when(kind[0] == 0)
    def _():
        place(0)

    @pl.when(kind[0] != 0)
    def _():
        place(1)


def split_heads(kind, keys, values, head_size):
    whole = pl.BlockSpec(memory_space=pltpu.VMEM)
    events, width = keys.shape
    return pl.pallas_call(
        lambda *refs: split_kernel(head_size, *refs),
        in_specs=[pl.BlockSpec(memory_space=pltpu.SMEM), whole, whole],
        out_specs=[whole] * 2,
        out_shape=[jax.ShapeDtypeStruct((2 * events, width // 2), jnp.bfloat16)] * 2,
        compiler_params=pltpu.CompilerParams(vmem_limit_bytes=32 * 1024 * 1024),
        cost_estimate=pl.CostEstimate(
            flops=4 * events * width, bytes_accessed=8 * events * width, transcendentals=0
        ),
    )(kind, keys, values)


def locate_kernel(table_rows, numbers, ids, slots, pair_slots, most):
    count, devices = ids.shape[1], most.shape[0]
    index = numbers[0]
    place, side = index // 2, lax.rem(index, 2)
    shard = ids[...] // table_rows
    member = lax.broadcasted_iota(jnp.int32, (devices, count), 0) == shard
    ranks = jnp.dot(marked(member), marked(earlier(count)), preferred_element_type=jnp.float32)
    rank = jnp.sum(jnp.where(member, ranks, 0.0), axis=0, keepdims=True)
    counts = jnp.sum(member.astype(jnp.float32), axis=1, keepdims=True)
    most[...] = jnp.broadcast_to(jnp.max(counts, axis=0, keepdims=True), most.shape).astype(
        jnp.int32
    )
    slot = rank.astype(jnp.int32) - numbers[1]
    source = shard // 2
    inside = (shard - 2 * source == side) & (slot >= 0) & (slot < slot_rows)
    ahead = lax.rem(source - place + devices, near_places)
    piece = jnp.where(ahead == 0, 0, jnp.where(ahead == near_places - 1, 1, ahead + 1))
    block = piece * (devices // 2 // near_places) + source // near_places
    facts = jnp.concatenate(
        [
            jnp.broadcast_to(jnp.where(inside, fact, -1).astype(jnp.float32), (8, count))
            for fact in (block, slot)
        ],
        axis=0,
    ).astype(jnp.bfloat16)

    def spread(chosen, out):
        both = lax.dot_general(
            marked(chosen), facts, (((1,), (1,)), ((), ())), preferred_element_type=jnp.float32
        )
        block_at, slot_at = both[:, :1].astype(jnp.int32), both[:, 8:9].astype(jnp.int32)
        out[...] = jnp.where(block_at < 0, -1, block_at * slot_rows + slot_at)

    own = count // devices
    at = lax.broadcasted_iota(jnp.int32, (count, count), 0)
    half = at // (count // 2)
    inner = at - half * (count // 2)
    owner_side = jnp.where(half == 0, side, 1 - side)
    original = (inner // own) * (2 * own) + owner_side * own + lax.rem(inner, own)
    spread(original == lax.broadcasted_iota(jnp.int32, (count, count), 1), slots)
    at = lax.broadcasted_iota(jnp.int32, (2 * own, count), 0)
    half = at // own
    owner_side = jnp.where(half == 0, side, 1 - side)
    original = place * (2 * own) + owner_side * own + at - half * own
    spread(original == lax.broadcasted_iota(jnp.int32, (2 * own, count), 1), pair_slots)


def locate(numbers, ids, table_rows, devices):
    whole = pl.BlockSpec(memory_space=pltpu.VMEM)
    count = ids.shape[0]
    return pl.pallas_call(
        lambda *refs: locate_kernel(table_rows, *refs),
        in_specs=[pl.BlockSpec(memory_space=pltpu.SMEM), whole],
        out_specs=[whole] * 3,
        out_shape=[
            jax.ShapeDtypeStruct((count, 1), jnp.int32),
            jax.ShapeDtypeStruct((2 * count // devices, 1), jnp.int32),
            jax.ShapeDtypeStruct((devices, 128), jnp.int32),
        ],
        compiler_params=pltpu.CompilerParams(vmem_limit_bytes=32 * 1024 * 1024),
        cost_estimate=pl.CostEstimate(
            flops=2 * count * count * devices, bytes_accessed=8 * count, transcendentals=0
        ),
    )(numbers, ids.reshape(1, -1))


def project_kernel(numbers, at, at_pair, rows_0, rows_1, rows_2, rows_3, rows_4, mine, other, *rest):
    proj_mine, proj_other, own_rows, slots = rest[-4:]
    cand_side, columns = proj_mine.shape
    own, width = own_rows.shape
    first = 0
    for rows in (rows_0, rows_1, rows_2, rows_3, rows_4):
        count = rows.shape[0]
        product_mine, product_other = (
            silu(
                lax.dot_general(
                    rows[...], part, (((1,), (1,)), ((), ())), preferred_element_type=jnp.float32
                )
            )
            for part in (mine[...], other[: mine.shape[0], :])
        )
        here = jnp.broadcast_to(numbers[0], product_mine.shape) % 2 == 0
        lanes = mine.shape[0]
        slots[first : first + count, :lanes] = jnp.where(
            here, product_mine, product_other
        ).astype(jnp.bfloat16)
        slots[first : first + count, lanes:] = jnp.where(
            here, product_other, product_mine
        ).astype(jnp.bfloat16)
        first += count
    place = lax.broadcasted_iota(jnp.int32, (cand_side, first), 1)
    for side, proj in ((0, proj_mine), (1, proj_other)):
        chosen = (at[side * cand_side : (side + 1) * cand_side, :] == place).astype(jnp.float32)
        proj[:cand_side, :] = jnp.dot(
            chosen.astype(jnp.bfloat16), slots[...], preferred_element_type=jnp.float32
        ).astype(jnp.bfloat16)
    place = lax.broadcasted_iota(jnp.int32, (2 * own, first), 1)
    chosen = (at_pair[...] == place).astype(jnp.float32).astype(jnp.bfloat16)
    total = None
    first = 0
    for rows in (rows_0, rows_1, rows_2, rows_3, rows_4):
        count = rows.shape[0]
        part = jnp.dot(
            chosen[:, first : first + count], rows[...], preferred_element_type=jnp.float32
        )
        total = part if total is None else total + part
        first += count
    own_rows[...] = total[:own].astype(jnp.bfloat16)
    for part in range(width // columns):
        proj_other[cand_side + part * own : cand_side + (part + 1) * own, :] = total[
            own:, part * columns : (part + 1) * columns
        ].astype(jnp.bfloat16)


def project(numbers, at, at_pair, rows, mine, other, ready):
    columns, width = 2 * mine.shape[0], mine.shape[1]
    cand_side = at.shape[0] // 2
    own = at_pair.shape[0] // 2
    slot_count = sum(piece.shape[0] for piece in rows)
    whole = pl.BlockSpec(memory_space=pltpu.VMEM)
    return pl.pallas_call(
        project_kernel,
        in_specs=[pl.BlockSpec(memory_space=pltpu.SMEM)]
        + [whole] * (4 + len(rows))
        + [pl.BlockSpec(memory_space=pl.ANY)] * len(ready),
        out_specs=[whole] * 3,
        out_shape=[
            jax.ShapeDtypeStruct((cand_side, columns), jnp.bfloat16),
            jax.ShapeDtypeStruct((cand_side + own * width // columns, columns), jnp.bfloat16),
            jax.ShapeDtypeStruct((own, width), jnp.bfloat16),
        ],
        scratch_shapes=[pltpu.VMEM((slot_count, columns), jnp.bfloat16)],
        compiler_params=pltpu.CompilerParams(vmem_limit_bytes=32 * 1024 * 1024),
        cost_estimate=pl.CostEstimate(
            flops=2 * slot_count * columns * (width + 2 * cand_side),
            bytes_accessed=2 * (slot_count + columns) * width,
            transcendentals=slot_count * columns,
        ),
    )(numbers, at, at_pair, *rows, mine, other, *ready)


def pack_kernel(feature_here, numbers, mine, arrived, own_rows, w_slice, w_other, *rest):
    queries, packed, embedded = rest[-3:]
    cand_side, columns = mine.shape
    own = own_rows.shape[0]
    proj = mine[...].astype(jnp.float32) + arrived[:cand_side, :].astype(jnp.float32)
    for part in range(own_rows.shape[1] // columns):
        lanes = slice(part * columns, (part + 1) * columns)
        other = arrived[cand_side + part * own : cand_side + (part + 1) * own, :]
        embedded[:, lanes] = (
            own_rows[:, lanes].astype(jnp.float32) + other.astype(jnp.float32)
        ).astype(jnp.bfloat16)
    block = 4 * feature_here
    queries[...] = jnp.concatenate(
        [
            proj[:, side * block + 2 * feature_here : side * block + 3 * feature_here]
            for side in range(2)
        ],
        axis=1,
    ).T.astype(jnp.bfloat16)
    column = packed.shape[0]
    packed[:, :, :columns] = proj.astype(jnp.bfloat16).reshape(column, own, columns)
    lanes = w_slice.shape[1]
    first = w_other.shape[0] - own
    here = jnp.broadcast_to(numbers[0], (own, lanes)) % 2 == 0
    parts = w_slice.shape[0] // own
    for part in range(parts):
        ours = w_slice[part * own : (part + 1) * own, :].astype(jnp.float32)
        theirs = w_other[first:, part * lanes : (part + 1) * lanes].astype(jnp.float32)
        for place, rows in (
            (part, jnp.where(here, ours, theirs)),
            (parts + part, jnp.where(here, theirs, ours)),
        ):
            packed[:, :, columns + place * lanes : columns + (place + 1) * lanes] = (
                jnp.broadcast_to(rows.astype(jnp.bfloat16)[None], (column, own, lanes))
            )


def pack(numbers, mine, arrived, own_rows, w_slice, w_other, feature_here, ready):
    cand_side, columns = mine.shape
    own = own_rows.shape[0]
    column = cand_side // own
    packed_width = columns + 2 * w_slice.shape[0] * w_slice.shape[1] // own
    whole = pl.BlockSpec(memory_space=pltpu.VMEM)
    return pl.pallas_call(
        lambda *refs: pack_kernel(feature_here, *refs),
        in_specs=[pl.BlockSpec(memory_space=pltpu.SMEM)]
        + [whole] * 5
        + [pl.BlockSpec(memory_space=pl.ANY)] * len(ready),
        out_specs=[whole] * 3,
        out_shape=[
            jax.ShapeDtypeStruct((2 * feature_here, cand_side), jnp.bfloat16),
            jax.ShapeDtypeStruct((column, own, packed_width), jnp.bfloat16),
            jax.ShapeDtypeStruct(own_rows.shape, jnp.bfloat16),
        ],
        compiler_params=pltpu.CompilerParams(vmem_limit_bytes=32 * 1024 * 1024),
        cost_estimate=pl.CostEstimate(
            flops=cand_side * columns, bytes_accessed=8 * cand_side * columns, transcendentals=0
        ),
    )(numbers, mine, arrived, own_rows, w_slice, w_other, *ready)


def attend_kernel(scale, heads, numbers, queries, *refs):
    keys_values, bias, live, summed = refs[:8], refs[8], refs[9], refs[-2]
    first_head = pl.program_id(0) * heads
    kind = numbers[0]
    head_size = queries.shape[0] // heads
    events = keys_values[0].shape[0]
    for head in range(heads):
        lanes = slice(head * head_size, (head + 1) * head_size)
        head_queries = queries[lanes, :].T
        head_bias = 0.5 * bias[pl.ds(2 * (first_head + head) + kind, 1), :]
        total = None
        for source in range(4):
            keys, values = keys_values[2 * source], keys_values[2 * source + 1]
            here = slice(source * events, (source + 1) * events)
            scores = lax.dot_general(
                head_queries,
                keys[:, lanes],
                (((1,), (1,)), ((), ())),
                preferred_element_type=jnp.float32,
            )
            weights = half_silu(scores * (0.5 * scale) + head_bias[:, here])
            weights = jnp.where(live[:, here] > 0.0, weights, 0.0).astype(jnp.bfloat16)
            part = jnp.dot(weights, values[:, lanes], preferred_element_type=jnp.float32)
            total = part if total is None else total + part
        summed[:, lanes] = total.astype(summed.dtype)


def attend(kind, queries, sources, bias, live, through):
    width, cand = queries.shape
    events = sources[0].shape[0] // 2
    head_size = 2 * width // bias.shape[0]
    heads = 2
    lanes = heads * head_size
    first = pl.BlockSpec((events, lanes), lambda h: (0, h))
    second = pl.BlockSpec((events, lanes), lambda h: (1, h))
    held = pl.BlockSpec(memory_space=pl.ANY)
    operands = [array for source in sources for array in (source, source)]
    return pl.pallas_call(
        lambda *refs: attend_kernel(head_size ** (-0.5), heads, *refs),
        grid=(width // lanes,),
        in_specs=[
            pl.BlockSpec(memory_space=pltpu.SMEM),
            pl.BlockSpec((lanes, cand), lambda h: (h, 0)),
        ]
        + [first, second] * len(sources)
        + [
            pl.BlockSpec(bias.shape, lambda h: (0, 0)),
            pl.BlockSpec(live.shape, lambda h: (0, 0)),
            held,
        ],
        out_specs=[pl.BlockSpec((cand, lanes), lambda h: (0, h)), held],
        out_shape=[
            jax.ShapeDtypeStruct((cand, width), jnp.float32),
            jax.ShapeDtypeStruct(through.shape, through.dtype),
        ],
        input_output_aliases={12: 1},
        compiler_params=pltpu.CompilerParams(vmem_limit_bytes=32 * 1024 * 1024),
        cost_estimate=pl.CostEstimate(
            flops=16 * cand * events * width,
            bytes_accessed=16 * events * width + 4 * cand * width,
            transcendentals=4 * cand * events * (width // head_size),
        ),
    )(kind, queries, *operands, bias, live, through)


def own_kernel(scale, rab, received, gain, self_term, gate):
    own, width = self_term.shape
    column = received.shape[0]
    lanes = width // column // 2
    gate_u, own_v, own_queries, own_k = (
        jnp.concatenate(
            [
                received[place, :, first : first + lanes].astype(jnp.float32)
                for place in range(column)
                for first in (part * lanes, (part + 4) * lanes)
            ],
            axis=1,
        )
        for part in range(4)
    )
    gate[...] = gate_u * gain[...]
    products = own_queries * own_k
    head_count = rab.shape[0]
    head_size = width // head_count
    for head in range(head_count):
        head_lanes = slice(head * head_size, (head + 1) * head_size)
        score = jnp.sum(products[:, head_lanes], axis=1, keepdims=True) * scale + rab[head, 0]
        self_term[:, head_lanes] = silu(score) * own_v[:, head_lanes]


def own_parts(received, rab, gain, own):
    width = gain.shape[0]
    whole = pl.BlockSpec(memory_space=pltpu.VMEM)
    scale = (width // rab.shape[0]) ** (-0.5)
    return pl.pallas_call(
        lambda *refs: own_kernel(scale, *refs),
        in_specs=[pl.BlockSpec(memory_space=pltpu.SMEM), whole, whole],
        out_specs=[whole] * 2,
        out_shape=[jax.ShapeDtypeStruct((own, width), jnp.float32)] * 2,
        compiler_params=pltpu.CompilerParams(vmem_limit_bytes=32 * 1024 * 1024),
        cost_estimate=pl.CostEstimate(
            flops=8 * own * width, bytes_accessed=32 * own * width, transcendentals=own
        ),
    )(rab, received, gain.reshape(1, -1))


def finish_kernel(head_size, numbers, parts, self_term, gate, embedded, *rest):
    weights, scored = rest[:-1], rest[-1]
    classes = []
    for kind in range(2):
        total = None
        for part in range(parts.shape[0]):
            if head_class(part) == kind:
                rows = parts[part].astype(jnp.float32)
                total = rows if total is None else total + rows
        classes.append(total)
    history_sum = jnp.concatenate(
        [
            classes[kind][:, first : first + head_size]
            for first in range(0, classes[0].shape[1], head_size)
            for kind in range(2)
        ],
        axis=1,
    )
    length = jnp.full((1, 1), numbers[0], jnp.int32).astype(jnp.float32)
    attended = history_sum * lax.rsqrt(length) + self_term[...]
    centre = jnp.mean(attended, axis=1, keepdims=True)
    spread = jnp.mean((attended - centre) ** 2, axis=1, keepdims=True)
    normed = (attended - centre) * lax.rsqrt(spread + 1e-05) * gate[...]
    normed = normed.astype(jnp.bfloat16)
    lanes = weights[0].shape[1]
    row_count = len(weights) // 2
    row, core = numbers[1], numbers[2]
    for index, columns_of in enumerate(weights):
        owner = core if index < row_count else 1 - core
        block = owner * row_count + lax.rem(row + row_count - index % row_count, row_count)
        columns = pl.ds(pl.multiple_of(block * lanes, lanes), lanes)
        projected = jnp.dot(normed, columns_of[...], preferred_element_type=jnp.float32)
        scored[:, columns] = (projected + embedded[:, columns].astype(jnp.float32)).astype(
            scored.dtype
        )


def finish(head_size, numbers, parts, self_term, gate, embedded, weights):
    whole = pl.BlockSpec(memory_space=pltpu.VMEM)
    rows, width = embedded.shape
    return pl.pallas_call(
        lambda *refs: finish_kernel(head_size, *refs),
        in_specs=[pl.BlockSpec(memory_space=pltpu.SMEM)] + [whole] * (4 + len(weights)),
        out_specs=whole,
        out_shape=jax.ShapeDtypeStruct((rows, width), jnp.bfloat16),
        compiler_params=pltpu.CompilerParams(vmem_limit_bytes=32 * 1024 * 1024),
        cost_estimate=pl.CostEstimate(
            flops=2 * rows * width * width, bytes_accessed=4 * width * width, transcendentals=0
        ),
    )(numbers, parts, self_term, gate, embedded, *weights)


def local(
    history_keys, history_values, lengths, item_ids, item_table, w_proj, rab, norm_gain, w_out
):
    device_count = lax.axis_size("seq")
    column = device_count // 2
    index_here = lax.axis_index("seq")
    place, side = index_here // 2, index_here % 2
    batch_here = lax.axis_index("batch")
    row, core = batch_here // 4, batch_here % 2
    row_count = lax.axis_size("batch") // 4
    events_here, width = history_keys.shape
    head_count = rab.shape[0]
    table_rows = item_table.shape[0]
    cand_total = item_ids.shape[0]
    cand_here = cand_total // device_count
    cand_side = cand_total // 2
    feature_here = w_proj.shape[2]
    out_lanes = width // (2 * row_count)
    length = lengths[0]

    far_places = column // near_places

    def numbers_at(first_rank):
        return jnp.stack([index_here, first_rank])

    numbers = numbers_at(jnp.int32(0))
    picked = pick(numbers, item_ids, item_table, far_places)
    picked, w_proj, values, keys, w_out = lax.optimization_barrier(
        (picked, w_proj, history_values, history_keys, w_out)
    )
    rows = gather_slots(picked)

    w_mine = w_proj.transpose(1, 2, 0).reshape(4 * feature_here, width)
    w_slice = lax.dynamic_slice_in_dim(w_out, (core * row_count + row) * out_lanes, out_lanes, 1)
    w_half = w_slice.shape[0] // 2
    w_sent = jnp.concatenate([w_slice[:w_half], w_slice[w_half:]], axis=1)
    w_sent = jnp.concatenate([w_mine, jnp.tile(w_sent, (1, width // (2 * out_lanes)))])
    w_other = swap_pair(w_sent)

    kind = head_class(place)

    own_events, sent_events = split_heads(kind[None], keys, values, width // head_count)
    place_events = swap_place(sent_events)
    sources = own_events, swap_pair(own_events), place_events, swap_pair(place_events)

    partner = 2 * partner_place(place, column) + side
    devices = jnp.stack([length, index_here, index_here ^ 1, partner, partner ^ 1])
    bias, live = biases(devices, rab, events_here)

    slots, pair_slots, most = locate(numbers, item_ids, table_rows, device_count)
    found = tuple(project(numbers, slots, pair_slots, rows, w_mine, w_other, (*sources[1:3], bias, live)))

    def another(state):
        first_rank, limit, found = state
        numbers = numbers_at(first_rank)
        rows = gather_slots(pick(numbers, item_ids, item_table, far_places))
        slots, pair_slots, _ = locate(numbers, item_ids, table_rows, device_count)
        more = project(numbers, slots, pair_slots, rows, w_mine, w_other, ())
        return first_rank + slot_rows, limit, tuple(a + b for a, b in zip(found, more))

    _, _, (proj_mine, proj_other, own_rows) = lax.while_loop(
        lambda state: state[0] < state[1], another, (jnp.int32(slot_rows), most[0, 0], found)
    )
    side_queries, packed, embedded = pack(
        numbers,
        proj_mine,
        swap_pair(proj_other),
        own_rows,
        w_slice,
        w_other,
        feature_here,
        sources[3:],
    )
    received = exchange(packed, column_groups())
    class_queries = lax.all_gather(
        side_queries, "seq", axis=0, tiled=True, axis_index_groups=class_groups()
    )

    summed, received = attend(kind[None], class_queries, sources, bias, live, received)
    parts = exchange(summed.reshape(column, cand_here, width // 2), column_groups())
    self_term, gate = own_parts(received, rab, norm_gain, cand_here)

    w_here = (
        received[:, :, 8 * feature_here :]
        .reshape(column, cand_here, 2 * w_slice.shape[0] // cand_here, out_lanes)
        .transpose(0, 2, 1, 3)
        .reshape(width, out_lanes)
    )
    weights = [w_here] + [from_row(w_here, shift) for shift in range(1, row_count)]
    weights = [*weights, *swap_core(jnp.stack(weights))]
    numbers = jnp.stack([length, row, core])
    return finish(width // head_count, numbers, parts, self_term, gate, embedded, weights)


def solution(mesh):
    return jax.shard_map(
        local,
        mesh=mesh,
        in_specs=(
            P(("batch", "seq"), None),
            P(("batch", "seq"), None),
            P("batch"),
            P("batch"),
            P("seq", None),
            P(None, None, "seq"),
            P(),
            P(),
            P("seq", None),
        ),
        out_specs=P(("batch", "seq"), None),
        check_vma=False,
    )
```

```python
import jax
import jax.numpy as jnp
from jax import lax
from jax.experimental import pallas as pl
from jax.experimental.pallas import tpu as pltpu
from jax.sharding import PartitionSpec as P

slot_rows = 32
near_places = 4


def groups_of(places):
    return [[2 * place + side for place in group] for side in range(2) for group in places]


def exchange(blocks, groups):
    return lax.all_to_all(
        blocks, "seq", split_axis=0, concat_axis=0, tiled=True, axis_index_groups=groups
    )


def column_groups():
    return groups_of([list(range(lax.axis_size("seq") // 2))])


def from_place(block, shift):
    count = lax.axis_size("seq")
    return lax.ppermute(block, "seq", [(i, (i + 2 * shift) % count) for i in range(count)])


def swap_pair(block):
    return lax.ppermute(block, "seq", [(i, i ^ 1) for i in range(lax.axis_size("seq"))])


def swap_core(block):
    return lax.ppermute(block, "batch", [(i, i ^ 1) for i in range(lax.axis_size("batch"))])


def from_row(block, shift):
    count = lax.axis_size("batch")
    return lax.ppermute(block, "batch", [(i, (i + 4 * shift) % count) for i in range(count)])


def gather_slots(blocks):
    column = lax.axis_size("seq") // 2
    far = groups_of([list(range(at, column, near_places)) for at in range(near_places)])
    blocks = exchange(blocks, far)
    rows = blocks.reshape(blocks.shape[0] * blocks.shape[1], blocks.shape[2])
    half = rows.shape[0] // 2
    return (
        rows,
        from_place(rows, 1),
        from_place(rows, -1),
        from_place(rows[:half], 2),
        from_place(rows[half:], -2),
    )


def bias_kernel(numbers, rab, bias, live):
    head_count, bucket_count = rab.shape
    sources = numbers.shape[0] - 1
    events = bias.shape[1] // sources
    step = lax.broadcasted_iota(jnp.int32, (head_count, events), 1)
    for source in range(sources):
        here = slice(source * events, (source + 1) * events)
        distance = numbers[0] - numbers[1 + source] * events - step
        bucket = jnp.zeros((head_count, events), jnp.int32)
        for power in range(bucket_count - 1):
            bucket = bucket + (distance >= 2**power).astype(jnp.int32)
        total = jnp.zeros((head_count, events), jnp.float32)
        for entry in range(bucket_count):
            total = total + jnp.where(bucket == entry, rab[:, entry : entry + 1], 0.0)
        bias[:, here] = total
        live[:, here] = (distance[:1] > 0).astype(jnp.float32)


def biases(numbers, rab, events):
    whole = pl.BlockSpec(memory_space=pltpu.VMEM)
    count = (numbers.shape[0] - 1) * events
    return pl.pallas_call(
        bias_kernel,
        in_specs=[pl.BlockSpec(memory_space=pltpu.SMEM), whole],
        out_specs=[whole] * 2,
        out_shape=[
            jax.ShapeDtypeStruct((rab.shape[0], count), jnp.float32),
            jax.ShapeDtypeStruct((1, count), jnp.float32),
        ],
        cost_estimate=pl.CostEstimate(
            flops=64 * rab.shape[0] * count, bytes_accessed=40 * count, transcendentals=0
        ),
    )(numbers, rab)


def silu(value):
    return half_silu(0.5 * value)


def half_silu(half):
    return half + half * jnp.tanh(half)


def marked(condition):
    return condition.astype(jnp.float32).astype(jnp.bfloat16)


def earlier(count):
    return lax.broadcasted_iota(jnp.int32, (count, count), 0) < lax.broadcasted_iota(
        jnp.int32, (count, count), 1
    )


def pick_kernel(numbers, ids, table, packed):
    rows, count = table.shape[0], ids.shape[1]
    copies, slot_count, _ = packed.shape
    there = ids[...] - numbers[0] * rows
    here = (there >= 0) & (there < rows)
    marks = jnp.broadcast_to(here.astype(jnp.float32), (8, count)).astype(jnp.bfloat16)
    rank = jnp.dot(marks, marked(earlier(count)), preferred_element_type=jnp.float32)[:1]
    slot = jnp.where(here, rank.astype(jnp.int32) - numbers[1], -1)
    taken = slot == lax.broadcasted_iota(jnp.int32, (slot_count, count), 0)
    wanted = there == lax.broadcasted_iota(jnp.int32, (rows, count), 0)
    picks = lax.dot_general(
        marked(taken), marked(wanted), (((1,), (1,)), ((), ())), preferred_element_type=jnp.float32
    ).astype(jnp.bfloat16)
    found = jnp.dot(picks, table[...], preferred_element_type=jnp.float32).astype(jnp.bfloat16)
    for copy in range(copies):
        packed[copy] = found


def pick(numbers, ids, table, copies):
    whole = pl.BlockSpec(memory_space=pltpu.VMEM)
    return pl.pallas_call(
        pick_kernel,
        in_specs=[pl.BlockSpec(memory_space=pltpu.SMEM), whole, whole],
        out_specs=whole,
        out_shape=jax.ShapeDtypeStruct((copies, slot_rows, table.shape[1]), jnp.bfloat16),
        compiler_params=pltpu.CompilerParams(vmem_limit_bytes=32 * 1024 * 1024),
        cost_estimate=pl.CostEstimate(
            flops=2 * slot_rows * table.shape[0] * table.shape[1],
            bytes_accessed=2 * table.shape[0] * table.shape[1],
            transcendentals=0,
        ),
    )(numbers, ids.reshape(1, -1), table)


def locate_kernel(table_rows, numbers, ids, slots, pair_slots, most):
    count, devices = ids.shape[1], most.shape[0]
    index = numbers[0]
    place, side = index // 2, lax.rem(index, 2)
    shard = ids[...] // table_rows
    member = lax.broadcasted_iota(jnp.int32, (devices, count), 0) == shard
    ranks = jnp.dot(marked(member), marked(earlier(count)), preferred_element_type=jnp.float32)
    rank = jnp.sum(jnp.where(member, ranks, 0.0), axis=0, keepdims=True)
    counts = jnp.sum(member.astype(jnp.float32), axis=1, keepdims=True)
    most[...] = jnp.broadcast_to(jnp.max(counts, axis=0, keepdims=True), most.shape).astype(
        jnp.int32
    )
    slot = rank.astype(jnp.int32) - numbers[1]
    source = shard // 2
    inside = (shard - 2 * source == side) & (slot >= 0) & (slot < slot_rows)
    ahead = lax.rem(source - place + devices, near_places)
    piece = jnp.where(ahead == 0, 0, jnp.where(ahead == near_places - 1, 1, ahead + 1))
    block = piece * (devices // 2 // near_places) + source // near_places
    facts = jnp.concatenate(
        [
            jnp.broadcast_to(jnp.where(inside, fact, -1).astype(jnp.float32), (8, count))
            for fact in (block, slot)
        ],
        axis=0,
    ).astype(jnp.bfloat16)

    def spread(chosen, out):
        both = lax.dot_general(
            marked(chosen), facts, (((1,), (1,)), ((), ())), preferred_element_type=jnp.float32
        )
        block_at, slot_at = both[:, :1].astype(jnp.int32), both[:, 8:9].astype(jnp.int32)
        out[...] = jnp.where(block_at < 0, -1, block_at * slot_rows + slot_at)

    own = count // devices
    at = lax.broadcasted_iota(jnp.int32, (count, count), 0)
    half = at // (count // 2)
    inner = at - half * (count // 2)
    owner_side = jnp.where(half == 0, side, 1 - side)
    original = (inner // own) * (2 * own) + owner_side * own + lax.rem(inner, own)
    spread(original == lax.broadcasted_iota(jnp.int32, (count, count), 1), slots)
    at = lax.broadcasted_iota(jnp.int32, (2 * own, count), 0)
    half = at // own
    owner_side = jnp.where(half == 0, side, 1 - side)
    original = place * (2 * own) + owner_side * own + at - half * own
    spread(original == lax.broadcasted_iota(jnp.int32, (2 * own, count), 1), pair_slots)


def locate(numbers, ids, table_rows, devices):
    whole = pl.BlockSpec(memory_space=pltpu.VMEM)
    count = ids.shape[0]
    return pl.pallas_call(
        lambda *refs: locate_kernel(table_rows, *refs),
        in_specs=[pl.BlockSpec(memory_space=pltpu.SMEM), whole],
        out_specs=[whole] * 3,
        out_shape=[
            jax.ShapeDtypeStruct((count, 1), jnp.int32),
            jax.ShapeDtypeStruct((2 * count // devices, 1), jnp.int32),
            jax.ShapeDtypeStruct((devices, 128), jnp.int32),
        ],
        compiler_params=pltpu.CompilerParams(vmem_limit_bytes=32 * 1024 * 1024),
        cost_estimate=pl.CostEstimate(
            flops=2 * count * count * devices, bytes_accessed=8 * count, transcendentals=0
        ),
    )(numbers, ids.reshape(1, -1))


def project_kernel(at, at_pair, rows_0, rows_1, rows_2, rows_3, rows_4, weights, *rest):
    proj_mine, proj_other, own_rows, slots = rest[-4:]
    cand_side, columns = proj_mine.shape
    own, width = own_rows.shape
    first = 0
    for rows in (rows_0, rows_1, rows_2, rows_3, rows_4):
        count = rows.shape[0]
        slots[first : first + count, :] = silu(
            lax.dot_general(
                rows[...],
                weights[...],
                (((1,), (1,)), ((), ())),
                preferred_element_type=jnp.float32,
            )
        ).astype(jnp.bfloat16)
        first += count
    place = lax.broadcasted_iota(jnp.int32, (cand_side, first), 1)
    for side, proj in ((0, proj_mine), (1, proj_other)):
        chosen = (at[side * cand_side : (side + 1) * cand_side, :] == place).astype(jnp.float32)
        proj[:cand_side, :] = jnp.dot(
            chosen.astype(jnp.bfloat16), slots[...], preferred_element_type=jnp.float32
        ).astype(jnp.bfloat16)
    place = lax.broadcasted_iota(jnp.int32, (2 * own, first), 1)
    chosen = (at_pair[...] == place).astype(jnp.float32).astype(jnp.bfloat16)
    total = None
    first = 0
    for rows in (rows_0, rows_1, rows_2, rows_3, rows_4):
        count = rows.shape[0]
        part = jnp.dot(
            chosen[:, first : first + count], rows[...], preferred_element_type=jnp.float32
        )
        total = part if total is None else total + part
        first += count
    own_rows[...] = total[:own].astype(jnp.bfloat16)
    for part in range(width // columns):
        proj_other[cand_side + part * own : cand_side + (part + 1) * own, :] = total[
            own:, part * columns : (part + 1) * columns
        ].astype(jnp.bfloat16)


def project(at, at_pair, rows, weights, ready):
    columns, width = weights.shape
    cand_side = at.shape[0] // 2
    own = at_pair.shape[0] // 2
    slot_count = sum(piece.shape[0] for piece in rows)
    whole = pl.BlockSpec(memory_space=pltpu.VMEM)
    return pl.pallas_call(
        project_kernel,
        in_specs=[whole] * (3 + len(rows)) + [pl.BlockSpec(memory_space=pl.ANY)] * len(ready),
        out_specs=[whole] * 3,
        out_shape=[
            jax.ShapeDtypeStruct((cand_side, columns), jnp.bfloat16),
            jax.ShapeDtypeStruct((cand_side + own * width // columns, columns), jnp.bfloat16),
            jax.ShapeDtypeStruct((own, width), jnp.bfloat16),
        ],
        scratch_shapes=[pltpu.VMEM((slot_count, columns), jnp.bfloat16)],
        compiler_params=pltpu.CompilerParams(vmem_limit_bytes=32 * 1024 * 1024),
        cost_estimate=pl.CostEstimate(
            flops=2 * slot_count * columns * (width + 2 * cand_side),
            bytes_accessed=2 * (slot_count + columns) * width,
            transcendentals=slot_count * columns,
        ),
    )(at, at_pair, *rows, weights, *ready)


def pack_kernel(feature_here, mine, arrived, own_rows, w_slice, *rest):
    queries, packed, embedded = rest[-3:]
    cand_side, columns = mine.shape
    own = own_rows.shape[0]
    proj = mine[...].astype(jnp.float32) + arrived[:cand_side, :].astype(jnp.float32)
    for part in range(own_rows.shape[1] // columns):
        lanes = slice(part * columns, (part + 1) * columns)
        other = arrived[cand_side + part * own : cand_side + (part + 1) * own, :]
        embedded[:, lanes] = (
            own_rows[:, lanes].astype(jnp.float32) + other.astype(jnp.float32)
        ).astype(jnp.bfloat16)
    block = 4 * feature_here
    queries[...] = proj[:, block : block + 2 * feature_here].T.astype(jnp.bfloat16)
    column, own, _ = packed.shape
    columns = 2 * block
    packed[:, :, :columns] = proj.astype(jnp.bfloat16).reshape(column, own, columns)
    lanes = w_slice.shape[1]
    for part in range(w_slice.shape[0] // own):
        packed[:, :, columns + part * lanes : columns + (part + 1) * lanes] = jnp.broadcast_to(
            w_slice[part * own : (part + 1) * own, :][None], (column, own, lanes)
        )


def pack(mine, arrived, own_rows, w_slice, feature_here):
    cand_side, columns = mine.shape
    own = own_rows.shape[0]
    column = cand_side // own
    packed_width = columns + w_slice.shape[0] * w_slice.shape[1] // own
    whole = pl.BlockSpec(memory_space=pltpu.VMEM)
    return pl.pallas_call(
        lambda *refs: pack_kernel(feature_here, *refs),
        in_specs=[whole] * 4,
        out_specs=[whole] * 3,
        out_shape=[
            jax.ShapeDtypeStruct((2 * feature_here, cand_side), jnp.bfloat16),
            jax.ShapeDtypeStruct((column, own, packed_width), jnp.bfloat16),
            jax.ShapeDtypeStruct(own_rows.shape, jnp.bfloat16),
        ],
        compiler_params=pltpu.CompilerParams(vmem_limit_bytes=32 * 1024 * 1024),
        cost_estimate=pl.CostEstimate(
            flops=cand_side * columns, bytes_accessed=8 * cand_side * columns, transcendentals=0
        ),
    )(mine, arrived, own_rows, w_slice)


def attend_kernel(scale, heads, *refs):
    queries, keys_a, keys_b, values_a, values_b, bias, live = refs[:7]
    summed = refs[-2]
    first_head = pl.program_id(0) * heads
    head_size = keys_a.shape[1] // heads
    for head in range(heads):
        lanes = slice(head * head_size, (head + 1) * head_size)
        head_queries = queries[lanes, :].T
        head_bias = 0.5 * bias[pl.ds(first_head + head, 1), :]
        total = None
        for source, (keys, values) in enumerate(((keys_a, values_a), (keys_b, values_b))):
            here = slice(source * keys.shape[0], (source + 1) * keys.shape[0])
            scores = lax.dot_general(
                head_queries,
                keys[:, lanes],
                (((1,), (1,)), ((), ())),
                preferred_element_type=jnp.float32,
            )
            weights = half_silu(scores * (0.5 * scale) + head_bias[:, here])
            weights = jnp.where(live[:, here] > 0.0, weights, 0.0).astype(jnp.bfloat16)
            part = jnp.dot(weights, values[:, lanes], preferred_element_type=jnp.float32)
            total = part if total is None else total + part
        summed[:, lanes] = total.astype(summed.dtype)


def attend(queries, keys, values, keys_other, values_other, bias, live, head_count, through):
    width, cand = queries.shape
    events = keys.shape[0]
    head_size = width // head_count
    heads = 4
    lanes = heads * head_size
    held = pl.BlockSpec(memory_space=pl.ANY)
    return pl.pallas_call(
        lambda *refs: attend_kernel(head_size ** (-0.5), heads, *refs),
        grid=(head_count // heads,),
        in_specs=[
            pl.BlockSpec((lanes, cand), lambda h: (h, 0)),
            pl.BlockSpec((events, lanes), lambda h: (0, h)),
            pl.BlockSpec((events, lanes), lambda h: (0, h)),
            pl.BlockSpec((events, lanes), lambda h: (0, h)),
            pl.BlockSpec((events, lanes), lambda h: (0, h)),
        ]
        + [pl.BlockSpec(array.shape, lambda h: (0, 0)) for array in (bias, live)]
        + [held],
        out_specs=[pl.BlockSpec((cand, lanes), lambda h: (0, h)), held],
        out_shape=[
            jax.ShapeDtypeStruct((cand, width), jnp.bfloat16),
            jax.ShapeDtypeStruct(through.shape, through.dtype),
        ],
        input_output_aliases={7: 1},
        compiler_params=pltpu.CompilerParams(vmem_limit_bytes=32 * 1024 * 1024),
        cost_estimate=pl.CostEstimate(
            flops=8 * cand * events * width,
            bytes_accessed=8 * events * width + 4 * cand * width,
            transcendentals=2 * cand * events * head_count,
        ),
    )(queries, keys, keys_other, values, values_other, bias, live, through)


def own_kernel(scale, rab, received, gain, self_term, gate):
    own, width = self_term.shape
    column = received.shape[0]
    lanes = width // column
    gate_u, own_v, own_queries, own_k = (
        jnp.concatenate(
            [
                received[place, :, part * lanes : (part + 1) * lanes].astype(jnp.float32)
                for place in range(column)
            ],
            axis=1,
        )
        for part in range(4)
    )
    gate[...] = gate_u * gain[...]
    products = own_queries * own_k
    head_count = rab.shape[0]
    head_size = width // head_count
    for head in range(head_count):
        head_lanes = slice(head * head_size, (head + 1) * head_size)
        score = jnp.sum(products[:, head_lanes], axis=1, keepdims=True) * scale + rab[head, 0]
        self_term[:, head_lanes] = silu(score) * own_v[:, head_lanes]


def own_parts(received, rab, gain, own):
    width = gain.shape[0]
    whole = pl.BlockSpec(memory_space=pltpu.VMEM)
    scale = (width // rab.shape[0]) ** (-0.5)
    return pl.pallas_call(
        lambda *refs: own_kernel(scale, *refs),
        in_specs=[pl.BlockSpec(memory_space=pltpu.SMEM), whole, whole],
        out_specs=[whole] * 2,
        out_shape=[jax.ShapeDtypeStruct((own, width), jnp.float32)] * 2,
        compiler_params=pltpu.CompilerParams(vmem_limit_bytes=32 * 1024 * 1024),
        cost_estimate=pl.CostEstimate(
            flops=8 * own * width, bytes_accessed=32 * own * width, transcendentals=own
        ),
    )(rab, received, gain.reshape(1, -1))


def finish_kernel(numbers, parts, self_term, gate, embedded, *rest):
    weights, scored = rest[:-1], rest[-1]
    history_sum = parts[0].astype(jnp.float32)
    for part in range(1, parts.shape[0]):
        history_sum = history_sum + parts[part].astype(jnp.float32)
    length = jnp.full((1, 1), numbers[0], jnp.int32).astype(jnp.float32)
    attended = history_sum * lax.rsqrt(length) + self_term[...]
    centre = jnp.mean(attended, axis=1, keepdims=True)
    spread = jnp.mean((attended - centre) ** 2, axis=1, keepdims=True)
    normed = (attended - centre) * lax.rsqrt(spread + 1e-05) * gate[...]
    normed = normed.astype(jnp.bfloat16)
    lanes = weights[0].shape[1]
    row_count = len(weights) // 2
    row, core = numbers[1], numbers[2]
    for index, columns_of in enumerate(weights):
        owner = core if index < row_count else 1 - core
        block = owner * row_count + lax.rem(row + row_count - index % row_count, row_count)
        columns = pl.ds(pl.multiple_of(block * lanes, lanes), lanes)
        projected = jnp.dot(normed, columns_of[...], preferred_element_type=jnp.float32)
        scored[:, columns] = (projected + embedded[:, columns].astype(jnp.float32)).astype(
            scored.dtype
        )


def finish(numbers, parts, self_term, gate, embedded, weights):
    whole = pl.BlockSpec(memory_space=pltpu.VMEM)
    rows, width = embedded.shape
    return pl.pallas_call(
        finish_kernel,
        in_specs=[pl.BlockSpec(memory_space=pltpu.SMEM)] + [whole] * (4 + len(weights)),
        out_specs=whole,
        out_shape=jax.ShapeDtypeStruct((rows, width), jnp.bfloat16),
        compiler_params=pltpu.CompilerParams(vmem_limit_bytes=32 * 1024 * 1024),
        cost_estimate=pl.CostEstimate(
            flops=2 * rows * width * width, bytes_accessed=4 * width * width, transcendentals=0
        ),
    )(numbers, parts, self_term, gate, embedded, *weights)


def local(
    history_keys, history_values, lengths, item_ids, item_table, w_proj, rab, norm_gain, w_out
):
    device_count = lax.axis_size("seq")
    column = device_count // 2
    index_here = lax.axis_index("seq")
    place, side = index_here // 2, index_here % 2
    batch_here = lax.axis_index("batch")
    row, core = batch_here // 4, batch_here % 2
    row_count = lax.axis_size("batch") // 4
    events_here, width = history_keys.shape
    head_count = rab.shape[0]
    table_rows = item_table.shape[0]
    cand_total = item_ids.shape[0]
    cand_here = cand_total // device_count
    cand_side = cand_total // 2
    feature_here = w_proj.shape[2]
    out_lanes = width // (2 * row_count)
    length = lengths[0]

    slice_rows = w_out.shape[0]

    far_places = column // near_places
    w_mine = w_proj.transpose(1, 2, 0).reshape(4 * feature_here, width)

    def numbers_at(first_rank):
        return jnp.stack([index_here, first_rank])

    picked = pick(numbers_at(jnp.int32(0)), item_ids, item_table, far_places)
    picked, w_sent, *sent = lax.optimization_barrier(
        (picked, w_mine, history_values, history_keys, w_out)
    )
    values_sent, keys_sent, w_slice = sent
    w_slice = lax.dynamic_slice_in_dim(
        w_slice, (core * row_count + row) * out_lanes, out_lanes, 1
    )
    rows = gather_slots(picked)
    w_other = swap_pair(jnp.concatenate([w_sent, w_slice.reshape(-1, width)]))
    slice_other = w_other[4 * feature_here :].reshape(w_slice.shape)
    w_other = w_other[: 4 * feature_here]
    keys_other, values_other = swap_pair(keys_sent), swap_pair(values_sent)
    w_pair = jnp.stack(
        [
            jnp.where(side == 0, w_mine, w_other).reshape(4, feature_here, width),
            jnp.where(side == 0, w_other, w_mine).reshape(4, feature_here, width),
        ],
        axis=1,
    ).reshape(8 * feature_here, width)
    slices = jnp.concatenate(
        [jnp.where(side == 0, w_slice, slice_other), jnp.where(side == 0, slice_other, w_slice)]
    )
    bias, live = biases(jnp.stack([length, index_here, index_here ^ 1]), rab, events_here)
    slots, pair_slots, most = locate(
        numbers_at(jnp.int32(0)), item_ids, table_rows, device_count
    )
    found = tuple(project(slots, pair_slots, rows, w_pair, (keys_other, values_other, bias, live)))

    def another(state):
        first_rank, limit, found = state
        numbers = numbers_at(first_rank)
        rows = gather_slots(pick(numbers, item_ids, item_table, far_places))
        slots, pair_slots, _ = locate(numbers, item_ids, table_rows, device_count)
        more = project(slots, pair_slots, rows, w_pair, ())
        return first_rank + slot_rows, limit, tuple(a + b for a, b in zip(found, more))

    _, _, (proj_mine, proj_other, own_rows) = lax.while_loop(
        lambda state: state[0] < state[1], another, (jnp.int32(slot_rows), most[0, 0], found)
    )
    side_queries, packed, embedded = pack(
        proj_mine, swap_pair(proj_other), own_rows, slices, feature_here
    )
    received = exchange(packed, column_groups())
    all_queries = lax.all_gather(
        side_queries, "seq", axis=0, tiled=True, axis_index_groups=column_groups()
    )

    summed, received = attend(
        all_queries,
        history_keys,
        history_values,
        keys_other,
        values_other,
        bias,
        live,
        head_count,
        received,
    )
    parts = exchange(summed.reshape(column, cand_here, width), column_groups())

    self_term, gate = own_parts(received, rab, norm_gain, cand_here)

    w_here = (
        received[:, :, 8 * feature_here :]
        .reshape(column, cand_here, 2 * slice_rows // cand_here, out_lanes)
        .transpose(0, 2, 1, 3)
        .reshape(width, out_lanes)
    )
    weights = [w_here] + [from_row(w_here, shift) for shift in range(1, row_count)]
    weights = [*weights, *swap_core(jnp.stack(weights))]
    numbers = jnp.stack([length, row, core])
    return finish(numbers, parts, self_term, gate, embedded, weights)


def solution(mesh):
    return jax.shard_map(
        local,
        mesh=mesh,
        in_specs=(
            P(("batch", "seq"), None),
            P(("batch", "seq"), None),
            P("batch"),
            P("batch"),
            P("seq", None),
            P(None, None, "seq"),
            P(),
            P(),
            P("seq", None),
        ),
        out_specs=P(("batch", "seq"), None),
        check_vma=False,
    )
```

```python
import jax
import jax.numpy as jnp
from jax import lax
from jax.experimental import pallas as pl
from jax.experimental.pallas import tpu as pltpu
from jax.sharding import PartitionSpec as P

slot_rows = 32
near_places = 4


def groups_of(places):
    return [[2 * place + side for place in group] for side in range(2) for group in places]


def exchange(blocks, groups):
    return lax.all_to_all(
        blocks, "seq", split_axis=0, concat_axis=0, tiled=True, axis_index_groups=groups
    )


def column_groups():
    return groups_of([list(range(lax.axis_size("seq") // 2))])


def from_place(block, shift):
    count = lax.axis_size("seq")
    return lax.ppermute(block, "seq", [(i, (i + 2 * shift) % count) for i in range(count)])


def swap_pair(block):
    return lax.ppermute(block, "seq", [(i, i ^ 1) for i in range(lax.axis_size("seq"))])


def swap_core(block):
    return lax.ppermute(block, "batch", [(i, i ^ 1) for i in range(lax.axis_size("batch"))])


def swap_half(block):
    return lax.ppermute(block, "batch", [(i, i ^ 2) for i in range(lax.axis_size("batch"))])


def from_row(block, shift):
    count = lax.axis_size("batch")
    return lax.ppermute(block, "batch", [(i, (i + 4 * shift) % count) for i in range(count)])


def gather_slots(blocks):
    column = lax.axis_size("seq") // 2
    far = groups_of([list(range(at, column, near_places)) for at in range(near_places)])
    blocks = exchange(blocks, far)
    rows = blocks.reshape(blocks.shape[0] * blocks.shape[1], blocks.shape[2])
    half = rows.shape[0] // 2
    return (
        rows,
        from_place(rows, 1),
        from_place(rows, -1),
        from_place(rows[:half], 2),
        from_place(rows[half:], -2),
    )


def bias_kernel(numbers, rab, bias, live):
    head_count, bucket_count = rab.shape
    sources = numbers.shape[0] - 1
    events = bias.shape[1] // sources
    step = lax.broadcasted_iota(jnp.int32, (head_count, events), 1)
    for source in range(sources):
        here = slice(source * events, (source + 1) * events)
        distance = numbers[0] - numbers[1 + source] * events - step
        bucket = jnp.zeros((head_count, events), jnp.int32)
        for power in range(bucket_count - 1):
            bucket = bucket + (distance >= 2**power).astype(jnp.int32)
        total = jnp.zeros((head_count, events), jnp.float32)
        for entry in range(bucket_count):
            total = total + jnp.where(bucket == entry, rab[:, entry : entry + 1], 0.0)
        bias[:, here] = total
        live[:, here] = (distance[:1] > 0).astype(jnp.float32)


def biases(numbers, rab, events):
    whole = pl.BlockSpec(memory_space=pltpu.VMEM)
    count = (numbers.shape[0] - 1) * events
    return pl.pallas_call(
        bias_kernel,
        in_specs=[pl.BlockSpec(memory_space=pltpu.SMEM), whole],
        out_specs=[whole] * 2,
        out_shape=[
            jax.ShapeDtypeStruct((rab.shape[0], count), jnp.float32),
            jax.ShapeDtypeStruct((1, count), jnp.float32),
        ],
        cost_estimate=pl.CostEstimate(
            flops=64 * rab.shape[0] * count, bytes_accessed=40 * count, transcendentals=0
        ),
    )(numbers, rab)


def silu(value):
    return half_silu(0.5 * value)


def half_silu(half):
    return half + half * jnp.tanh(half)


def marked(condition):
    return condition.astype(jnp.float32).astype(jnp.bfloat16)


def earlier(count):
    return lax.broadcasted_iota(jnp.int32, (count, count), 0) < lax.broadcasted_iota(
        jnp.int32, (count, count), 1
    )


def pick_kernel(numbers, ids, table, packed):
    rows, count = table.shape[0], ids.shape[1]
    copies, slot_count, _ = packed.shape
    there = ids[...] - numbers[0] * rows
    here = (there >= 0) & (there < rows)
    marks = jnp.broadcast_to(here.astype(jnp.float32), (8, count)).astype(jnp.bfloat16)
    rank = jnp.dot(marks, marked(earlier(count)), preferred_element_type=jnp.float32)[:1]
    slot = jnp.where(here, rank.astype(jnp.int32) - numbers[1], -1)
    taken = slot == lax.broadcasted_iota(jnp.int32, (slot_count, count), 0)
    wanted = there == lax.broadcasted_iota(jnp.int32, (rows, count), 0)
    picks = lax.dot_general(
        marked(taken), marked(wanted), (((1,), (1,)), ((), ())), preferred_element_type=jnp.float32
    ).astype(jnp.bfloat16)
    found = jnp.dot(picks, table[...], preferred_element_type=jnp.float32).astype(jnp.bfloat16)
    for copy in range(copies):
        packed[copy] = found


def pick(numbers, ids, table, copies):
    whole = pl.BlockSpec(memory_space=pltpu.VMEM)
    return pl.pallas_call(
        pick_kernel,
        in_specs=[pl.BlockSpec(memory_space=pltpu.SMEM), whole, whole],
        out_specs=whole,
        out_shape=jax.ShapeDtypeStruct((copies, slot_rows, table.shape[1]), jnp.bfloat16),
        compiler_params=pltpu.CompilerParams(vmem_limit_bytes=32 * 1024 * 1024),
        cost_estimate=pl.CostEstimate(
            flops=2 * slot_rows * table.shape[0] * table.shape[1],
            bytes_accessed=2 * table.shape[0] * table.shape[1],
            transcendentals=0,
        ),
    )(numbers, ids.reshape(1, -1), table)


def locate_kernel(table_rows, numbers, ids, slots, pair_slots, most):
    count, devices = ids.shape[1], most.shape[0]
    index = numbers[0]
    place, side = index // 2, lax.rem(index, 2)
    shard = ids[...] // table_rows
    member = lax.broadcasted_iota(jnp.int32, (devices, count), 0) == shard
    ranks = jnp.dot(marked(member), marked(earlier(count)), preferred_element_type=jnp.float32)
    rank = jnp.sum(jnp.where(member, ranks, 0.0), axis=0, keepdims=True)
    counts = jnp.sum(member.astype(jnp.float32), axis=1, keepdims=True)
    most[...] = jnp.broadcast_to(jnp.max(counts, axis=0, keepdims=True), most.shape).astype(
        jnp.int32
    )
    slot = rank.astype(jnp.int32) - numbers[1]
    source = shard // 2
    inside = (shard - 2 * source == side) & (slot >= 0) & (slot < slot_rows)
    ahead = lax.rem(source - place + devices, near_places)
    piece = jnp.where(ahead == 0, 0, jnp.where(ahead == near_places - 1, 1, ahead + 1))
    block = piece * (devices // 2 // near_places) + source // near_places
    facts = jnp.concatenate(
        [
            jnp.broadcast_to(jnp.where(inside, fact, -1).astype(jnp.float32), (8, count))
            for fact in (block, slot)
        ],
        axis=0,
    ).astype(jnp.bfloat16)

    def spread(chosen, out):
        both = lax.dot_general(
            marked(chosen), facts, (((1,), (1,)), ((), ())), preferred_element_type=jnp.float32
        )
        block_at, slot_at = both[:, :1].astype(jnp.int32), both[:, 8:9].astype(jnp.int32)
        out[...] = jnp.where(block_at < 0, -1, block_at * slot_rows + slot_at)

    own = count // devices
    at = lax.broadcasted_iota(jnp.int32, (count, count), 0)
    half = at // (count // 2)
    inner = at - half * (count // 2)
    owner_side = jnp.where(half == 0, side, 1 - side)
    original = (inner // own) * (2 * own) + owner_side * own + lax.rem(inner, own)
    spread(original == lax.broadcasted_iota(jnp.int32, (count, count), 1), slots)
    at = lax.broadcasted_iota(jnp.int32, (2 * own, count), 0)
    half = at // own
    owner_side = jnp.where(half == 0, side, 1 - side)
    original = place * (2 * own) + owner_side * own + at - half * own
    spread(original == lax.broadcasted_iota(jnp.int32, (2 * own, count), 1), pair_slots)


def locate(numbers, ids, table_rows, devices):
    whole = pl.BlockSpec(memory_space=pltpu.VMEM)
    count = ids.shape[0]
    return pl.pallas_call(
        lambda *refs: locate_kernel(table_rows, *refs),
        in_specs=[pl.BlockSpec(memory_space=pltpu.SMEM), whole],
        out_specs=[whole] * 3,
        out_shape=[
            jax.ShapeDtypeStruct((count, 1), jnp.int32),
            jax.ShapeDtypeStruct((2 * count // devices, 1), jnp.int32),
            jax.ShapeDtypeStruct((devices, 128), jnp.int32),
        ],
        compiler_params=pltpu.CompilerParams(vmem_limit_bytes=32 * 1024 * 1024),
        cost_estimate=pl.CostEstimate(
            flops=2 * count * count * devices, bytes_accessed=8 * count, transcendentals=0
        ),
    )(numbers, ids.reshape(1, -1))


def project_kernel(at, at_pair, rows_0, rows_1, rows_2, rows_3, rows_4, weights, *rest):
    proj_mine, proj_other, own_rows, slots = rest[-4:]
    cand_side, columns = proj_mine.shape
    own, width = own_rows.shape
    first = 0
    for rows in (rows_0, rows_1, rows_2, rows_3, rows_4):
        count = rows.shape[0]
        slots[first : first + count, :] = silu(
            lax.dot_general(
                rows[...],
                weights[...],
                (((1,), (1,)), ((), ())),
                preferred_element_type=jnp.float32,
            )
        ).astype(jnp.bfloat16)
        first += count
    place = lax.broadcasted_iota(jnp.int32, (cand_side, first), 1)
    for side, proj in ((0, proj_mine), (1, proj_other)):
        chosen = (at[side * cand_side : (side + 1) * cand_side, :] == place).astype(jnp.float32)
        proj[:cand_side, :] = jnp.dot(
            chosen.astype(jnp.bfloat16), slots[...], preferred_element_type=jnp.float32
        ).astype(jnp.bfloat16)
    place = lax.broadcasted_iota(jnp.int32, (2 * own, first), 1)
    chosen = (at_pair[...] == place).astype(jnp.float32).astype(jnp.bfloat16)
    total = None
    first = 0
    for rows in (rows_0, rows_1, rows_2, rows_3, rows_4):
        count = rows.shape[0]
        part = jnp.dot(
            chosen[:, first : first + count], rows[...], preferred_element_type=jnp.float32
        )
        total = part if total is None else total + part
        first += count
    own_rows[...] = total[:own].astype(jnp.bfloat16)
    for part in range(width // columns):
        proj_other[cand_side + part * own : cand_side + (part + 1) * own, :] = total[
            own:, part * columns : (part + 1) * columns
        ].astype(jnp.bfloat16)


def project(at, at_pair, rows, weights, ready):
    columns, width = weights.shape
    cand_side = at.shape[0] // 2
    own = at_pair.shape[0] // 2
    slot_count = sum(piece.shape[0] for piece in rows)
    whole = pl.BlockSpec(memory_space=pltpu.VMEM)
    return pl.pallas_call(
        project_kernel,
        in_specs=[whole] * (3 + len(rows)) + [pl.BlockSpec(memory_space=pl.ANY)] * len(ready),
        out_specs=[whole] * 3,
        out_shape=[
            jax.ShapeDtypeStruct((cand_side, columns), jnp.bfloat16),
            jax.ShapeDtypeStruct((cand_side + own * width // columns, columns), jnp.bfloat16),
            jax.ShapeDtypeStruct((own, width), jnp.bfloat16),
        ],
        scratch_shapes=[pltpu.VMEM((slot_count, columns), jnp.bfloat16)],
        compiler_params=pltpu.CompilerParams(vmem_limit_bytes=32 * 1024 * 1024),
        cost_estimate=pl.CostEstimate(
            flops=2 * slot_count * columns * (width + 2 * cand_side),
            bytes_accessed=2 * (slot_count + columns) * width,
            transcendentals=slot_count * columns,
        ),
    )(at, at_pair, *rows, weights, *ready)


def pack_kernel(feature_here, mine, arrived, own_rows, w_slice, *rest):
    queries, packed, embedded = rest[-3:]
    cand_side, columns = mine.shape
    own = own_rows.shape[0]
    proj = mine[...].astype(jnp.float32) + arrived[:cand_side, :].astype(jnp.float32)
    for part in range(own_rows.shape[1] // columns):
        lanes = slice(part * columns, (part + 1) * columns)
        other = arrived[cand_side + part * own : cand_side + (part + 1) * own, :]
        embedded[:, lanes] = (
            own_rows[:, lanes].astype(jnp.float32) + other.astype(jnp.float32)
        ).astype(jnp.bfloat16)
    block = 4 * feature_here
    queries[...] = proj[:, block : block + 2 * feature_here].T.astype(jnp.bfloat16)
    column, own, _ = packed.shape
    columns = 2 * block
    packed[:, :, :columns] = proj.astype(jnp.bfloat16).reshape(column, own, columns)
    lanes = w_slice.shape[1]
    for part in range(w_slice.shape[0] // own):
        packed[:, :, columns + part * lanes : columns + (part + 1) * lanes] = jnp.broadcast_to(
            w_slice[part * own : (part + 1) * own, :][None], (column, own, lanes)
        )


def pack(mine, arrived, own_rows, w_slice, feature_here):
    cand_side, columns = mine.shape
    own = own_rows.shape[0]
    column = cand_side // own
    packed_width = columns + w_slice.shape[0] * w_slice.shape[1] // own
    whole = pl.BlockSpec(memory_space=pltpu.VMEM)
    return pl.pallas_call(
        lambda *refs: pack_kernel(feature_here, *refs),
        in_specs=[whole] * 4,
        out_specs=[whole] * 3,
        out_shape=[
            jax.ShapeDtypeStruct((2 * feature_here, cand_side), jnp.bfloat16),
            jax.ShapeDtypeStruct((column, own, packed_width), jnp.bfloat16),
            jax.ShapeDtypeStruct(own_rows.shape, jnp.bfloat16),
        ],
        compiler_params=pltpu.CompilerParams(vmem_limit_bytes=32 * 1024 * 1024),
        cost_estimate=pl.CostEstimate(
            flops=cand_side * columns, bytes_accessed=8 * cand_side * columns, transcendentals=0
        ),
    )(mine, arrived, own_rows, w_slice)


def attend_kernel(scale, heads, *refs):
    queries, keys_a, keys_b, values_a, values_b, bias, live = refs[:7]
    summed = refs[-2]
    first_head = pl.program_id(0) * heads
    head_size = keys_a.shape[1] // heads
    for head in range(heads):
        lanes = slice(head * head_size, (head + 1) * head_size)
        head_queries = queries[lanes, :].T
        head_bias = 0.5 * bias[pl.ds(first_head + head, 1), :]
        total = None
        for source, (keys, values) in enumerate(((keys_a, values_a), (keys_b, values_b))):
            here = slice(source * keys.shape[0], (source + 1) * keys.shape[0])
            scores = lax.dot_general(
                head_queries,
                keys[:, lanes],
                (((1,), (1,)), ((), ())),
                preferred_element_type=jnp.float32,
            )
            weights = half_silu(scores * (0.5 * scale) + head_bias[:, here])
            weights = jnp.where(live[:, here] > 0.0, weights, 0.0).astype(jnp.bfloat16)
            part = jnp.dot(weights, values[:, lanes], preferred_element_type=jnp.float32)
            total = part if total is None else total + part
        summed[:, lanes] = total.astype(summed.dtype)


def attend(queries, keys, values, keys_other, values_other, bias, live, head_count, through):
    width, cand = queries.shape
    events = keys.shape[0]
    head_size = width // head_count
    heads = 4
    lanes = heads * head_size
    held = pl.BlockSpec(memory_space=pl.ANY)
    return pl.pallas_call(
        lambda *refs: attend_kernel(head_size ** (-0.5), heads, *refs),
        grid=(head_count // heads,),
        in_specs=[
            pl.BlockSpec((lanes, cand), lambda h: (h, 0)),
            pl.BlockSpec((events, lanes), lambda h: (0, h)),
            pl.BlockSpec((events, lanes), lambda h: (0, h)),
            pl.BlockSpec((events, lanes), lambda h: (0, h)),
            pl.BlockSpec((events, lanes), lambda h: (0, h)),
        ]
        + [pl.BlockSpec(array.shape, lambda h: (0, 0)) for array in (bias, live)]
        + [held],
        out_specs=[pl.BlockSpec((cand, lanes), lambda h: (0, h)), held],
        out_shape=[
            jax.ShapeDtypeStruct((cand, width), jnp.bfloat16),
            jax.ShapeDtypeStruct(through.shape, through.dtype),
        ],
        input_output_aliases={7: 1},
        compiler_params=pltpu.CompilerParams(vmem_limit_bytes=32 * 1024 * 1024),
        cost_estimate=pl.CostEstimate(
            flops=8 * cand * events * width,
            bytes_accessed=8 * events * width + 4 * cand * width,
            transcendentals=2 * cand * events * head_count,
        ),
    )(queries, keys, keys_other, values, values_other, bias, live, through)


def own_kernel(scale, rab, received, gain, self_term, gate):
    own, width = self_term.shape
    column = received.shape[0]
    lanes = width // column
    gate_u, own_v, own_queries, own_k = (
        jnp.concatenate(
            [
                received[place, :, part * lanes : (part + 1) * lanes].astype(jnp.float32)
                for place in range(column)
            ],
            axis=1,
        )
        for part in range(4)
    )
    gate[...] = gate_u * gain[...]
    products = own_queries * own_k
    head_count = rab.shape[0]
    head_size = width // head_count
    for head in range(head_count):
        head_lanes = slice(head * head_size, (head + 1) * head_size)
        score = jnp.sum(products[:, head_lanes], axis=1, keepdims=True) * scale + rab[head, 0]
        self_term[:, head_lanes] = silu(score) * own_v[:, head_lanes]


def own_parts(received, rab, gain, own):
    width = gain.shape[0]
    whole = pl.BlockSpec(memory_space=pltpu.VMEM)
    scale = (width // rab.shape[0]) ** (-0.5)
    return pl.pallas_call(
        lambda *refs: own_kernel(scale, *refs),
        in_specs=[pl.BlockSpec(memory_space=pltpu.SMEM), whole, whole],
        out_specs=[whole] * 2,
        out_shape=[jax.ShapeDtypeStruct((own, width), jnp.float32)] * 2,
        compiler_params=pltpu.CompilerParams(vmem_limit_bytes=32 * 1024 * 1024),
        cost_estimate=pl.CostEstimate(
            flops=8 * own * width, bytes_accessed=32 * own * width, transcendentals=own
        ),
    )(rab, received, gain.reshape(1, -1))


def finish_kernel(numbers, parts, self_term, gate, embedded, *rest):
    weights, scored = rest[:-1], rest[-1]
    history_sum = parts[0].astype(jnp.float32)
    for part in range(1, parts.shape[0]):
        history_sum = history_sum + parts[part].astype(jnp.float32)
    length = jnp.full((1, 1), numbers[0], jnp.int32).astype(jnp.float32)
    attended = history_sum * lax.rsqrt(length) + self_term[...]
    centre = jnp.mean(attended, axis=1, keepdims=True)
    spread = jnp.mean((attended - centre) ** 2, axis=1, keepdims=True)
    normed = (attended - centre) * lax.rsqrt(spread + 1e-05) * gate[...]
    normed = normed.astype(jnp.bfloat16)
    lanes = weights[0].shape[1]
    row_count = len(weights) // 2
    row, core = numbers[1], numbers[2]
    for index, columns_of in enumerate(weights):
        owner = core if index < row_count else 1 - core
        block = owner * row_count + lax.rem(row + row_count - index % row_count, row_count)
        columns = pl.ds(pl.multiple_of(block * lanes, lanes), lanes)
        projected = jnp.dot(normed, columns_of[...], preferred_element_type=jnp.float32)
        scored[:, columns] = (projected + embedded[:, columns].astype(jnp.float32)).astype(
            scored.dtype
        )


def finish(numbers, parts, self_term, gate, embedded, weights):
    whole = pl.BlockSpec(memory_space=pltpu.VMEM)
    rows, width = embedded.shape
    return pl.pallas_call(
        finish_kernel,
        in_specs=[pl.BlockSpec(memory_space=pltpu.SMEM)] + [whole] * (4 + len(weights)),
        out_specs=whole,
        out_shape=jax.ShapeDtypeStruct((rows, width), jnp.bfloat16),
        compiler_params=pltpu.CompilerParams(vmem_limit_bytes=32 * 1024 * 1024),
        cost_estimate=pl.CostEstimate(
            flops=2 * rows * width * width, bytes_accessed=4 * width * width, transcendentals=0
        ),
    )(numbers, parts, self_term, gate, embedded, *weights)


def local(
    history_keys, history_values, lengths, item_ids, item_table, w_proj, rab, norm_gain, w_out
):
    device_count = lax.axis_size("seq")
    column = device_count // 2
    index_here = lax.axis_index("seq")
    place, side = index_here // 2, index_here % 2
    batch_here = lax.axis_index("batch")
    row_count = lax.axis_size("batch") // 4
    row = (batch_here // 4 + row_count // 2 * (batch_here // 2 % 2)) % row_count
    core = batch_here % 2
    events_here, width = history_keys.shape
    head_count = rab.shape[0]
    table_rows = item_table.shape[0]
    cand_total = item_ids.shape[0]
    cand_here = cand_total // device_count
    cand_side = cand_total // 2
    feature_here = w_proj.shape[2]
    out_lanes = width // (2 * row_count)
    length = lengths[0]

    slice_rows = w_out.shape[0]

    far_places = column // near_places
    w_mine = w_proj.transpose(1, 2, 0).reshape(4 * feature_here, width)

    def numbers_at(first_rank):
        return jnp.stack([index_here, first_rank])

    picked = pick(numbers_at(jnp.int32(0)), item_ids, item_table, far_places)
    picked, w_sent, *sent = lax.optimization_barrier(
        (picked, w_mine, history_values, history_keys, w_out)
    )
    values_sent, keys_sent, w_slice = sent
    w_slice = lax.dynamic_slice_in_dim(
        w_slice, (core * row_count + row) * out_lanes, out_lanes, 1
    )
    rows = gather_slots(picked)
    w_other = swap_pair(jnp.concatenate([w_sent, w_slice.reshape(-1, width)]))
    slice_other = w_other[4 * feature_here :].reshape(w_slice.shape)
    w_other = w_other[: 4 * feature_here]
    keys_other, values_other = swap_pair(keys_sent), swap_pair(values_sent)
    w_pair = jnp.stack(
        [
            jnp.where(side == 0, w_mine, w_other).reshape(4, feature_here, width),
            jnp.where(side == 0, w_other, w_mine).reshape(4, feature_here, width),
        ],
        axis=1,
    ).reshape(8 * feature_here, width)
    slices = jnp.concatenate(
        [jnp.where(side == 0, w_slice, slice_other), jnp.where(side == 0, slice_other, w_slice)]
    )
    bias, live = biases(jnp.stack([length, index_here, index_here ^ 1]), rab, events_here)
    slots, pair_slots, most = locate(
        numbers_at(jnp.int32(0)), item_ids, table_rows, device_count
    )
    found = tuple(project(slots, pair_slots, rows, w_pair, (keys_other, values_other, bias, live)))

    def another(state):
        first_rank, limit, found = state
        numbers = numbers_at(first_rank)
        rows = gather_slots(pick(numbers, item_ids, item_table, far_places))
        slots, pair_slots, _ = locate(numbers, item_ids, table_rows, device_count)
        more = project(slots, pair_slots, rows, w_pair, ())
        return first_rank + slot_rows, limit, tuple(a + b for a, b in zip(found, more))

    _, _, (proj_mine, proj_other, own_rows) = lax.while_loop(
        lambda state: state[0] < state[1], another, (jnp.int32(slot_rows), most[0, 0], found)
    )
    side_queries, packed, embedded = pack(
        proj_mine, swap_pair(proj_other), own_rows, slices, feature_here
    )
    received = exchange(packed, column_groups())
    all_queries = lax.all_gather(
        side_queries, "seq", axis=0, tiled=True, axis_index_groups=column_groups()
    )

    summed, received = attend(
        all_queries,
        history_keys,
        history_values,
        keys_other,
        values_other,
        bias,
        live,
        head_count,
        received,
    )
    parts = exchange(summed.reshape(column, cand_here, width), column_groups())

    self_term, gate = own_parts(received, rab, norm_gain, cand_here)

    w_here = (
        received[:, :, 8 * feature_here :]
        .reshape(column, cand_here, 2 * slice_rows // cand_here, out_lanes)
        .transpose(0, 2, 1, 3)
        .reshape(width, out_lanes)
    )
    weights = [w_here] + [
        swap_half(w_here) if 2 * shift == row_count else from_row(w_here, shift)
        for shift in range(1, row_count)
    ]
    weights = [*weights, *swap_core(jnp.stack(weights))]
    numbers = jnp.stack([length, row, core])
    return finish(numbers, parts, self_term, gate, embedded, weights)


def solution(mesh):
    return jax.shard_map(
        local,
        mesh=mesh,
        in_specs=(
            P(("batch", "seq"), None),
            P(("batch", "seq"), None),
            P("batch"),
            P("batch"),
            P("seq", None),
            P(None, None, "seq"),
            P(),
            P(),
            P("seq", None),
        ),
        out_specs=P(("batch", "seq"), None),
        check_vma=False,
    )
```

```python
import jax
import jax.numpy as jnp
from jax import lax
from jax.experimental import pallas as pl
from jax.experimental.pallas import tpu as pltpu
from jax.sharding import PartitionSpec as P

slot_rows = 32
near_places = 4


def groups_of(places):
    return [[2 * place + side for place in group] for side in range(2) for group in places]


def exchange(blocks, groups):
    return lax.all_to_all(
        blocks, "seq", split_axis=0, concat_axis=0, tiled=True, axis_index_groups=groups
    )


def column_groups():
    return groups_of([list(range(lax.axis_size("seq") // 2))])


def from_place(block, shift):
    count = lax.axis_size("seq")
    return lax.ppermute(block, "seq", [(i, (i + 2 * shift) % count) for i in range(count)])


def swap_pair(block):
    return lax.ppermute(block, "seq", [(i, i ^ 1) for i in range(lax.axis_size("seq"))])


def swap_core(block):
    return lax.ppermute(block, "batch", [(i, i ^ 1) for i in range(lax.axis_size("batch"))])


def from_row(block, shift):
    count = lax.axis_size("batch")
    return lax.ppermute(block, "batch", [(i, (i + 4 * shift) % count) for i in range(count)])


def gather_slots(blocks):
    column = lax.axis_size("seq") // 2
    far = groups_of([list(range(at, column, near_places)) for at in range(near_places)])
    blocks = exchange(blocks, far)
    rows = blocks.reshape(blocks.shape[0] * blocks.shape[1], blocks.shape[2])
    return rows, from_place(rows, 1), from_place(rows, -1), from_place(rows, 2)


def bias_kernel(numbers, rab, bias, live):
    head_count, bucket_count = rab.shape
    sources = numbers.shape[0] - 1
    events = bias.shape[1] // sources
    step = lax.broadcasted_iota(jnp.int32, (head_count, events), 1)
    for source in range(sources):
        here = slice(source * events, (source + 1) * events)
        distance = numbers[0] - numbers[1 + source] * events - step
        bucket = jnp.zeros((head_count, events), jnp.int32)
        for power in range(bucket_count - 1):
            bucket = bucket + (distance >= 2**power).astype(jnp.int32)
        total = jnp.zeros((head_count, events), jnp.float32)
        for entry in range(bucket_count):
            total = total + jnp.where(bucket == entry, rab[:, entry : entry + 1], 0.0)
        bias[:, here] = total
        live[:, here] = (distance[:1] > 0).astype(jnp.float32)


def biases(numbers, rab, events):
    whole = pl.BlockSpec(memory_space=pltpu.VMEM)
    count = (numbers.shape[0] - 1) * events
    return pl.pallas_call(
        bias_kernel,
        in_specs=[pl.BlockSpec(memory_space=pltpu.SMEM), whole],
        out_specs=[whole] * 2,
        out_shape=[
            jax.ShapeDtypeStruct((rab.shape[0], count), jnp.float32),
            jax.ShapeDtypeStruct((1, count), jnp.float32),
        ],
        cost_estimate=pl.CostEstimate(
            flops=64 * rab.shape[0] * count, bytes_accessed=40 * count, transcendentals=0
        ),
    )(numbers, rab)


def silu(value):
    return half_silu(0.5 * value)


def half_silu(half):
    return half + half * jnp.tanh(half)


def marked(condition):
    return condition.astype(jnp.float32).astype(jnp.bfloat16)


def earlier(count):
    return lax.broadcasted_iota(jnp.int32, (count, count), 0) < lax.broadcasted_iota(
        jnp.int32, (count, count), 1
    )


def pick_kernel(numbers, ids, table, packed):
    rows, count = table.shape[0], ids.shape[1]
    copies, slot_count, _ = packed.shape
    there = ids[...] - numbers[0] * rows
    here = (there >= 0) & (there < rows)
    marks = jnp.broadcast_to(here.astype(jnp.float32), (8, count)).astype(jnp.bfloat16)
    rank = jnp.dot(marks, marked(earlier(count)), preferred_element_type=jnp.float32)[:1]
    slot = jnp.where(here, rank.astype(jnp.int32) - numbers[1], -1)
    taken = slot == lax.broadcasted_iota(jnp.int32, (slot_count, count), 0)
    wanted = there == lax.broadcasted_iota(jnp.int32, (rows, count), 0)
    picks = lax.dot_general(
        marked(taken), marked(wanted), (((1,), (1,)), ((), ())), preferred_element_type=jnp.float32
    ).astype(jnp.bfloat16)
    found = jnp.dot(picks, table[...], preferred_element_type=jnp.float32).astype(jnp.bfloat16)
    for copy in range(copies):
        packed[copy] = found


def pick(numbers, ids, table, copies):
    whole = pl.BlockSpec(memory_space=pltpu.VMEM)
    return pl.pallas_call(
        pick_kernel,
        in_specs=[pl.BlockSpec(memory_space=pltpu.SMEM), whole, whole],
        out_specs=whole,
        out_shape=jax.ShapeDtypeStruct((copies, slot_rows, table.shape[1]), jnp.bfloat16),
        compiler_params=pltpu.CompilerParams(vmem_limit_bytes=32 * 1024 * 1024),
        cost_estimate=pl.CostEstimate(
            flops=2 * slot_rows * table.shape[0] * table.shape[1],
            bytes_accessed=2 * table.shape[0] * table.shape[1],
            transcendentals=0,
        ),
    )(numbers, ids.reshape(1, -1), table)


def locate_kernel(table_rows, numbers, ids, slots, pair_slots, most):
    count, devices = ids.shape[1], most.shape[0]
    index = numbers[0]
    place, side = index // 2, lax.rem(index, 2)
    shard = ids[...] // table_rows
    member = lax.broadcasted_iota(jnp.int32, (devices, count), 0) == shard
    ranks = jnp.dot(marked(member), marked(earlier(count)), preferred_element_type=jnp.float32)
    rank = jnp.sum(jnp.where(member, ranks, 0.0), axis=0, keepdims=True)
    counts = jnp.sum(member.astype(jnp.float32), axis=1, keepdims=True)
    most[...] = jnp.broadcast_to(jnp.max(counts, axis=0, keepdims=True), most.shape).astype(
        jnp.int32
    )
    slot = rank.astype(jnp.int32) - numbers[1]
    source = shard // 2
    inside = (shard - 2 * source == side) & (slot >= 0) & (slot < slot_rows)
    ahead = lax.rem(source - place + devices, near_places)
    piece = jnp.where(ahead == 0, 0, jnp.where(ahead == near_places - 1, 1, ahead + 1))
    block = piece * (devices // 2 // near_places) + source // near_places
    facts = jnp.concatenate(
        [
            jnp.broadcast_to(jnp.where(inside, fact, -1).astype(jnp.float32), (8, count))
            for fact in (block, slot)
        ],
        axis=0,
    ).astype(jnp.bfloat16)

    def spread(chosen, out):
        both = lax.dot_general(
            marked(chosen), facts, (((1,), (1,)), ((), ())), preferred_element_type=jnp.float32
        )
        block_at, slot_at = both[:, :1].astype(jnp.int32), both[:, 8:9].astype(jnp.int32)
        out[...] = jnp.where(block_at < 0, -1, block_at * slot_rows + slot_at)

    own = count // devices
    at = lax.broadcasted_iota(jnp.int32, (count, count), 0)
    half = at // (count // 2)
    inner = at - half * (count // 2)
    owner_side = jnp.where(half == 0, side, 1 - side)
    original = (inner // own) * (2 * own) + owner_side * own + lax.rem(inner, own)
    spread(original == lax.broadcasted_iota(jnp.int32, (count, count), 1), slots)
    at = lax.broadcasted_iota(jnp.int32, (2 * own, count), 0)
    half = at // own
    owner_side = jnp.where(half == 0, side, 1 - side)
    original = place * (2 * own) + owner_side * own + at - half * own
    spread(original == lax.broadcasted_iota(jnp.int32, (2 * own, count), 1), pair_slots)


def locate(numbers, ids, table_rows, devices):
    whole = pl.BlockSpec(memory_space=pltpu.VMEM)
    count = ids.shape[0]
    return pl.pallas_call(
        lambda *refs: locate_kernel(table_rows, *refs),
        in_specs=[pl.BlockSpec(memory_space=pltpu.SMEM), whole],
        out_specs=[whole] * 3,
        out_shape=[
            jax.ShapeDtypeStruct((count, 1), jnp.int32),
            jax.ShapeDtypeStruct((2 * count // devices, 1), jnp.int32),
            jax.ShapeDtypeStruct((devices, 128), jnp.int32),
        ],
        compiler_params=pltpu.CompilerParams(vmem_limit_bytes=32 * 1024 * 1024),
        cost_estimate=pl.CostEstimate(
            flops=2 * count * count * devices, bytes_accessed=8 * count, transcendentals=0
        ),
    )(numbers, ids.reshape(1, -1))


def project_kernel(at, at_pair, rows_0, rows_1, rows_2, rows_3, weights, *rest):
    proj_mine, proj_other, own_rows, slots = rest[-4:]
    cand_side, columns = proj_mine.shape
    own, width = own_rows.shape
    first = 0
    for rows in (rows_0, rows_1, rows_2, rows_3):
        count = rows.shape[0]
        slots[first : first + count, :] = silu(
            lax.dot_general(
                rows[...],
                weights[...],
                (((1,), (1,)), ((), ())),
                preferred_element_type=jnp.float32,
            )
        ).astype(jnp.bfloat16)
        first += count
    place = lax.broadcasted_iota(jnp.int32, (cand_side, first), 1)
    for side, proj in ((0, proj_mine), (1, proj_other)):
        chosen = (at[side * cand_side : (side + 1) * cand_side, :] == place).astype(jnp.float32)
        proj[:cand_side, :] = jnp.dot(
            chosen.astype(jnp.bfloat16), slots[...], preferred_element_type=jnp.float32
        ).astype(jnp.bfloat16)
    place = lax.broadcasted_iota(jnp.int32, (2 * own, first), 1)
    chosen = (at_pair[...] == place).astype(jnp.float32).astype(jnp.bfloat16)
    total = None
    first = 0
    for rows in (rows_0, rows_1, rows_2, rows_3):
        count = rows.shape[0]
        part = jnp.dot(
            chosen[:, first : first + count], rows[...], preferred_element_type=jnp.float32
        )
        total = part if total is None else total + part
        first += count
    own_rows[...] = total[:own].astype(jnp.bfloat16)
    for part in range(width // columns):
        proj_other[cand_side + part * own : cand_side + (part + 1) * own, :] = total[
            own:, part * columns : (part + 1) * columns
        ].astype(jnp.bfloat16)


def project(at, at_pair, rows, weights, ready):
    columns, width = weights.shape
    cand_side = at.shape[0] // 2
    own = at_pair.shape[0] // 2
    slot_count = sum(piece.shape[0] for piece in rows)
    whole = pl.BlockSpec(memory_space=pltpu.VMEM)
    return pl.pallas_call(
        project_kernel,
        in_specs=[whole] * (3 + len(rows)) + [pl.BlockSpec(memory_space=pl.ANY)] * len(ready),
        out_specs=[whole] * 3,
        out_shape=[
            jax.ShapeDtypeStruct((cand_side, columns), jnp.bfloat16),
            jax.ShapeDtypeStruct((cand_side + own * width // columns, columns), jnp.bfloat16),
            jax.ShapeDtypeStruct((own, width), jnp.bfloat16),
        ],
        scratch_shapes=[pltpu.VMEM((slot_count, columns), jnp.bfloat16)],
        compiler_params=pltpu.CompilerParams(vmem_limit_bytes=32 * 1024 * 1024),
        cost_estimate=pl.CostEstimate(
            flops=2 * slot_count * columns * (width + 2 * cand_side),
            bytes_accessed=2 * (slot_count + columns) * width,
            transcendentals=slot_count * columns,
        ),
    )(at, at_pair, *rows, weights, *ready)


def pack_kernel(feature_here, mine, arrived, own_rows, w_slice, *rest):
    queries, packed, embedded = rest[-3:]
    cand_side, columns = mine.shape
    own = own_rows.shape[0]
    proj = mine[...].astype(jnp.float32) + arrived[:cand_side, :].astype(jnp.float32)
    for part in range(own_rows.shape[1] // columns):
        lanes = slice(part * columns, (part + 1) * columns)
        other = arrived[cand_side + part * own : cand_side + (part + 1) * own, :]
        embedded[:, lanes] = (
            own_rows[:, lanes].astype(jnp.float32) + other.astype(jnp.float32)
        ).astype(jnp.bfloat16)
    block = 4 * feature_here
    queries[...] = proj[:, block : block + 2 * feature_here].T.astype(jnp.bfloat16)
    column, own, _ = packed.shape
    columns = 2 * block
    packed[:, :, :columns] = proj.astype(jnp.bfloat16).reshape(column, own, columns)
    lanes = w_slice.shape[1]
    for part in range(w_slice.shape[0] // own):
        packed[:, :, columns + part * lanes : columns + (part + 1) * lanes] = jnp.broadcast_to(
            w_slice[part * own : (part + 1) * own, :][None], (column, own, lanes)
        )


def pack(mine, arrived, own_rows, w_slice, feature_here):
    cand_side, columns = mine.shape
    own = own_rows.shape[0]
    column = cand_side // own
    packed_width = columns + w_slice.shape[0] * w_slice.shape[1] // own
    whole = pl.BlockSpec(memory_space=pltpu.VMEM)
    return pl.pallas_call(
        lambda *refs: pack_kernel(feature_here, *refs),
        in_specs=[whole] * 4,
        out_specs=[whole] * 3,
        out_shape=[
            jax.ShapeDtypeStruct((2 * feature_here, cand_side), jnp.bfloat16),
            jax.ShapeDtypeStruct((column, own, packed_width), jnp.bfloat16),
            jax.ShapeDtypeStruct(own_rows.shape, jnp.bfloat16),
        ],
        compiler_params=pltpu.CompilerParams(vmem_limit_bytes=32 * 1024 * 1024),
        cost_estimate=pl.CostEstimate(
            flops=cand_side * columns, bytes_accessed=8 * cand_side * columns, transcendentals=0
        ),
    )(mine, arrived, own_rows, w_slice)


def attend_kernel(scale, heads, *refs):
    queries, keys_a, keys_b, values_a, values_b, bias, live = refs[:7]
    summed = refs[-2]
    first_head = pl.program_id(0) * heads
    head_size = keys_a.shape[1] // heads
    for head in range(heads):
        lanes = slice(head * head_size, (head + 1) * head_size)
        head_queries = queries[lanes, :].T
        head_bias = 0.5 * bias[pl.ds(first_head + head, 1), :]
        total = None
        for source, (keys, values) in enumerate(((keys_a, values_a), (keys_b, values_b))):
            here = slice(source * keys.shape[0], (source + 1) * keys.shape[0])
            scores = lax.dot_general(
                head_queries,
                keys[:, lanes],
                (((1,), (1,)), ((), ())),
                preferred_element_type=jnp.float32,
            )
            weights = half_silu(scores * (0.5 * scale) + head_bias[:, here])
            weights = jnp.where(live[:, here] > 0.0, weights, 0.0).astype(jnp.bfloat16)
            part = jnp.dot(weights, values[:, lanes], preferred_element_type=jnp.float32)
            total = part if total is None else total + part
        summed[:, lanes] = total.astype(summed.dtype)


def attend(queries, keys, values, keys_other, values_other, bias, live, head_count, through):
    width, cand = queries.shape
    events = keys.shape[0]
    head_size = width // head_count
    heads = 4
    lanes = heads * head_size
    held = pl.BlockSpec(memory_space=pl.ANY)
    return pl.pallas_call(
        lambda *refs: attend_kernel(head_size ** (-0.5), heads, *refs),
        grid=(head_count // heads,),
        in_specs=[
            pl.BlockSpec((lanes, cand), lambda h: (h, 0)),
            pl.BlockSpec((events, lanes), lambda h: (0, h)),
            pl.BlockSpec((events, lanes), lambda h: (0, h)),
            pl.BlockSpec((events, lanes), lambda h: (0, h)),
            pl.BlockSpec((events, lanes), lambda h: (0, h)),
        ]
        + [pl.BlockSpec(array.shape, lambda h: (0, 0)) for array in (bias, live)]
        + [held],
        out_specs=[pl.BlockSpec((cand, lanes), lambda h: (0, h)), held],
        out_shape=[
            jax.ShapeDtypeStruct((cand, width), jnp.bfloat16),
            jax.ShapeDtypeStruct(through.shape, through.dtype),
        ],
        input_output_aliases={7: 1},
        compiler_params=pltpu.CompilerParams(vmem_limit_bytes=32 * 1024 * 1024),
        cost_estimate=pl.CostEstimate(
            flops=8 * cand * events * width,
            bytes_accessed=8 * events * width + 4 * cand * width,
            transcendentals=2 * cand * events * head_count,
        ),
    )(queries, keys, keys_other, values, values_other, bias, live, through)


def own_kernel(scale, rab, received, gain, self_term, gate):
    own, width = self_term.shape
    column = received.shape[0]
    lanes = width // column
    gate_u, own_v, own_queries, own_k = (
        jnp.concatenate(
            [
                received[place, :, part * lanes : (part + 1) * lanes].astype(jnp.float32)
                for place in range(column)
            ],
            axis=1,
        )
        for part in range(4)
    )
    gate[...] = gate_u * gain[...]
    products = own_queries * own_k
    head_count = rab.shape[0]
    head_size = width // head_count
    for head in range(head_count):
        head_lanes = slice(head * head_size, (head + 1) * head_size)
        score = jnp.sum(products[:, head_lanes], axis=1, keepdims=True) * scale + rab[head, 0]
        self_term[:, head_lanes] = silu(score) * own_v[:, head_lanes]


def own_parts(received, rab, gain, own):
    width = gain.shape[0]
    whole = pl.BlockSpec(memory_space=pltpu.VMEM)
    scale = (width // rab.shape[0]) ** (-0.5)
    return pl.pallas_call(
        lambda *refs: own_kernel(scale, *refs),
        in_specs=[pl.BlockSpec(memory_space=pltpu.SMEM), whole, whole],
        out_specs=[whole] * 2,
        out_shape=[jax.ShapeDtypeStruct((own, width), jnp.float32)] * 2,
        compiler_params=pltpu.CompilerParams(vmem_limit_bytes=32 * 1024 * 1024),
        cost_estimate=pl.CostEstimate(
            flops=8 * own * width, bytes_accessed=32 * own * width, transcendentals=own
        ),
    )(rab, received, gain.reshape(1, -1))


def finish_kernel(numbers, parts, self_term, gate, embedded, *rest):
    weights, scored = rest[:-1], rest[-1]
    history_sum = parts[0].astype(jnp.float32)
    for part in range(1, parts.shape[0]):
        history_sum = history_sum + parts[part].astype(jnp.float32)
    length = jnp.full((1, 1), numbers[0], jnp.int32).astype(jnp.float32)
    attended = history_sum * lax.rsqrt(length) + self_term[...]
    centre = jnp.mean(attended, axis=1, keepdims=True)
    spread = jnp.mean((attended - centre) ** 2, axis=1, keepdims=True)
    normed = (attended - centre) * lax.rsqrt(spread + 1e-05) * gate[...]
    normed = normed.astype(jnp.bfloat16)
    lanes = weights[0].shape[1]
    row_count = len(weights) // 2
    row, core = numbers[1], numbers[2]
    for index, columns_of in enumerate(weights):
        owner = core if index < row_count else 1 - core
        block = owner * row_count + lax.rem(row + row_count - index % row_count, row_count)
        columns = pl.ds(pl.multiple_of(block * lanes, lanes), lanes)
        projected = jnp.dot(normed, columns_of[...], preferred_element_type=jnp.float32)
        scored[:, columns] = (projected + embedded[:, columns].astype(jnp.float32)).astype(
            scored.dtype
        )


def finish(numbers, parts, self_term, gate, embedded, weights):
    whole = pl.BlockSpec(memory_space=pltpu.VMEM)
    rows, width = embedded.shape
    return pl.pallas_call(
        finish_kernel,
        in_specs=[pl.BlockSpec(memory_space=pltpu.SMEM)] + [whole] * (4 + len(weights)),
        out_specs=whole,
        out_shape=jax.ShapeDtypeStruct((rows, width), jnp.bfloat16),
        compiler_params=pltpu.CompilerParams(vmem_limit_bytes=32 * 1024 * 1024),
        cost_estimate=pl.CostEstimate(
            flops=2 * rows * width * width, bytes_accessed=4 * width * width, transcendentals=0
        ),
    )(numbers, parts, self_term, gate, embedded, *weights)


def local(
    history_keys, history_values, lengths, item_ids, item_table, w_proj, rab, norm_gain, w_out
):
    device_count = lax.axis_size("seq")
    column = device_count // 2
    index_here = lax.axis_index("seq")
    place, side = index_here // 2, index_here % 2
    batch_here = lax.axis_index("batch")
    row, core = batch_here // 4, batch_here % 2
    row_count = lax.axis_size("batch") // 4
    events_here, width = history_keys.shape
    head_count = rab.shape[0]
    table_rows = item_table.shape[0]
    cand_total = item_ids.shape[0]
    cand_here = cand_total // device_count
    cand_side = cand_total // 2
    feature_here = w_proj.shape[2]
    out_lanes = width // (2 * row_count)
    length = lengths[0]

    slice_rows = w_out.shape[0]

    far_places = column // near_places
    w_mine = w_proj.transpose(1, 2, 0).reshape(4 * feature_here, width)

    def numbers_at(first_rank):
        return jnp.stack([index_here, first_rank])

    picked = pick(numbers_at(jnp.int32(0)), item_ids, item_table, far_places)
    picked, w_sent, *sent = lax.optimization_barrier(
        (picked, w_mine, history_values, history_keys, w_out)
    )
    values_sent, keys_sent, w_slice = sent
    w_slice = lax.dynamic_slice_in_dim(
        w_slice, (core * row_count + row) * out_lanes, out_lanes, 1
    )
    rows = gather_slots(picked)
    w_other = swap_pair(jnp.concatenate([w_sent, w_slice.reshape(-1, width)]))
    slice_other = w_other[4 * feature_here :].reshape(w_slice.shape)
    w_other = w_other[: 4 * feature_here]
    keys_other, values_other = swap_pair(keys_sent), swap_pair(values_sent)
    w_pair = jnp.stack(
        [
            jnp.where(side == 0, w_mine, w_other).reshape(4, feature_here, width),
            jnp.where(side == 0, w_other, w_mine).reshape(4, feature_here, width),
        ],
        axis=1,
    ).reshape(8 * feature_here, width)
    slices = jnp.concatenate(
        [jnp.where(side == 0, w_slice, slice_other), jnp.where(side == 0, slice_other, w_slice)]
    )
    bias, live = biases(jnp.stack([length, index_here, index_here ^ 1]), rab, events_here)
    slots, pair_slots, most = locate(
        numbers_at(jnp.int32(0)), item_ids, table_rows, device_count
    )
    found = tuple(project(slots, pair_slots, rows, w_pair, (keys_other, values_other, bias, live)))

    def another(state):
        first_rank, limit, found = state
        numbers = numbers_at(first_rank)
        rows = gather_slots(pick(numbers, item_ids, item_table, far_places))
        slots, pair_slots, _ = locate(numbers, item_ids, table_rows, device_count)
        more = project(slots, pair_slots, rows, w_pair, ())
        return first_rank + slot_rows, limit, tuple(a + b for a, b in zip(found, more))

    _, _, (proj_mine, proj_other, own_rows) = lax.while_loop(
        lambda state: state[0] < state[1], another, (jnp.int32(slot_rows), most[0, 0], found)
    )
    side_queries, packed, embedded = pack(
        proj_mine, swap_pair(proj_other), own_rows, slices, feature_here
    )
    received = exchange(packed, column_groups())
    all_queries = lax.all_gather(
        side_queries, "seq", axis=0, tiled=True, axis_index_groups=column_groups()
    )

    summed, received = attend(
        all_queries,
        history_keys,
        history_values,
        keys_other,
        values_other,
        bias,
        live,
        head_count,
        received,
    )
    parts = exchange(summed.reshape(column, cand_here, width), column_groups())

    self_term, gate = own_parts(received, rab, norm_gain, cand_here)

    w_here = (
        received[:, :, 8 * feature_here :]
        .reshape(column, cand_here, 2 * slice_rows // cand_here, out_lanes)
        .transpose(0, 2, 1, 3)
        .reshape(width, out_lanes)
    )
    weights = [w_here] + [from_row(w_here, shift) for shift in range(1, row_count)]
    weights = [*weights, *swap_core(jnp.stack(weights))]
    numbers = jnp.stack([length, row, core])
    return finish(numbers, parts, self_term, gate, embedded, weights)


def solution(mesh):
    return jax.shard_map(
        local,
        mesh=mesh,
        in_specs=(
            P(("batch", "seq"), None),
            P(("batch", "seq"), None),
            P("batch"),
            P("batch"),
            P("seq", None),
            P(None, None, "seq"),
            P(),
            P(),
            P("seq", None),
        ),
        out_specs=P(("batch", "seq"), None),
        check_vma=False,
    )
```
